32 devices in a mesh: crop: 2 (over core), row: 4 (over z), col: 4 (over y, x).
Axes of the slice: x: 2, y: 2, z: 4, core: 2. Of those that a mesh axis runs over, the one named last changes fastest.
Arguments:
- pair: float32 [2, 512, 512, 128], P('crop', 'row', 'col'), parts along dimension 0, may hold values from -6 to 6
- gain_input: float32 [128], replicated, may hold values from 0.1 to 1.9
- weights_in: float32 [128, 512], replicated, may hold values from -0.5 to 0.5
- gate_weights: float32 [128, 128], replicated, may hold values from -0.5 to 0.5
- weights_out: float32 [128, 128], replicated, may hold values from -0.5 to 0.5
- gain_product: float32 [128], replicated, may hold values from 0.1 to 1.9
- gain_transition: float32 [128], replicated, may hold values from 0.1 to 1.9
- transition_in: float32 [128, 1024], replicated, may hold values from -0.5 to 0.5
- transition_out: float32 [512, 128], replicated, may hold values from -0.25 to 0.25
- distogram_weights: float32 [128, 64], replicated, may hold values from -0.5 to 0.5
- distogram_bias: float32 [64], replicated, may hold values from -4 to 4
Outputs:
- logits: float32 [2, 512, 512, 64], P('crop', 'row', 'col'), parts along dimension 0
The draws below stay inside these ranges and needn't reach their ends.
There are 2 independent parts, one for each index of `crop`. The reference program is written for one: setup_inputs(seed, part) draws one part's arguments, and reference() takes and returns one part's arrays. A program takes and returns all parts, laid end to end along the dimension named above; an argument that names none is the same for every part. Nothing has to cross between parts.
All inputs are finite; a program needn't handle non-finite values.
Results may differ from the reference program's by a relative error of at most 0.00007.
Values sent between devices are 32-bit elements; how exact they have to be, the bound alone decides.
No kernel may reach another device: no remote copies, remote signals or barrier semaphores. Data moves between devices by JAX's collectives and lax.ppermute only.
A program may use at most 192 MiB of HBM per device.

```python
import jax
import jax.numpy as jnp
from jax import lax

PAIR_W = 128
HIDDEN_SIZE = 512
BINS = 64
TOKENS = 512
CROPS = 1


def block_scale(key, shape, cuts, least, top_value):
    factor_of, own = 1.0, jax.random.fold_in(key, 6)
    for dim, shards_of in cuts:
        heights = jnp.exp(jax.random.uniform(jax.random.fold_in(own, dim), (shards_of,), jnp.float32, least / len(cuts), top_value / len(cuts)))
        factor_of = factor_of * jnp.repeat(heights, shape[dim] // shards_of).reshape([-1 if axis == dim else 1 for axis in range(len(shape))])
    return factor_of


def bell_draw(own_key, dims, scale, reach, split=(), held_as=jnp.bfloat16):
    factor_of = block_scale(own_key, dims, split, -0.22, 0.18) if split else 1.0
    result = jax.random.normal(own_key, dims, jnp.float32) * scale * factor_of
    return jnp.minimum(jnp.maximum(result, -reach), reach).astype(held_as)


def setup_inputs(seed: int = 0, part: int = 0) -> dict:
    key_of = jax.random.split(jax.random.key(seed), 12)
    part_splits = jax.random.split(jax.random.fold_in(key_of[11], part), 12)
    return {
        "pair": bell_draw(part_splits[0], (CROPS, TOKENS, TOKENS, PAIR_W), 1.0, 6.0, ((1, 4), (2, 4)), jnp.float32),
        "gain_input": jnp.clip(1.0 + 0.18 * jax.random.normal(key_of[1], (PAIR_W,), jnp.float32), 0.1, 1.9),
        "weights_in": bell_draw(key_of[2], (PAIR_W, 4 * PAIR_W), PAIR_W ** -0.5, 0.5, (), jnp.float32),
        "gate_weights": bell_draw(key_of[3], (PAIR_W, PAIR_W), PAIR_W ** -0.5, 0.5, (), jnp.float32),
        "weights_out": bell_draw(key_of[4], (PAIR_W, PAIR_W), PAIR_W ** -0.5, 0.5, (), jnp.float32),
        "gain_product": jnp.clip(1.0 + 0.18 * jax.random.normal(key_of[5], (PAIR_W,), jnp.float32), 0.1, 1.9),
        "gain_transition": jnp.clip(1.0 + 0.18 * jax.random.normal(key_of[6], (PAIR_W,), jnp.float32), 0.1, 1.9),
        "transition_in": bell_draw(key_of[7], (PAIR_W, 2 * HIDDEN_SIZE), PAIR_W ** -0.5, 0.5, (), jnp.float32),
        "transition_out": bell_draw(key_of[8], (HIDDEN_SIZE, PAIR_W), HIDDEN_SIZE ** -0.5, 0.25, (), jnp.float32),
        "distogram_weights": bell_draw(key_of[9], (PAIR_W, BINS), PAIR_W ** -0.5, 0.5, (), jnp.float32),
        "distogram_bias": bell_draw(key_of[10], (BINS,), 1.0, 4.0, (), jnp.float32),
    }


HIGH = lax.Precision.HIGHEST

def layer_norm(values, gain):
    center = values - lax.optimization_barrier(jnp.mean(values, axis=-1, keepdims=True))
    spread = lax.optimization_barrier(jnp.mean(center * center, axis=-1, keepdims=True))
    return center * lax.rsqrt(spread + 1e-05) * gain

def project(values, weights):
    return jnp.einsum('...c,cd->...d', values, weights, precision=HIGH)

def reference(pair, gain_input, weights_in, gate_weights, weights_out, gain_product, gain_transition, transition_in, transition_out, distogram_weights, distogram_bias):

    def one_crop(square):
        normed = layer_norm(square, gain_input)
        projected = project(normed, weights_in)
        left_hand = jax.nn.sigmoid(projected[..., PAIR_W:2 * PAIR_W]) * projected[..., :PAIR_W]
        right_hand = jax.nn.sigmoid(projected[..., 3 * PAIR_W:]) * projected[..., 2 * PAIR_W:3 * PAIR_W]
        product = jnp.einsum('ikc,jkc->ijc', left_hand, right_hand, precision=HIGH)
        gate = jax.nn.sigmoid(project(normed, gate_weights))
        updated = square + gate * project(layer_norm(product, gain_product), weights_out)

        def transition(line):
            hidden = project(layer_norm(line, gain_transition), transition_in)
            activated = jax.nn.silu(hidden[:, :HIDDEN_SIZE]) * hidden[:, HIDDEN_SIZE:]
            return line + project(activated, transition_out)
        pair_out = lax.map(transition, updated)
        symmetric = pair_out + jnp.swapaxes(pair_out, 0, 1)
        return project(symmetric, distogram_weights) + distogram_bias
    return lax.map(one_crop, pair)
```

```python
import functools

import jax
import jax.numpy as jnp
from jax import lax
from jax.experimental import pallas as pl
from jax.experimental.pallas import tpu as pltpu
from jax.sharding import Mesh, PartitionSpec as P

HIGH = lax.Precision.HIGHEST
LANES = 128
GROUP = 8
CHUNKS = 4
VMEM = 56 * 1024 * 1024
SCALE = 8


def layer_norm(values, gain):
    center = values - jnp.mean(values, axis=-1, keepdims=True)
    spread = jnp.mean(center * center, axis=-1, keepdims=True)
    return center * lax.rsqrt(spread + 1e-05) * gain


def project(values, weights):
    return jnp.einsum("...c,cd->...d", values, weights, precision=HIGH)


def outgoing(left_hand, right_hand):
    return jnp.einsum("bikc,bjkc->bijc", left_hand, right_hand, precision=HIGH)


def mirrored(values):
    columns = lax.all_to_all(values, ("row", "col"), split_axis=2, concat_axis=1, tiled=True)
    return jnp.swapaxes(columns, 1, 2)


def general_shards(
    pair,
    gain_input,
    weights_in,
    gate_weights,
    weights_out,
    gain_product,
    gain_transition,
    transition_in,
    transition_out,
    distogram_weights,
    distogram_bias,
):
    row_count = lax.axis_size("row")
    col_count = lax.axis_size("col")
    crops, tile_rows, tile_cols, width = pair.shape
    normed = layer_norm(pair, gain_input)
    projected = project(normed, weights_in)
    left_hand = jax.nn.sigmoid(projected[..., width : 2 * width]) * projected[..., :width]
    right_hand = jax.nn.sigmoid(projected[..., 3 * width :]) * projected[..., 2 * width : 3 * width]
    stacked = jnp.stack([left_hand, right_hand], axis=0)
    received = lax.all_to_all(stacked, ("row", "col"), split_axis=4, concat_axis=2, tiled=True)
    items = received.shape[1]
    owned = received.shape[4]
    square = received.reshape(2, items, row_count, col_count, tile_rows, tile_cols, owned)
    square = square.transpose(0, 1, 2, 4, 3, 5, 6).reshape(
        2, items, row_count * tile_rows, col_count * tile_cols, owned
    )
    result = outgoing(square[0], square[1])
    product = lax.all_to_all(result, ("row", "col"), split_axis=1, concat_axis=3, tiled=True)
    base = lax.all_to_all(pair, "col", split_axis=1, concat_axis=2, tiled=True)
    normed_base = layer_norm(base, gain_input)
    gate = jax.nn.sigmoid(project(normed_base, gate_weights))
    updated = base + gate * project(layer_norm(product, gain_product), weights_out)
    hidden = project(layer_norm(updated, gain_transition), transition_in)
    hidden_width = transition_out.shape[0]
    activated = jax.nn.silu(hidden[..., :hidden_width]) * hidden[..., hidden_width:]
    pair_out = updated + project(activated, transition_out)
    symmetric = pair_out + mirrored(pair_out)
    line_logits = project(symmetric, distogram_weights) + distogram_bias
    return lax.all_to_all(line_logits, "col", split_axis=2, concat_axis=1, tiled=True)


def split_weights(weights, gain=None):
    if gain is not None:
        weights = gain[:, None] * weights
    flipped = weights.T
    high = lax.reduce_precision(flipped, 8, 7)
    low = flipped - high
    return jnp.concatenate([high, high, low], axis=1).astype(jnp.bfloat16)


def estimate(flops, moved):
    return pl.CostEstimate(flops=flops // SCALE, bytes_accessed=moved // SCALE, transcendentals=0)


def parts(values):
    high = values.astype(jnp.bfloat16)
    low = (values - high.astype(jnp.float32)).astype(jnp.bfloat16)
    return high, low


def times(weights3, values):
    high, low = parts(values)
    return jnp.dot(
        weights3, jnp.concatenate([high, low, high], axis=0), preferred_element_type=jnp.float32
    )


def normalized(values):
    center = values - jnp.mean(values, axis=0, keepdims=True)
    spread = jnp.mean(center * center, axis=0, keepdims=True)
    return center * lax.rsqrt(spread + 1e-05)


def hands_kernel(pair_ref, weights_ref, out_ref):
    rows, _, width = pair_ref.shape
    per = 4
    flat = out_ref.reshape(width * rows, LANES)
    for start in range(0, rows, per):
        values = jnp.concatenate([pair_ref[start + n].T for n in range(per)], axis=1)
        projected = times(weights_ref[...], normalized(values))
        result = jax.nn.sigmoid(projected[width:]) * projected[:width]
        for n in range(per):
            flat[pl.ds(start + n, width, stride=rows), :] = result[:, n * LANES : (n + 1) * LANES]


def hands(pair, weights3, first, rows):
    _, tile_cols, width = pair.shape
    lead = first // GROUP
    return pl.pallas_call(
        hands_kernel,
        grid=(rows // GROUP,),
        in_specs=[
            pl.BlockSpec((GROUP, tile_cols, width), lambda g: (lead + g, 0, 0)),
            pl.BlockSpec(weights3.shape, lambda g: (0, 0)),
        ],
        out_specs=pl.BlockSpec((width, GROUP, tile_cols), lambda g: (0, g, 0)),
        out_shape=jax.ShapeDtypeStruct((width, rows, tile_cols), jnp.float32),
        compiler_params=pltpu.CompilerParams(vmem_limit_bytes=VMEM),
        cost_estimate=estimate(6 * rows * tile_cols * width * 2 * width, 8 * rows * tile_cols * width),
        name="hands",
    )(pair, weights3)


def product_kernel(left_ref, right_ref, out_ref):
    cols = right_ref.shape[1] // 2

    def lines(ref):
        return jnp.concatenate(
            [
                jnp.concatenate([ref[lo * cols + c, 0] for c in range(cols)], axis=1)
                for lo in range(2)
            ],
            axis=0,
        )

    left_high, left_low = parts(lines(left_ref))
    right_high, right_low = parts(
        jnp.concatenate([lines(right_ref.at[half]) for half in range(2)], axis=0)
    )
    result = lax.dot_general(
        jnp.concatenate([right_high, right_high, right_low], axis=1),
        jnp.concatenate([left_high, left_low, left_high], axis=1),
        (((1,), (1,)), ((), ())),
        preferred_element_type=jnp.float32,
    )
    rows = right_ref.shape[3]
    wide = result.shape[1] // 2
    for line in range(2):
        for plane in range(cols):
            out_ref[line * cols + plane, 0] = result[
                plane * rows : (plane + 1) * rows, line * wide : (line + 1) * wide
            ]


def product(left, right):
    _, sources, owned, rows, width = right.shape
    wide = left.shape[2]
    k_all = width * sources // 2
    return pl.pallas_call(
        product_kernel,
        grid=(owned,),
        in_specs=[
            pl.BlockSpec((sources, 1, wide, width), lambda n: (0, n, 0, 0)),
            pl.BlockSpec((2, sources, 1, rows, width), lambda n: (0, 0, n, 0, 0)),
        ],
        out_specs=pl.BlockSpec((sources, 1, rows, wide), lambda n: (0, n, 0, 0)),
        out_shape=jax.ShapeDtypeStruct((sources, owned, rows, wide), jnp.float32),
        compiler_params=pltpu.CompilerParams(vmem_limit_bytes=VMEM),
        cost_estimate=estimate(
            6 * owned * 4 * rows * 2 * wide * k_all, 4 * owned * k_all * (2 * wide + 4 * rows)
        ),
        name="product",
    )(left, right)


def head_kernel(
    pair_ref, product_ref, gate_ref, output_ref, up_ref, down_ref, bins_ref, out_ref
):
    tile_rows, cols, width = pair_ref.shape
    bins = out_ref.shape[1]
    per = 4
    flat_pair = pair_ref.reshape(tile_rows * cols, width)
    flat_product = product_ref.reshape(width * cols, tile_rows)
    hidden_width = up_ref.shape[0] // 2
    for start in range(0, cols, per):
        values = jnp.concatenate(
            [flat_pair[pl.ds(start + n, tile_rows, stride=cols), :].T for n in range(per)], axis=1
        )
        product_values = jnp.concatenate(
            [flat_product[pl.ds(start + n, width, stride=cols), :] for n in range(per)], axis=1
        )
        gate = jax.nn.sigmoid(times(gate_ref[...], normalized(values)))
        updated = values + gate * times(output_ref[...], normalized(product_values))
        hidden = times(up_ref[...], normalized(updated))
        activated = jax.nn.silu(hidden[:hidden_width]) * hidden[hidden_width:]
        pair_out = updated + times(down_ref[...], activated)
        logits = times(bins_ref[...], pair_out)
        for n in range(per):
            out_ref[start + n] = logits[:, n * tile_rows : (n + 1) * tile_rows]


def head(pair, product_values, chunk, gate3, output3, up3, down3, bins3):
    tile_rows, tile_cols, width = pair.shape
    chunk_cols = product_values.shape[1]
    steps = chunk_cols // GROUP
    bins = bins3.shape[0]
    whole = lambda array: pl.BlockSpec(array.shape, lambda g: (0, 0))
    macs = gate3.size + output3.size + up3.size + down3.size + bins3.size
    return pl.pallas_call(
        head_kernel,
        grid=(steps,),
        in_specs=[
            pl.BlockSpec((tile_rows, GROUP, width), lambda g: (0, chunk * steps + g, 0)),
            pl.BlockSpec((width, GROUP, tile_rows), lambda g: (0, g, 0)),
            whole(gate3),
            whole(output3),
            whole(up3),
            whole(down3),
            whole(bins3),
        ],
        out_specs=pl.BlockSpec((GROUP, bins, tile_rows), lambda g: (g, 0, 0)),
        out_shape=jax.ShapeDtypeStruct((chunk_cols, bins, tile_rows), jnp.float32),
        compiler_params=pltpu.CompilerParams(vmem_limit_bytes=VMEM),
        cost_estimate=estimate(
            2 * chunk_cols * tile_rows * macs, 4 * chunk_cols * tile_rows * (2 * width + bins)
        ),
        name="head",
    )(pair, product_values, gate3, output3, up3, down3, bins3)


def mover(count):
    every = [(r, c) for r in range(count) for c in range(count)]

    def move(values, target):
        pairs = [(r * count + c, target(r, c)) for r, c in every]
        return lax.ppermute(values, ("half", "lo", "col"), pairs)

    return move


def swap_steps(count, turn):
    aside = lambda r, c: r * count + (c ^ r ^ turn)
    return [aside, lambda r, c: (c ^ r ^ turn) * count + c, aside]


def half_shards(
    pair,
    gain_input,
    weights_in,
    gate_weights,
    weights_out,
    gain_product,
    gain_transition,
    transition_in,
    transition_out,
    distogram_weights,
    distogram_bias,
):
    row_count = 2 * lax.axis_size("lo")
    col_count = lax.axis_size("col")
    _, tile_rows, tile_cols, width = pair.shape
    tile = pair[0]
    chunk_rows = tile_rows // CHUNKS
    in3 = split_weights(weights_in, gain_input)
    left3, right3 = in3[: 2 * width], in3[2 * width :]
    gate3 = split_weights(gate_weights, gain_input)
    output3 = split_weights(weights_out, gain_product)
    up3 = split_weights(transition_in, gain_transition)
    down3 = split_weights(transition_out)
    bins3 = split_weights(distogram_weights)
    sources = 2 * col_count
    owned = width // sources

    def spread(values):
        values = values.reshape(sources, owned, *values.shape[1:])
        return lax.all_to_all(values, ("lo", "col"), split_axis=0, concat_axis=0, tiled=True)

    others = []
    for chunk in range(CHUNKS):
        right = spread(hands(tile, right3, chunk * chunk_rows, chunk_rows))
        others.append(lax.all_gather(right, "half"))
    left = spread(hands(tile, left3, 0, tile_rows))

    move = mover(row_count)
    own, mirror, steps = [], [], []
    for chunk in range(CHUNKS):
        values = product(left, others[chunk])
        values = lax.all_to_all(values, ("lo", "col"), split_axis=0, concat_axis=0, tiled=True)
        values = values.reshape(width, chunk_rows, tile_rows)
        if chunk:
            values, mirror = lax.optimization_barrier((values, mirror))
        logits = head(tile, values, chunk, gate3, output3, up3, down3, bins3)
        own.append(logits)
        mirror.append(logits)
        last = chunk == CHUNKS - 1
        steps.append([lambda r, c: c * row_count + r] if last else swap_steps(row_count, chunk))
        for n in range(chunk + 1):
            if steps[n]:
                mirror[n] = move(mirror[n], steps[n].pop(0))
    for n in range(CHUNKS):
        for step in steps[n]:
            mirror[n] = move(mirror[n], step)
    turned = jnp.transpose(jnp.concatenate(own, axis=0), (2, 1, 0))
    logits = turned + jnp.concatenate(mirror, axis=0) + distogram_bias[None, :, None]
    return jnp.swapaxes(logits, 1, 2)[None]


def solution(mesh):
    names = mesh.axis_names
    crops, rows, cols = (mesh.shape[name] for name in names)

    def run(pair, *parameters):
        crop_count, height, across, width = pair.shape
        tile_rows, tile_cols = height // rows, across // cols
        by_halves = (
            crop_count == crops
            and rows == cols == 4
            and tile_rows == tile_cols == LANES
            and width == LANES
        )
        if by_halves:
            halves = Mesh(mesh.devices.reshape(crops, 2, rows // 2, cols), ("crop", "half", "lo", "col"))
            spec, used, body = P("crop", ("half", "lo"), "col", None), halves, half_shards
        else:
            spec, used, body = P("crop", "row", "col", None), mesh, general_shards
        return jax.shard_map(
            body,
            mesh=used,
            in_specs=(spec,) + (P(),) * len(parameters),
            out_specs=spec,
            check_vma=False,
        )(pair, *parameters)

    return run
```

```python
import functools

import jax
import jax.numpy as jnp
from jax import lax
from jax.experimental import pallas as pl
from jax.experimental.pallas import tpu as pltpu
from jax.sharding import Mesh, PartitionSpec as P

HIGH = lax.Precision.HIGHEST
LANES = 128
GROUP = 8
CHUNKS = (56, 48, 24)
VMEM = 56 * 1024 * 1024
SCALE = 8


def layer_norm(values, gain):
    center = values - jnp.mean(values, axis=-1, keepdims=True)
    spread = jnp.mean(center * center, axis=-1, keepdims=True)
    return center * lax.rsqrt(spread + 1e-05) * gain


def project(values, weights):
    return jnp.einsum("...c,cd->...d", values, weights, precision=HIGH)


def outgoing(left_hand, right_hand):
    return jnp.einsum("bikc,bjkc->bijc", left_hand, right_hand, precision=HIGH)


def mirrored(values):
    columns = lax.all_to_all(values, ("row", "col"), split_axis=2, concat_axis=1, tiled=True)
    return jnp.swapaxes(columns, 1, 2)


def general_shards(
    pair,
    gain_input,
    weights_in,
    gate_weights,
    weights_out,
    gain_product,
    gain_transition,
    transition_in,
    transition_out,
    distogram_weights,
    distogram_bias,
):
    row_count = lax.axis_size("row")
    col_count = lax.axis_size("col")
    crops, tile_rows, tile_cols, width = pair.shape
    normed = layer_norm(pair, gain_input)
    projected = project(normed, weights_in)
    left_hand = jax.nn.sigmoid(projected[..., width : 2 * width]) * projected[..., :width]
    right_hand = jax.nn.sigmoid(projected[..., 3 * width :]) * projected[..., 2 * width : 3 * width]
    stacked = jnp.stack([left_hand, right_hand], axis=0)
    received = lax.all_to_all(stacked, ("row", "col"), split_axis=4, concat_axis=2, tiled=True)
    items = received.shape[1]
    owned = received.shape[4]
    square = received.reshape(2, items, row_count, col_count, tile_rows, tile_cols, owned)
    square = square.transpose(0, 1, 2, 4, 3, 5, 6).reshape(
        2, items, row_count * tile_rows, col_count * tile_cols, owned
    )
    result = outgoing(square[0], square[1])
    product = lax.all_to_all(result, ("row", "col"), split_axis=1, concat_axis=3, tiled=True)
    base = lax.all_to_all(pair, "col", split_axis=1, concat_axis=2, tiled=True)
    normed_base = layer_norm(base, gain_input)
    gate = jax.nn.sigmoid(project(normed_base, gate_weights))
    updated = base + gate * project(layer_norm(product, gain_product), weights_out)
    hidden = project(layer_norm(updated, gain_transition), transition_in)
    hidden_width = transition_out.shape[0]
    activated = jax.nn.silu(hidden[..., :hidden_width]) * hidden[..., hidden_width:]
    pair_out = updated + project(activated, transition_out)
    symmetric = pair_out + mirrored(pair_out)
    line_logits = project(symmetric, distogram_weights) + distogram_bias
    return lax.all_to_all(line_logits, "col", split_axis=2, concat_axis=1, tiled=True)


def split_weights(weights, gain=None):
    if gain is not None:
        weights = gain[:, None] * weights
    flipped = weights.T
    high = lax.reduce_precision(flipped, 8, 7)
    low = flipped - high
    return jnp.concatenate([high, high, low], axis=1).astype(jnp.bfloat16)


def estimate(flops, moved):
    return pl.CostEstimate(flops=flops // SCALE, bytes_accessed=moved // SCALE, transcendentals=0)


def parts(values):
    high = values.astype(jnp.bfloat16)
    low = (values - high.astype(jnp.float32)).astype(jnp.bfloat16)
    return high, low


def times(weights3, values):
    high, low = parts(values)
    return jnp.dot(
        weights3, jnp.concatenate([high, low, high], axis=0), preferred_element_type=jnp.float32
    )


def normalized(values):
    center = values - jnp.mean(values, axis=0, keepdims=True)
    spread = jnp.mean(center * center, axis=0, keepdims=True)
    return center * lax.rsqrt(spread + 1e-05)


def hands_kernel(pair_ref, weights_ref, out_ref):
    rows, _, width = pair_ref.shape
    per = 4
    flat = out_ref.reshape(width * rows, LANES)
    for start in range(0, rows, per):
        values = jnp.concatenate([pair_ref[start + n].T for n in range(per)], axis=1)
        projected = times(weights_ref[...], normalized(values))
        result = jax.nn.sigmoid(projected[width:]) * projected[:width]
        for n in range(per):
            flat[pl.ds(start + n, width, stride=rows), :] = result[:, n * LANES : (n + 1) * LANES]


def hands(pair, weights3, first, rows):
    _, tile_cols, width = pair.shape
    lead = first // GROUP
    return pl.pallas_call(
        hands_kernel,
        grid=(rows // GROUP,),
        in_specs=[
            pl.BlockSpec((GROUP, tile_cols, width), lambda g: (lead + g, 0, 0)),
            pl.BlockSpec(weights3.shape, lambda g: (0, 0)),
        ],
        out_specs=pl.BlockSpec((width, GROUP, tile_cols), lambda g: (0, g, 0)),
        out_shape=jax.ShapeDtypeStruct((width, rows, tile_cols), jnp.float32),
        compiler_params=pltpu.CompilerParams(vmem_limit_bytes=VMEM),
        cost_estimate=estimate(6 * rows * tile_cols * width * 2 * width, 8 * rows * tile_cols * width),
        name="hands",
    )(pair, weights3)


def product_kernel(left_ref, right_ref, out_ref):
    cols = right_ref.shape[1] // 2

    def lines(ref):
        return jnp.concatenate(
            [
                jnp.concatenate([ref[lo * cols + c, 0] for c in range(cols)], axis=1)
                for lo in range(2)
            ],
            axis=0,
        )

    left_high, left_low = parts(lines(left_ref))
    right_high, right_low = parts(
        jnp.concatenate([lines(right_ref.at[half]) for half in range(2)], axis=0)
    )
    result = lax.dot_general(
        jnp.concatenate([right_high, right_high, right_low], axis=1),
        jnp.concatenate([left_high, left_low, left_high], axis=1),
        (((1,), (1,)), ((), ())),
        preferred_element_type=jnp.float32,
    )
    rows = right_ref.shape[3]
    wide = result.shape[1] // 2
    for line in range(2):
        for plane in range(cols):
            out_ref[line * cols + plane, 0] = result[
                plane * rows : (plane + 1) * rows, line * wide : (line + 1) * wide
            ]


def product(left, right):
    _, sources, owned, rows, width = right.shape
    wide = left.shape[2]
    k_all = width * sources // 2
    return pl.pallas_call(
        product_kernel,
        grid=(owned,),
        in_specs=[
            pl.BlockSpec((sources, 1, wide, width), lambda n: (0, n, 0, 0)),
            pl.BlockSpec((2, sources, 1, rows, width), lambda n: (0, 0, n, 0, 0)),
        ],
        out_specs=pl.BlockSpec((sources, 1, rows, wide), lambda n: (0, n, 0, 0)),
        out_shape=jax.ShapeDtypeStruct((sources, owned, rows, wide), jnp.float32),
        compiler_params=pltpu.CompilerParams(vmem_limit_bytes=VMEM),
        cost_estimate=estimate(
            6 * owned * 4 * rows * 2 * wide * k_all, 4 * owned * k_all * (2 * wide + 4 * rows)
        ),
        name="product",
    )(left, right)


def head_kernel(
    pair_ref, product_ref, gate_ref, output_ref, up_ref, down_ref, bins_ref, out_ref
):
    tile_rows, cols, width = pair_ref.shape
    bins = out_ref.shape[1]
    per = 4
    flat_pair = pair_ref.reshape(tile_rows * cols, width)
    flat_product = product_ref.reshape(width * cols, tile_rows)
    hidden_width = up_ref.shape[0] // 2
    for start in range(0, cols, per):
        values = jnp.concatenate(
            [flat_pair[pl.ds(start + n, tile_rows, stride=cols), :].T for n in range(per)], axis=1
        )
        product_values = jnp.concatenate(
            [flat_product[pl.ds(start + n, width, stride=cols), :] for n in range(per)], axis=1
        )
        gate = jax.nn.sigmoid(times(gate_ref[...], normalized(values)))
        updated = values + gate * times(output_ref[...], normalized(product_values))
        hidden = times(up_ref[...], normalized(updated))
        activated = jax.nn.silu(hidden[:hidden_width]) * hidden[hidden_width:]
        pair_out = updated + times(down_ref[...], activated)
        logits = times(bins_ref[...], pair_out)
        for n in range(per):
            out_ref[start + n] = logits[:, n * tile_rows : (n + 1) * tile_rows]


def head(pair, product_values, first, gate3, output3, up3, down3, bins3):
    tile_rows, tile_cols, width = pair.shape
    chunk_cols = product_values.shape[1]
    steps = chunk_cols // GROUP
    lead = first // GROUP
    bins = bins3.shape[0]
    whole = lambda array: pl.BlockSpec(array.shape, lambda g: (0, 0))
    macs = gate3.size + output3.size + up3.size + down3.size + bins3.size
    return pl.pallas_call(
        head_kernel,
        grid=(steps,),
        in_specs=[
            pl.BlockSpec((tile_rows, GROUP, width), lambda g: (0, lead + g, 0)),
            pl.BlockSpec((width, GROUP, tile_rows), lambda g: (0, g, 0)),
            whole(gate3),
            whole(output3),
            whole(up3),
            whole(down3),
            whole(bins3),
        ],
        out_specs=pl.BlockSpec((GROUP, bins, tile_rows), lambda g: (g, 0, 0)),
        out_shape=jax.ShapeDtypeStruct((chunk_cols, bins, tile_rows), jnp.float32),
        compiler_params=pltpu.CompilerParams(vmem_limit_bytes=VMEM),
        cost_estimate=estimate(
            2 * chunk_cols * tile_rows * macs, 4 * chunk_cols * tile_rows * (2 * width + bins)
        ),
        name="head",
    )(pair, product_values, gate3, output3, up3, down3, bins3)


def mover(count):
    every = [(r, c) for r in range(count) for c in range(count)]

    def move(values, target):
        pairs = [(r * count + c, target(r, c)) for r, c in every]
        return lax.ppermute(values, ("half", "lo", "col"), pairs)

    return move


def swap_steps(count, turn):
    aside = lambda r, c: r * count + (c ^ r ^ turn)
    return [aside, lambda r, c: (c ^ r ^ turn) * count + c, aside]


def half_shards(
    pair,
    gain_input,
    weights_in,
    gate_weights,
    weights_out,
    gain_product,
    gain_transition,
    transition_in,
    transition_out,
    distogram_weights,
    distogram_bias,
):
    row_count = 2 * lax.axis_size("lo")
    col_count = lax.axis_size("col")
    _, tile_rows, tile_cols, width = pair.shape
    tile = pair[0]
    in3 = split_weights(weights_in, gain_input)
    left3, right3 = in3[: 2 * width], in3[2 * width :]
    gate3 = split_weights(gate_weights, gain_input)
    output3 = split_weights(weights_out, gain_product)
    up3 = split_weights(transition_in, gain_transition)
    down3 = split_weights(transition_out)
    bins3 = split_weights(distogram_weights)
    sources = 2 * col_count
    owned = width // sources

    def spread(values):
        values = values.reshape(sources, owned, *values.shape[1:])
        return lax.all_to_all(values, ("lo", "col"), split_axis=0, concat_axis=0, tiled=True)

    firsts = [sum(CHUNKS[:n]) for n in range(len(CHUNKS))]
    rights = [spread(hands(tile, right3, 0, CHUNKS[0]))]
    left = spread(hands(tile, left3, 0, tile_rows))
    later, left = lax.optimization_barrier((tile, left))
    for first, rows in zip(firsts[1:], CHUNKS[1:]):
        rights.append(spread(hands(later, right3, first, rows)))
    gathered = [lax.all_gather(right, "half") for right in rights]

    def product_and_spread(right):
        values = product(left, right)
        values = lax.all_to_all(values, ("lo", "col"), split_axis=0, concat_axis=0, tiled=True)
        return values.reshape(width, values.shape[2], tile_rows)

    def run_head(values, chunk):
        return head(tile, values, firsts[chunk], gate3, output3, up3, down3, bins3)

    move = mover(row_count)
    tie = lax.optimization_barrier
    way = [swap_steps(row_count, turn) for turn in range(2)]
    own = [run_head(product_and_spread(gathered[0]), 0)]
    mirror = [move(own[0], way[0][0])]
    right, mirror[0] = tie((gathered[1], mirror[0]))
    mirror[0] = move(mirror[0], way[0][1])
    values, mirror[0] = tie((product_and_spread(right), mirror[0]))
    own.append(run_head(values, 1))
    mirror[0] = move(mirror[0], way[0][2])
    mirror.append(move(own[1], way[1][0]))
    right, mirror = tie((gathered[2], mirror))
    mirror[1] = move(mirror[1], way[1][1])
    values, mirror = tie((product_and_spread(right), mirror))
    own.append(run_head(values, 2))
    mirror[1] = move(mirror[1], way[1][2])
    mirror.append(move(own[2], lambda r, c: c * row_count + r))
    turned = jnp.transpose(jnp.concatenate(own, axis=0), (2, 1, 0))
    logits = turned + jnp.concatenate(mirror, axis=0) + distogram_bias[None, :, None]
    return jnp.swapaxes(logits, 1, 2)[None]


def solution(mesh):
    names = mesh.axis_names
    crops, rows, cols = (mesh.shape[name] for name in names)

    def run(pair, *parameters):
        crop_count, height, across, width = pair.shape
        tile_rows, tile_cols = height // rows, across // cols
        by_halves = (
            crop_count == crops
            and rows == cols == 4
            and tile_rows == tile_cols == LANES
            and width == LANES
        )
        if by_halves:
            halves = Mesh(mesh.devices.reshape(crops, 2, rows // 2, cols), ("crop", "half", "lo", "col"))
            spec, used, body = P("crop", ("half", "lo"), "col", None), halves, half_shards
        else:
            spec, used, body = P("crop", "row", "col", None), mesh, general_shards
        return jax.shard_map(
            body,
            mesh=used,
            in_specs=(spec,) + (P(),) * len(parameters),
            out_specs=spec,
            check_vma=False,
        )(pair, *parameters)

    return run
```

```python
import functools

import jax
import jax.numpy as jnp
from jax import lax
from jax.experimental import pallas as pl
from jax.experimental.pallas import tpu as pltpu
from jax.sharding import Mesh, PartitionSpec as P

HIGH = lax.Precision.HIGHEST
LANES = 128
GROUP = 8
CHUNKS = (40, 56, 32)
VMEM = 56 * 1024 * 1024
SCALE = 8


def layer_norm(values, gain):
    center = values - jnp.mean(values, axis=-1, keepdims=True)
    spread = jnp.mean(center * center, axis=-1, keepdims=True)
    return center * lax.rsqrt(spread + 1e-05) * gain


def project(values, weights):
    return jnp.einsum("...c,cd->...d", values, weights, precision=HIGH)


def outgoing(left_hand, right_hand):
    return jnp.einsum("bikc,bjkc->bijc", left_hand, right_hand, precision=HIGH)


def mirrored(values):
    columns = lax.all_to_all(values, ("row", "col"), split_axis=2, concat_axis=1, tiled=True)
    return jnp.swapaxes(columns, 1, 2)


def general_shards(
    pair,
    gain_input,
    weights_in,
    gate_weights,
    weights_out,
    gain_product,
    gain_transition,
    transition_in,
    transition_out,
    distogram_weights,
    distogram_bias,
):
    row_count = lax.axis_size("row")
    col_count = lax.axis_size("col")
    crops, tile_rows, tile_cols, width = pair.shape
    normed = layer_norm(pair, gain_input)
    projected = project(normed, weights_in)
    left_hand = jax.nn.sigmoid(projected[..., width : 2 * width]) * projected[..., :width]
    right_hand = jax.nn.sigmoid(projected[..., 3 * width :]) * projected[..., 2 * width : 3 * width]
    stacked = jnp.stack([left_hand, right_hand], axis=0)
    received = lax.all_to_all(stacked, ("row", "col"), split_axis=4, concat_axis=2, tiled=True)
    items = received.shape[1]
    owned = received.shape[4]
    square = received.reshape(2, items, row_count, col_count, tile_rows, tile_cols, owned)
    square = square.transpose(0, 1, 2, 4, 3, 5, 6).reshape(
        2, items, row_count * tile_rows, col_count * tile_cols, owned
    )
    result = outgoing(square[0], square[1])
    product = lax.all_to_all(result, ("row", "col"), split_axis=1, concat_axis=3, tiled=True)
    base = lax.all_to_all(pair, "col", split_axis=1, concat_axis=2, tiled=True)
    normed_base = layer_norm(base, gain_input)
    gate = jax.nn.sigmoid(project(normed_base, gate_weights))
    updated = base + gate * project(layer_norm(product, gain_product), weights_out)
    hidden = project(layer_norm(updated, gain_transition), transition_in)
    hidden_width = transition_out.shape[0]
    activated = jax.nn.silu(hidden[..., :hidden_width]) * hidden[..., hidden_width:]
    pair_out = updated + project(activated, transition_out)
    symmetric = pair_out + mirrored(pair_out)
    line_logits = project(symmetric, distogram_weights) + distogram_bias
    return lax.all_to_all(line_logits, "col", split_axis=2, concat_axis=1, tiled=True)


def split_weights(weights, gain=None):
    if gain is not None:
        weights = gain[:, None] * weights
    flipped = weights.T
    high = lax.reduce_precision(flipped, 8, 7)
    low = flipped - high
    return jnp.concatenate([high, high, low], axis=1).astype(jnp.bfloat16)


def estimate(flops, moved):
    return pl.CostEstimate(flops=flops // SCALE, bytes_accessed=moved // SCALE, transcendentals=0)


def parts(values):
    high = values.astype(jnp.bfloat16)
    low = (values - high.astype(jnp.float32)).astype(jnp.bfloat16)
    return high, low


def times(weights3, values):
    high, low = parts(values)
    return jnp.dot(
        weights3, jnp.concatenate([high, low, high], axis=0), preferred_element_type=jnp.float32
    )


def normalized(values):
    center = values - jnp.mean(values, axis=0, keepdims=True)
    spread = jnp.mean(center * center, axis=0, keepdims=True)
    return center * lax.rsqrt(spread + 1e-05)


def hands_kernel(pair_ref, weights_ref, out_ref):
    rows, _, width = pair_ref.shape
    per = 4
    flat = out_ref.reshape(width * rows, LANES)
    for start in range(0, rows, per):
        values = jnp.concatenate([pair_ref[start + n].T for n in range(per)], axis=1)
        projected = times(weights_ref[...], normalized(values))
        result = jax.nn.sigmoid(projected[width:]) * projected[:width]
        for n in range(per):
            flat[pl.ds(start + n, width, stride=rows), :] = result[:, n * LANES : (n + 1) * LANES]


def hands(pair, weights3, left, right):
    _, tile_cols, width = pair.shape
    rows = left[1] + right[1]
    turn = left[1] // GROUP
    lead, shift = left[0] // GROUP, right[0] // GROUP - turn
    return pl.pallas_call(
        hands_kernel,
        grid=(rows // GROUP,),
        in_specs=[
            pl.BlockSpec((GROUP, tile_cols, width), lambda g: (g + jnp.where(g < turn, lead, shift), 0, 0)),
            pl.BlockSpec((2 * width, 3 * width), lambda g: (jnp.where(g < turn, 0, 1), 0)),
        ],
        out_specs=pl.BlockSpec((width, GROUP, tile_cols), lambda g: (0, g, 0)),
        out_shape=jax.ShapeDtypeStruct((width, rows, tile_cols), jnp.float32),
        compiler_params=pltpu.CompilerParams(vmem_limit_bytes=VMEM),
        cost_estimate=estimate(6 * rows * tile_cols * width * 2 * width, 8 * rows * tile_cols * width),
        name="hands",
    )(pair, weights3)


def product_kernel(low_ref, high_ref, right_ref, out_ref):
    cols = right_ref.shape[1] // 2

    def line(ref, lo):
        return jnp.concatenate([ref[lo * cols + c, 0] for c in range(cols)], axis=1)

    left_high, left_low = parts(
        jnp.concatenate([line(ref, lo) for lo in range(2) for ref in (low_ref, high_ref)], axis=0)
    )
    right_high, right_low = parts(
        jnp.concatenate([line(right_ref.at[half], lo) for half in range(2) for lo in range(2)], axis=0)
    )
    result = lax.dot_general(
        jnp.concatenate([right_high, right_high, right_low], axis=1),
        jnp.concatenate([left_high, left_low, left_high], axis=1),
        (((1,), (1,)), ((), ())),
        preferred_element_type=jnp.float32,
    )
    rows = right_ref.shape[3]
    wide = result.shape[1] // 2
    for lo in range(2):
        for plane in range(cols):
            out_ref[lo * cols + plane, 0] = result[
                plane * rows : (plane + 1) * rows, lo * wide : (lo + 1) * wide
            ]


def product(low, high, right, wide):
    _, sources, owned, rows, width = right.shape
    k_all = width * sources // 2
    return pl.pallas_call(
        product_kernel,
        grid=(owned,),
        in_specs=[
            pl.BlockSpec((sources, 1, wide // 2, width), lambda n: (0, n, 0, 0)),
            pl.BlockSpec((sources, 1, wide // 2, width), lambda n: (0, n, 0, 0)),
            pl.BlockSpec((2, sources, 1, rows, width), lambda n: (0, 0, n, 0, 0)),
        ],
        out_specs=pl.BlockSpec((sources, 1, rows, wide), lambda n: (0, n, 0, 0)),
        out_shape=jax.ShapeDtypeStruct((sources, owned, rows, wide), jnp.float32),
        compiler_params=pltpu.CompilerParams(vmem_limit_bytes=VMEM),
        cost_estimate=estimate(
            6 * owned * 4 * rows * 2 * wide * k_all, 4 * owned * k_all * (2 * wide + 4 * rows)
        ),
        name="product",
    )(low, high, right)


def head_kernel(
    pair_ref, product_ref, gate_ref, output_ref, up_ref, down_ref, bins_ref, *out_refs
):
    tile_rows, cols, width = pair_ref.shape
    bins = out_refs[0].shape[1]
    per = 4
    flat_pair = pair_ref.reshape(tile_rows * cols, width)
    flat_product = product_ref.reshape(width * cols, tile_rows)
    hidden_width = up_ref.shape[0] // 2
    for start in range(0, cols, per):
        values = jnp.concatenate(
            [flat_pair[pl.ds(start + n, tile_rows, stride=cols), :].T for n in range(per)], axis=1
        )
        product_values = jnp.concatenate(
            [flat_product[pl.ds(start + n, width, stride=cols), :] for n in range(per)], axis=1
        )
        gate = jax.nn.sigmoid(times(gate_ref[...], normalized(values)))
        updated = values + gate * times(output_ref[...], normalized(product_values))
        hidden = times(up_ref[...], normalized(updated))
        activated = jax.nn.silu(hidden[:hidden_width]) * hidden[hidden_width:]
        pair_out = updated + times(down_ref[...], activated)
        logits = times(bins_ref[...], pair_out)
        for n in range(per):
            for part, out_ref in enumerate(out_refs):
                out_ref[start + n] = logits[
                    part * bins : (part + 1) * bins, n * tile_rows : (n + 1) * tile_rows
                ]


def head(pair, product_values, first, gate3, output3, up3, down3, bins3):
    tile_rows, tile_cols, width = pair.shape
    chunk_cols = product_values.shape[1]
    steps = chunk_cols // GROUP
    lead = first // GROUP
    bins = bins3.shape[0] // 2
    whole = lambda array: pl.BlockSpec(array.shape, lambda g: (0, 0))
    macs = gate3.size + output3.size + up3.size + down3.size + bins3.size
    return pl.pallas_call(
        head_kernel,
        grid=(steps,),
        in_specs=[
            pl.BlockSpec((tile_rows, GROUP, width), lambda g: (0, lead + g, 0)),
            pl.BlockSpec((width, GROUP, tile_rows), lambda g: (0, g, 0)),
            whole(gate3),
            whole(output3),
            whole(up3),
            whole(down3),
            whole(bins3),
        ],
        out_specs=[pl.BlockSpec((GROUP, bins, tile_rows), lambda g: (g, 0, 0))] * 2,
        out_shape=[jax.ShapeDtypeStruct((chunk_cols, bins, tile_rows), jnp.float32)] * 2,
        compiler_params=pltpu.CompilerParams(vmem_limit_bytes=VMEM),
        cost_estimate=estimate(
            2 * chunk_cols * tile_rows * macs, 4 * chunk_cols * tile_rows * 2 * (width + bins)
        ),
        name="head",
    )(pair, product_values, gate3, output3, up3, down3, bins3)


def turned_kernel(bias_ref, *refs):
    out_ref, sources = refs[-1], refs[:-1]
    count = len(sources) // 2
    tile_rows, _, bins, tile_cols = out_ref.shape
    flat = out_ref.reshape(tile_rows * 2 * bins, tile_cols)
    for part in range(2):
        for n in range(bins):
            values = [
                ref.reshape(ref.shape[0] * bins, tile_rows)[pl.ds(n, ref.shape[0], stride=bins), :]
                for ref in sources[part * count : (part + 1) * count]
            ]
            result = jnp.concatenate(values, axis=0).T + bias_ref[part, n : n + 1, :]
            flat[pl.ds(part * bins + n, tile_rows, stride=2 * bins), :] = result


def turned(bias, own):
    arrays = [block[part] for part in range(2) for block in own]
    _, bins, tile_rows = arrays[0].shape
    tile_cols = sum(block[0].shape[0] for block in own)
    block = lambda rows: pl.BlockSpec((rows, GROUP, tile_rows), lambda g: (0, g, 0))
    return pl.pallas_call(
        turned_kernel,
        grid=(bins // GROUP,),
        in_specs=[pl.BlockSpec((2, GROUP, tile_cols), lambda g: (0, g, 0))]
        + [block(array.shape[0]) for array in arrays],
        out_specs=pl.BlockSpec((tile_rows, 2, GROUP, tile_cols), lambda g: (0, 0, g, 0)),
        out_shape=jax.ShapeDtypeStruct((tile_rows, 2, bins, tile_cols), jnp.float32),
        compiler_params=pltpu.CompilerParams(vmem_limit_bytes=VMEM),
        cost_estimate=estimate(0, 8 * tile_rows * 2 * bins * tile_cols),
        name="turned",
    )(bias, *arrays)


def joined_kernel(base_ref, low_ref, high_ref, out_ref):
    out_ref[:, 0] = base_ref[:, 0] + low_ref[...]
    out_ref[:, 1] = base_ref[:, 1] + high_ref[...]


def joined(base, mirror, first):
    rows, bins, tile_cols = mirror[0].shape
    lead = first // GROUP
    whole = pl.BlockSpec((GROUP, 2, bins, tile_cols), lambda g: (lead + g, 0, 0, 0))
    block = pl.BlockSpec((GROUP, bins, tile_cols), lambda g: (g, 0, 0))
    return pl.pallas_call(
        joined_kernel,
        grid=(rows // GROUP,),
        in_specs=[whole, block, block],
        out_specs=whole,
        out_shape=jax.ShapeDtypeStruct(base.shape, jnp.float32),
        input_output_aliases={0: 0},
        compiler_params=pltpu.CompilerParams(vmem_limit_bytes=VMEM),
        cost_estimate=estimate(0, 24 * rows * bins * tile_cols),
        name="joined",
    )(base, *mirror)


def mirrored_halves(block, count):
    every = [(r, c) for r in range(count) for c in range(count)]

    def move(values, target):
        pairs = [(r * count + c, target(r, c)) for r, c in every]
        return lax.ppermute(values, ("half", "lo", "col"), pairs)

    low = move(block[0], lambda r, c: c * count + r)
    high = move(block[1], lambda r, c: r * count + (c ^ 2))
    return low, move(high, lambda r, c: (c ^ 2) * count + r)


def half_shards(
    pair,
    gain_input,
    weights_in,
    gate_weights,
    weights_out,
    gain_product,
    gain_transition,
    transition_in,
    transition_out,
    distogram_weights,
    distogram_bias,
):
    row_count = 2 * lax.axis_size("lo")
    col_count = lax.axis_size("col")
    _, tile_rows, tile_cols, width = pair.shape
    tile = pair[0]
    in3 = split_weights(weights_in, gain_input)
    gate3 = split_weights(gate_weights, gain_input)
    output3 = split_weights(weights_out, gain_product)
    up3 = split_weights(transition_in, gain_transition)
    down3 = split_weights(transition_out)
    bins3 = split_weights(distogram_weights)
    sources = 2 * col_count
    owned = width // sources

    def spread(values):
        values = values.reshape(sources, owned, *values.shape[1:])
        return lax.all_to_all(values, ("lo", "col"), split_axis=0, concat_axis=0, tiled=True)

    tie = lax.optimization_barrier
    firsts = [sum(CHUNKS[:n]) for n in range(len(CHUNKS))]
    lower = tile_rows // 2

    def gather(values, first):
        return lax.all_gather(values[:, :, first:], "half")

    sent = [
        hands(tile, in3, (0, 0), (firsts[0], CHUNKS[0])),
        hands(tile, in3, (0, lower), (firsts[1], CHUNKS[1])),
        hands(tile, in3, (lower, lower), (firsts[2], CHUNKS[2])),
    ]
    gathered = [gather(spread(sent[0]), 0)]
    low = spread(sent[1])
    gathered.append(gather(low, lower))
    gathered[0], sent[2] = tie((gathered[0], sent[2]))
    high = spread(sent[2])
    gathered.append(gather(high, lower))

    def blocks(right):
        return product(low, high, right, tile_rows)

    def finish(values, chunk):
        values = lax.all_to_all(values, ("lo", "col"), split_axis=0, concat_axis=0, tiled=True)
        values = values.reshape(width, CHUNKS[chunk], tile_rows)
        return head(tile, values, firsts[chunk], gate3, output3, up3, down3, bins3)

    own = [finish(blocks(gathered[0]), 0)]
    mirror = [mirrored_halves(own[0], row_count)]
    values, gathered[2], mirror[0] = tie((blocks(gathered[1]), gathered[2], mirror[0]))
    own.append(finish(values, 1))
    own.append(finish(blocks(gathered[2]), 2))
    mirror += [mirrored_halves(block, row_count) for block in own[1:]]
    bins = distogram_bias.shape[0] // 2
    bias = jnp.broadcast_to(distogram_bias.reshape(2, bins, 1), (2, bins, tile_cols))
    logits = turned(bias, own)
    for first, block in zip(firsts, mirror):
        logits = joined(logits, block, first)
    logits = logits.reshape(tile_rows, 2 * bins, tile_cols)
    return jnp.swapaxes(logits, 1, 2)[None]


def solution(mesh):
    names = mesh.axis_names
    crops, rows, cols = (mesh.shape[name] for name in names)

    def run(pair, *parameters):
        crop_count, height, across, width = pair.shape
        tile_rows, tile_cols = height // rows, across // cols
        by_halves = (
            crop_count == crops
            and rows == cols == 4
            and tile_rows == tile_cols == LANES
            and width == LANES
        )
        if by_halves:
            halves = Mesh(mesh.devices.reshape(crops, 2, rows // 2, cols), ("crop", "half", "lo", "col"))
            spec, used, body = P("crop", ("half", "lo"), "col", None), halves, half_shards
        else:
            spec, used, body = P("crop", "row", "col", None), mesh, general_shards
        return jax.shard_map(
            body,
            mesh=used,
            in_specs=(spec,) + (P(),) * len(parameters),
            out_specs=spec,
            check_vma=False,
        )(pair, *parameters)

    return run
```

```python
import functools

import jax
import jax.numpy as jnp
from jax import lax
from jax.experimental import pallas as pl
from jax.experimental.pallas import tpu as pltpu
from jax.sharding import Mesh, PartitionSpec as P

HIGH = lax.Precision.HIGHEST
LANES = 128
GROUP = 8
CHUNKS = (40, 56, 32)
LOWER = 40
PARTS = 4
VMEM = 56 * 1024 * 1024
SCALE = 8


def layer_norm(values, gain):
    center = values - jnp.mean(values, axis=-1, keepdims=True)
    spread = jnp.mean(center * center, axis=-1, keepdims=True)
    return center * lax.rsqrt(spread + 1e-05) * gain


def project(values, weights):
    return jnp.einsum("...c,cd->...d", values, weights, precision=HIGH)


def outgoing(left_hand, right_hand):
    return jnp.einsum("bikc,bjkc->bijc", left_hand, right_hand, precision=HIGH)


def mirrored(values):
    columns = lax.all_to_all(values, ("row", "col"), split_axis=2, concat_axis=1, tiled=True)
    return jnp.swapaxes(columns, 1, 2)


def general_shards(
    pair,
    gain_input,
    weights_in,
    gate_weights,
    weights_out,
    gain_product,
    gain_transition,
    transition_in,
    transition_out,
    distogram_weights,
    distogram_bias,
):
    row_count = lax.axis_size("row")
    col_count = lax.axis_size("col")
    crops, tile_rows, tile_cols, width = pair.shape
    normed = layer_norm(pair, gain_input)
    projected = project(normed, weights_in)
    left_hand = jax.nn.sigmoid(projected[..., width : 2 * width]) * projected[..., :width]
    right_hand = jax.nn.sigmoid(projected[..., 3 * width :]) * projected[..., 2 * width : 3 * width]
    stacked = jnp.stack([left_hand, right_hand], axis=0)
    received = lax.all_to_all(stacked, ("row", "col"), split_axis=4, concat_axis=2, tiled=True)
    items = received.shape[1]
    owned = received.shape[4]
    square = received.reshape(2, items, row_count, col_count, tile_rows, tile_cols, owned)
    square = square.transpose(0, 1, 2, 4, 3, 5, 6).reshape(
        2, items, row_count * tile_rows, col_count * tile_cols, owned
    )
    result = outgoing(square[0], square[1])
    product = lax.all_to_all(result, ("row", "col"), split_axis=1, concat_axis=3, tiled=True)
    base = lax.all_to_all(pair, "col", split_axis=1, concat_axis=2, tiled=True)
    normed_base = layer_norm(base, gain_input)
    gate = jax.nn.sigmoid(project(normed_base, gate_weights))
    updated = base + gate * project(layer_norm(product, gain_product), weights_out)
    hidden = project(layer_norm(updated, gain_transition), transition_in)
    hidden_width = transition_out.shape[0]
    activated = jax.nn.silu(hidden[..., :hidden_width]) * hidden[..., hidden_width:]
    pair_out = updated + project(activated, transition_out)
    symmetric = pair_out + mirrored(pair_out)
    line_logits = project(symmetric, distogram_weights) + distogram_bias
    return lax.all_to_all(line_logits, "col", split_axis=2, concat_axis=1, tiled=True)


def split_weights(weights, gain=None):
    if gain is not None:
        weights = gain[:, None] * weights
    flipped = weights.T
    high = lax.reduce_precision(flipped, 8, 7)
    low = flipped - high
    return jnp.concatenate([high, high, low], axis=1).astype(jnp.bfloat16)


def estimate(flops, moved):
    return pl.CostEstimate(flops=flops // SCALE, bytes_accessed=moved // SCALE, transcendentals=0)


def parts(values):
    high = values.astype(jnp.bfloat16)
    low = (values - high.astype(jnp.float32)).astype(jnp.bfloat16)
    return high, low


def times(weights3, values):
    high, low = parts(values)
    return jnp.dot(
        weights3, jnp.concatenate([high, low, high], axis=0), preferred_element_type=jnp.float32
    )


def normalized(values):
    center = values - jnp.mean(values, axis=0, keepdims=True)
    spread = jnp.mean(center * center, axis=0, keepdims=True)
    return center * lax.rsqrt(spread + 1e-05)


def hands_kernel(pair_ref, weights_ref, out_ref):
    rows, _, width = pair_ref.shape
    per = 4
    flat = out_ref.reshape(width * rows, LANES)
    for start in range(0, rows, per):
        values = jnp.concatenate([pair_ref[start + n].T for n in range(per)], axis=1)
        projected = times(weights_ref[...], normalized(values))
        result = jax.nn.sigmoid(projected[width:]) * projected[:width]
        for n in range(per):
            flat[pl.ds(start + n, width, stride=rows), :] = result[:, n * LANES : (n + 1) * LANES]


def hands(pair, weights3, left, right):
    _, tile_cols, width = pair.shape
    rows = left[1] + right[1]
    turn = left[1] // GROUP
    lead, shift = left[0] // GROUP, right[0] // GROUP - turn
    return pl.pallas_call(
        hands_kernel,
        grid=(rows // GROUP,),
        in_specs=[
            pl.BlockSpec((GROUP, tile_cols, width), lambda g: (g + jnp.where(g < turn, lead, shift), 0, 0)),
            pl.BlockSpec((2 * width, 3 * width), lambda g: (jnp.where(g < turn, 0, 1), 0)),
        ],
        out_specs=pl.BlockSpec((width, GROUP, tile_cols), lambda g: (0, g, 0)),
        out_shape=jax.ShapeDtypeStruct((width, rows, tile_cols), jnp.float32),
        compiler_params=pltpu.CompilerParams(vmem_limit_bytes=VMEM),
        cost_estimate=estimate(6 * rows * tile_cols * width * 2 * width, 8 * rows * tile_cols * width),
        name="hands",
    )(pair, weights3)


def product_kernel(half_ref, low_ref, high_ref, own_ref, other_ref, out_ref):
    cols = own_ref.shape[0] // 2
    half = half_ref[0]

    def line(ref, lo):
        return jnp.concatenate([ref[lo * cols + c, 0] for c in range(cols)], axis=1)

    left_high, left_low = parts(
        jnp.concatenate([line(ref, lo) for lo in range(2) for ref in (low_ref, high_ref)], axis=0)
    )
    right_high, right_low = parts(
        jnp.concatenate([line(ref, lo) for ref in (own_ref, other_ref) for lo in range(2)], axis=0)
    )
    result = lax.dot_general(
        jnp.concatenate([right_high, right_high, right_low], axis=1),
        jnp.concatenate([left_high, left_low, left_high], axis=1),
        (((1,), (1,)), ((), ())),
        preferred_element_type=jnp.float32,
    )
    rows = own_ref.shape[2]
    wide = result.shape[1] // 2
    for lo in range(2):
        for piece in range(cols):
            source, other_lo = divmod(piece, 2)
            plane = 2 * jnp.where(half == source, 0, 1) + other_lo
            out_ref[lo * cols + plane, 0] = result[
                piece * rows : (piece + 1) * rows, lo * wide : (lo + 1) * wide
            ]


def product(half, low, high, own, other, wide):
    sources, owned, rows, width = own.shape
    k_all = width * sources // 2
    spec = lambda height: pl.BlockSpec((sources, 1, height, width), lambda n, half: (0, n, 0, 0))
    return pl.pallas_call(
        product_kernel,
        grid_spec=pltpu.PrefetchScalarGridSpec(
            num_scalar_prefetch=1,
            grid=(owned,),
            in_specs=[spec(LOWER), spec(wide - LOWER), spec(rows), spec(rows)],
            out_specs=pl.BlockSpec((sources, 1, rows, wide), lambda n, half: (0, n, 0, 0)),
        ),
        out_shape=jax.ShapeDtypeStruct((sources, owned, rows, wide), jnp.float32),
        compiler_params=pltpu.CompilerParams(vmem_limit_bytes=VMEM),
        cost_estimate=estimate(
            6 * owned * 4 * rows * 2 * wide * k_all, 4 * owned * k_all * (2 * wide + 4 * rows)
        ),
        name="product",
    )(half, low, high, own, other)


def head_kernel(
    pair_ref, product_ref, gate_ref, output_ref, up_ref, down_ref, bins_ref, *out_refs
):
    tile_rows, cols, width = pair_ref.shape
    bins = out_refs[0].shape[1]
    per = 4
    flat_pair = pair_ref.reshape(tile_rows * cols, width)
    flat_product = product_ref.reshape(width * cols, tile_rows)
    hidden_width = up_ref.shape[0] // 2
    for start in range(0, cols, per):
        values = jnp.concatenate(
            [flat_pair[pl.ds(start + n, tile_rows, stride=cols), :].T for n in range(per)], axis=1
        )
        product_values = jnp.concatenate(
            [flat_product[pl.ds(start + n, width, stride=cols), :] for n in range(per)], axis=1
        )
        gate = jax.nn.sigmoid(times(gate_ref[...], normalized(values)))
        updated = values + gate * times(output_ref[...], normalized(product_values))
        hidden = times(up_ref[...], normalized(updated))
        activated = jax.nn.silu(hidden[:hidden_width]) * hidden[hidden_width:]
        pair_out = updated + times(down_ref[...], activated)
        logits = times(bins_ref[...], pair_out)
        for n in range(per):
            for part, out_ref in enumerate(out_refs):
                out_ref[start + n] = logits[
                    part * bins : (part + 1) * bins, n * tile_rows : (n + 1) * tile_rows
                ]


def head(pair, product_values, first, gate3, output3, up3, down3, bins3):
    tile_rows, tile_cols, width = pair.shape
    chunk_cols = product_values.shape[1]
    steps = chunk_cols // GROUP
    lead = first // GROUP
    bins = bins3.shape[0] // PARTS
    whole = lambda array: pl.BlockSpec(array.shape, lambda g: (0, 0))
    macs = gate3.size + output3.size + up3.size + down3.size + bins3.size
    return pl.pallas_call(
        head_kernel,
        grid=(steps,),
        in_specs=[
            pl.BlockSpec((tile_rows, GROUP, width), lambda g: (0, lead + g, 0)),
            pl.BlockSpec((width, GROUP, tile_rows), lambda g: (0, g, 0)),
            whole(gate3),
            whole(output3),
            whole(up3),
            whole(down3),
            whole(bins3),
        ],
        out_specs=[pl.BlockSpec((GROUP, bins, tile_rows), lambda g: (g, 0, 0))] * PARTS,
        out_shape=[jax.ShapeDtypeStruct((chunk_cols, bins, tile_rows), jnp.float32)] * PARTS,
        compiler_params=pltpu.CompilerParams(vmem_limit_bytes=VMEM),
        cost_estimate=estimate(
            2 * chunk_cols * tile_rows * macs, 4 * chunk_cols * tile_rows * (2 * width + PARTS * bins)
        ),
        name="head",
    )(pair, product_values, gate3, output3, up3, down3, bins3)


def turned_kernel(bias_ref, *refs):
    out_ref, sources = refs[-1], refs[:-1]
    count = len(sources) // PARTS
    tile_rows, _, bins, tile_cols = out_ref.shape
    flat = out_ref.reshape(tile_rows * PARTS * bins, tile_cols)
    for part in range(PARTS):
        for n in range(bins):
            values = [
                ref.reshape(ref.shape[0] * bins, tile_rows)[pl.ds(n, ref.shape[0], stride=bins), :]
                for ref in sources[part * count : (part + 1) * count]
            ]
            result = jnp.concatenate(values, axis=0).T + bias_ref[part, n : n + 1, :]
            flat[pl.ds(part * bins + n, tile_rows, stride=PARTS * bins), :] = result


def turned(bias, own):
    arrays = [block[part] for part in range(PARTS) for block in own]
    _, bins, tile_rows = arrays[0].shape
    tile_cols = sum(block[0].shape[0] for block in own)
    block = lambda rows: pl.BlockSpec((rows, GROUP, tile_rows), lambda g: (0, g, 0))
    return pl.pallas_call(
        turned_kernel,
        grid=(bins // GROUP,),
        in_specs=[pl.BlockSpec((PARTS, GROUP, tile_cols), lambda g: (0, g, 0))]
        + [block(array.shape[0]) for array in arrays],
        out_specs=pl.BlockSpec((tile_rows, PARTS, GROUP, tile_cols), lambda g: (0, 0, g, 0)),
        out_shape=jax.ShapeDtypeStruct((tile_rows, PARTS, bins, tile_cols), jnp.float32),
        compiler_params=pltpu.CompilerParams(vmem_limit_bytes=VMEM),
        cost_estimate=estimate(0, 8 * tile_rows * PARTS * bins * tile_cols),
        name="turned",
    )(bias, *arrays)


def joined_kernel(base_ref, *refs):
    out_ref = refs[-1]
    for part, ref in enumerate(refs[:-1]):
        out_ref[:, part] = base_ref[:, part] + ref[...]


def joined(base, mirror, first):
    rows, bins, tile_cols = mirror[0].shape
    lead = first // GROUP
    whole = pl.BlockSpec((GROUP, PARTS, bins, tile_cols), lambda g: (lead + g, 0, 0, 0))
    block = pl.BlockSpec((GROUP, bins, tile_cols), lambda g: (g, 0, 0))
    return pl.pallas_call(
        joined_kernel,
        grid=(rows // GROUP,),
        in_specs=[whole] + [block] * PARTS,
        out_specs=whole,
        out_shape=jax.ShapeDtypeStruct(base.shape, jnp.float32),
        input_output_aliases={0: 0},
        compiler_params=pltpu.CompilerParams(vmem_limit_bytes=VMEM),
        cost_estimate=estimate(0, 12 * PARTS * rows * bins * tile_cols),
        name="joined",
    )(base, *mirror)


def mirrored_parts(block, count):
    every = [(r, c) for r in range(count) for c in range(count)]

    def move(values, target):
        pairs = [(r * count + c, target(r, c)) for r, c in every]
        return lax.ppermute(values, ("half", "lo", "col"), pairs)

    result = []
    for part, values in enumerate(block):
        if part:
            values = move(values, lambda r, c: r * count + (c ^ part))
        result.append(move(values, lambda r, c: (c ^ part) * count + r))
    return result


def half_shards(
    pair,
    gain_input,
    weights_in,
    gate_weights,
    weights_out,
    gain_product,
    gain_transition,
    transition_in,
    transition_out,
    distogram_weights,
    distogram_bias,
):
    row_count = 2 * lax.axis_size("lo")
    col_count = lax.axis_size("col")
    _, tile_rows, tile_cols, width = pair.shape
    tile = pair[0]
    in3 = split_weights(weights_in, gain_input)
    gate3 = split_weights(gate_weights, gain_input)
    output3 = split_weights(weights_out, gain_product)
    up3 = split_weights(transition_in, gain_transition)
    down3 = split_weights(transition_out)
    bins3 = split_weights(distogram_weights)
    sources = 2 * col_count
    owned = width // sources

    def spread(values):
        values = values.reshape(sources, owned, *values.shape[1:])
        return lax.all_to_all(values, ("lo", "col"), split_axis=0, concat_axis=0, tiled=True)

    tie = lax.optimization_barrier
    half = lax.axis_index("half").astype(jnp.int32).reshape(1)
    firsts = [sum(CHUNKS[:n]) for n in range(len(CHUNKS))]
    upper = tile_rows - LOWER

    def exchange(values):
        return lax.ppermute(values, "half", [(0, 1), (1, 0)])

    def finish(values, chunk):
        values = lax.all_to_all(values, ("lo", "col"), split_axis=0, concat_axis=0, tiled=True)
        values = values.reshape(width, CHUNKS[chunk], tile_rows)
        return head(tile, values, firsts[chunk], gate3, output3, up3, down3, bins3)

    right = spread(hands(tile, in3, (0, 0), (firsts[0], CHUNKS[0])))
    rights, others = [right], [exchange(right)]
    low = spread(hands(tile, in3, (0, LOWER), (firsts[1], CHUNKS[1])))
    rights.append(low[:, :, LOWER:])
    others.append(exchange(rights[1]))
    sent = hands(tile, in3, (LOWER, upper), (firsts[2], CHUNKS[2]))
    sent, others[0] = tie((sent, others[0]))
    high = spread(sent)
    rights.append(high[:, :, upper:])
    others.append(exchange(rights[2]))

    def blocks(chunk):
        return product(half, low, high, rights[chunk], others[chunk], tile_rows)

    values, others[1] = tie((blocks(0), others[1]))
    own = [finish(values, 0)]
    mirror = [mirrored_parts(own[0], row_count)]
    values, others[2], mirror[0] = tie((blocks(1), others[2], mirror[0]))
    own.append(finish(values, 1))
    own.append(finish(blocks(2), 2))
    mirror += [mirrored_parts(block, row_count) for block in own[1:]]
    bins = distogram_bias.shape[0] // PARTS
    bias = jnp.broadcast_to(distogram_bias.reshape(PARTS, bins, 1), (PARTS, bins, tile_cols))
    logits = turned(bias, own)
    for first, block in zip(firsts, mirror):
        logits = joined(logits, block, first)
    logits = logits.reshape(tile_rows, PARTS * bins, tile_cols)
    return jnp.swapaxes(logits, 1, 2)[None]


def solution(mesh):
    names = mesh.axis_names
    crops, rows, cols = (mesh.shape[name] for name in names)

    def run(pair, *parameters):
        crop_count, height, across, width = pair.shape
        tile_rows, tile_cols = height // rows, across // cols
        by_halves = (
            crop_count == crops
            and rows == cols == 4
            and tile_rows == tile_cols == LANES
            and width == LANES
        )
        if by_halves:
            halves = Mesh(mesh.devices.reshape(crops, 2, rows // 2, cols), ("crop", "half", "lo", "col"))
            spec, used, body = P("crop", ("half", "lo"), "col", None), halves, half_shards
        else:
            spec, used, body = P("crop", "row", "col", None), mesh, general_shards
        return jax.shard_map(
            body,
            mesh=used,
            in_specs=(spec,) + (P(),) * len(parameters),
            out_specs=spec,
            check_vma=False,
        )(pair, *parameters)

    return run
```

```python
import functools

import jax
import jax.numpy as jnp
from jax import lax
from jax.experimental import pallas as pl
from jax.experimental.pallas import tpu as pltpu
from jax.sharding import Mesh, PartitionSpec as P

HIGH = lax.Precision.HIGHEST
LANES = 128
GROUP = 8
CHUNKS = (40, 40, 48)
LOWER = 48
PARTS = (4, 2)
VMEM = 56 * 1024 * 1024
SCALE = 8


def layer_norm(values, gain):
    center = values - jnp.mean(values, axis=-1, keepdims=True)
    spread = jnp.mean(center * center, axis=-1, keepdims=True)
    return center * lax.rsqrt(spread + 1e-05) * gain


def project(values, weights):
    return jnp.einsum("...c,cd->...d", values, weights, precision=HIGH)


def outgoing(left_hand, right_hand):
    return jnp.einsum("bikc,bjkc->bijc", left_hand, right_hand, precision=HIGH)


def mirrored(values):
    columns = lax.all_to_all(values, ("row", "col"), split_axis=2, concat_axis=1, tiled=True)
    return jnp.swapaxes(columns, 1, 2)


def general_shards(
    pair,
    gain_input,
    weights_in,
    gate_weights,
    weights_out,
    gain_product,
    gain_transition,
    transition_in,
    transition_out,
    distogram_weights,
    distogram_bias,
):
    row_count = lax.axis_size("row")
    col_count = lax.axis_size("col")
    crops, tile_rows, tile_cols, width = pair.shape
    normed = layer_norm(pair, gain_input)
    projected = project(normed, weights_in)
    left_hand = jax.nn.sigmoid(projected[..., width : 2 * width]) * projected[..., :width]
    right_hand = jax.nn.sigmoid(projected[..., 3 * width :]) * projected[..., 2 * width : 3 * width]
    stacked = jnp.stack([left_hand, right_hand], axis=0)
    received = lax.all_to_all(stacked, ("row", "col"), split_axis=4, concat_axis=2, tiled=True)
    items = received.shape[1]
    owned = received.shape[4]
    square = received.reshape(2, items, row_count, col_count, tile_rows, tile_cols, owned)
    square = square.transpose(0, 1, 2, 4, 3, 5, 6).reshape(
        2, items, row_count * tile_rows, col_count * tile_cols, owned
    )
    result = outgoing(square[0], square[1])
    product = lax.all_to_all(result, ("row", "col"), split_axis=1, concat_axis=3, tiled=True)
    base = lax.all_to_all(pair, "col", split_axis=1, concat_axis=2, tiled=True)
    normed_base = layer_norm(base, gain_input)
    gate = jax.nn.sigmoid(project(normed_base, gate_weights))
    updated = base + gate * project(layer_norm(product, gain_product), weights_out)
    hidden = project(layer_norm(updated, gain_transition), transition_in)
    hidden_width = transition_out.shape[0]
    activated = jax.nn.silu(hidden[..., :hidden_width]) * hidden[..., hidden_width:]
    pair_out = updated + project(activated, transition_out)
    symmetric = pair_out + mirrored(pair_out)
    line_logits = project(symmetric, distogram_weights) + distogram_bias
    return lax.all_to_all(line_logits, "col", split_axis=2, concat_axis=1, tiled=True)


def split_weights(weights, gain=None):
    if gain is not None:
        weights = gain[:, None] * weights
    flipped = weights.T
    high = lax.reduce_precision(flipped, 8, 7)
    low = flipped - high
    return jnp.concatenate([high, high, low], axis=1).astype(jnp.bfloat16)


def estimate(flops, moved):
    return pl.CostEstimate(flops=flops // SCALE, bytes_accessed=moved // SCALE, transcendentals=0)


def parts(values):
    high = values.astype(jnp.bfloat16)
    low = (values - high.astype(jnp.float32)).astype(jnp.bfloat16)
    return high, low


def times(weights3, values):
    high, low = parts(values)
    return jnp.dot(
        weights3, jnp.concatenate([high, low, high], axis=0), preferred_element_type=jnp.float32
    )


def normalized(values):
    center = values - jnp.mean(values, axis=0, keepdims=True)
    spread = jnp.mean(center * center, axis=0, keepdims=True)
    return center * lax.rsqrt(spread + 1e-05)


def hands_kernel(pair_ref, weights_ref, out_ref):
    rows, _, width = pair_ref.shape
    per = 4
    flat = out_ref.reshape(width * rows, LANES)
    for start in range(0, rows, per):
        values = jnp.concatenate([pair_ref[start + n].T for n in range(per)], axis=1)
        projected = times(weights_ref[...], normalized(values))
        result = jax.nn.sigmoid(projected[width:]) * projected[:width]
        for n in range(per):
            flat[pl.ds(start + n, width, stride=rows), :] = result[:, n * LANES : (n + 1) * LANES]


def hands(pair, weights3, left, right):
    _, tile_cols, width = pair.shape
    rows = left[1] + right[1]
    turn = left[1] // GROUP
    lead, shift = left[0] // GROUP, right[0] // GROUP - turn
    return pl.pallas_call(
        hands_kernel,
        grid=(rows // GROUP,),
        in_specs=[
            pl.BlockSpec((GROUP, tile_cols, width), lambda g: (g + jnp.where(g < turn, lead, shift), 0, 0)),
            pl.BlockSpec((2 * width, 3 * width), lambda g: (jnp.where(g < turn, 0, 1), 0)),
        ],
        out_specs=pl.BlockSpec((width, GROUP, tile_cols), lambda g: (0, g, 0)),
        out_shape=jax.ShapeDtypeStruct((width, rows, tile_cols), jnp.float32),
        compiler_params=pltpu.CompilerParams(vmem_limit_bytes=VMEM),
        cost_estimate=estimate(6 * rows * tile_cols * width * 2 * width, 8 * rows * tile_cols * width),
        name="hands",
    )(pair, weights3)


def product_kernel(half_ref, low_ref, high_ref, own_ref, other_ref, *refs):
    out_ref = refs[-1]
    cols = own_ref.shape[0] // 2
    half = half_ref[0]

    def line(ref, lo):
        return jnp.concatenate([ref[lo * cols + c, 0] for c in range(cols)], axis=1)

    left_high, left_low = parts(
        jnp.concatenate([line(ref, lo) for lo in range(2) for ref in (low_ref, high_ref)], axis=0)
    )
    right_high, right_low = parts(
        jnp.concatenate([line(ref, lo) for ref in (own_ref, other_ref) for lo in range(2)], axis=0)
    )
    result = lax.dot_general(
        jnp.concatenate([right_high, right_high, right_low], axis=1),
        jnp.concatenate([left_high, left_low, left_high], axis=1),
        (((1,), (1,)), ((), ())),
        preferred_element_type=jnp.float32,
    )
    rows = own_ref.shape[2]
    wide = result.shape[1] // 2
    for lo in range(2):
        for piece in range(cols):
            source, other_lo = divmod(piece, 2)
            plane = 2 * jnp.where(half == source, 0, 1) + other_lo
            out_ref[lo * cols + plane, 0] = result[
                piece * rows : (piece + 1) * rows, lo * wide : (lo + 1) * wide
            ]


def product(half, low, high, own, other, wide, blocks=1, into=None):
    sources, owned, rows, width = own.shape
    k_all = width * sources // 2
    spec = lambda height: pl.BlockSpec((sources, 1, height, width), lambda n, half: (0, n, 0, 0))
    place = 0 if into is None else blocks - 1
    kept = [] if into is None else [into]
    return pl.pallas_call(
        product_kernel,
        grid_spec=pltpu.PrefetchScalarGridSpec(
            num_scalar_prefetch=1,
            grid=(owned,),
            in_specs=[spec(LOWER), spec(wide - LOWER), spec(rows), spec(rows)]
            + [pl.BlockSpec(memory_space=pl.ANY)] * len(kept),
            out_specs=pl.BlockSpec((sources, 1, rows, wide), lambda n, half: (0, n, place, 0)),
        ),
        out_shape=jax.ShapeDtypeStruct((sources, owned, blocks * rows, wide), jnp.float32),
        input_output_aliases={5: 0} if kept else {},
        compiler_params=pltpu.CompilerParams(vmem_limit_bytes=VMEM),
        cost_estimate=estimate(
            6 * owned * 4 * rows * 2 * wide * k_all, 4 * owned * k_all * (2 * wide + 4 * rows)
        ),
        name="product",
    )(half, low, high, own, other, *kept)


def head_kernel(
    pair_ref, product_ref, gate_ref, output_ref, up_ref, down_ref, bins_ref, *out_refs
):
    tile_rows, cols, width = pair_ref.shape
    bins = out_refs[0].shape[1]
    per = 4
    flat_pair = pair_ref.reshape(tile_rows * cols, width)
    flat_product = product_ref.reshape(width * cols, tile_rows)
    hidden_width = up_ref.shape[0] // 2
    for start in range(0, cols, per):
        values = jnp.concatenate(
            [flat_pair[pl.ds(start + n, tile_rows, stride=cols), :].T for n in range(per)], axis=1
        )
        product_values = jnp.concatenate(
            [flat_product[pl.ds(start + n, width, stride=cols), :] for n in range(per)], axis=1
        )
        gate = jax.nn.sigmoid(times(gate_ref[...], normalized(values)))
        updated = values + gate * times(output_ref[...], normalized(product_values))
        hidden = times(up_ref[...], normalized(updated))
        activated = jax.nn.silu(hidden[:hidden_width]) * hidden[hidden_width:]
        pair_out = updated + times(down_ref[...], activated)
        logits = times(bins_ref[...], pair_out)
        for n in range(per):
            for part, out_ref in enumerate(out_refs):
                out_ref[start + n] = logits[
                    part * bins : (part + 1) * bins, n * tile_rows : (n + 1) * tile_rows
                ]


def head(pair, product_values, first, count, gate3, output3, up3, down3, bins3):
    tile_rows, tile_cols, width = pair.shape
    chunk_cols = product_values.shape[1]
    steps = chunk_cols // GROUP
    lead = first // GROUP
    bins = bins3.shape[0] // count
    whole = lambda array: pl.BlockSpec(array.shape, lambda g: (0, 0))
    macs = gate3.size + output3.size + up3.size + down3.size + bins3.size
    return pl.pallas_call(
        head_kernel,
        grid=(steps,),
        in_specs=[
            pl.BlockSpec((tile_rows, GROUP, width), lambda g: (0, lead + g, 0)),
            pl.BlockSpec((width, GROUP, tile_rows), lambda g: (0, g, 0)),
            whole(gate3),
            whole(output3),
            whole(up3),
            whole(down3),
            whole(bins3),
        ],
        out_specs=[pl.BlockSpec((GROUP, bins, tile_rows), lambda g: (g, 0, 0))] * count,
        out_shape=[jax.ShapeDtypeStruct((chunk_cols, bins, tile_rows), jnp.float32)] * count,
        compiler_params=pltpu.CompilerParams(vmem_limit_bytes=VMEM),
        cost_estimate=estimate(
            2 * chunk_cols * tile_rows * macs, 4 * chunk_cols * tile_rows * (2 * width + count * bins)
        ),
        name="head",
    )(pair, product_values, gate3, output3, up3, down3, bins3)


def symmetric_kernel(bias_ref, *refs):
    out_ref, blocks = refs[-1], refs[:-1]
    tile_rows, quarters, bins, tile_cols = out_ref.shape
    count = len(blocks) // (2 * quarters)
    flat = out_ref.reshape(tile_rows * quarters * bins, tile_cols)
    for quarter in range(quarters):
        for n in range(bins):

            def joined(start):
                chosen = blocks[(start + quarter) * count : (start + quarter + 1) * count]
                values = [
                    ref.reshape(ref.shape[0] * bins, ref.shape[2])[
                        pl.ds(n, ref.shape[0], stride=bins), :
                    ]
                    for ref in chosen
                ]
                return jnp.concatenate(values, axis=0)

            result = joined(0).T + joined(quarters) + bias_ref[quarter, n : n + 1, :]
            flat[pl.ds(quarter * bins + n, tile_rows, stride=quarters * bins), :] = result


def symmetric(bias, own, mirror):
    quarters, bins, tile_cols = bias.shape
    tile_rows = own[0][0].shape[2]
    arrays, specs = [], []
    for quarter in range(quarters):
        for block in own:
            part, rest = divmod(quarter * bins, block[0].shape[1])
            arrays.append((part, rest // GROUP, block[0].shape))
    chosen = [own[n % len(own)][part] for n, (part, _, _) in enumerate(arrays)]
    chosen += [mirror[n % len(own)][part] for n, (part, _, _) in enumerate(arrays)]
    specs = [
        pl.BlockSpec((shape[0], GROUP, shape[2]), lambda g, lead=lead: (0, lead + g, 0))
        for _, lead, shape in arrays
    ] * 2
    return pl.pallas_call(
        symmetric_kernel,
        grid=(bins // GROUP,),
        in_specs=[pl.BlockSpec((quarters, GROUP, tile_cols), lambda g: (0, g, 0))] + specs,
        out_specs=pl.BlockSpec((tile_rows, quarters, GROUP, tile_cols), lambda g: (0, 0, g, 0)),
        out_shape=jax.ShapeDtypeStruct((tile_rows, quarters, bins, tile_cols), jnp.float32),
        compiler_params=pltpu.CompilerParams(vmem_limit_bytes=VMEM),
        cost_estimate=estimate(0, 12 * tile_rows * quarters * bins * tile_cols),
        name="symmetric",
    )(bias, *chosen)


def move(values, count, target):
    every = [(r, c) for r in range(count) for c in range(count)]
    pairs = [(r * count + c, target(r, c)) for r, c in every]
    return lax.ppermute(values, ("half", "lo", "col"), pairs)


def turn_of(block, part):
    return part if len(block) == 4 else 2 * part


def aside(block, count):
    return [block[0]] + [
        move(block[n], count, lambda r, c: r * count + (c ^ turn_of(block, n)))
        for n in range(1, len(block))
    ]


def across(block, count, part):
    return move(block[part], count, lambda r, c: (c ^ turn_of(block, part)) * count + r)


def half_shards(
    pair,
    gain_input,
    weights_in,
    gate_weights,
    weights_out,
    gain_product,
    gain_transition,
    transition_in,
    transition_out,
    distogram_weights,
    distogram_bias,
):
    row_count = 2 * lax.axis_size("lo")
    col_count = lax.axis_size("col")
    _, tile_rows, tile_cols, width = pair.shape
    tile = pair[0]
    in3 = split_weights(weights_in, gain_input)
    gate3 = split_weights(gate_weights, gain_input)
    output3 = split_weights(weights_out, gain_product)
    up3 = split_weights(transition_in, gain_transition)
    down3 = split_weights(transition_out)
    bins3 = split_weights(distogram_weights)
    sources = 2 * col_count
    owned = width // sources

    def spread(values):
        values = values.reshape(sources, owned, *values.shape[1:])
        return lax.all_to_all(values, ("lo", "col"), split_axis=0, concat_axis=0, tiled=True)

    tie = lax.optimization_barrier
    half = lax.axis_index("half").astype(jnp.int32).reshape(1)
    firsts = [sum(CHUNKS[:n]) for n in range(len(CHUNKS))]
    upper = tile_rows - LOWER

    def exchange(values):
        return lax.ppermute(values, "half", [(0, 1), (1, 0)])

    def blocks(chunk, count=1, into=None):
        return product(half, low, high, rights[chunk], others[chunk], tile_rows, count, into)

    def delivered(values):
        values = lax.all_to_all(values, ("lo", "col"), split_axis=0, concat_axis=0, tiled=True)
        return values.reshape(width, values.shape[2], tile_rows)

    def run_head(values, first, count):
        return head(tile, values, first, count, gate3, output3, up3, down3, bins3)

    def mirrored_parts(block):
        shifted = aside(block, row_count)
        return [across(shifted, row_count, part) for part in range(len(block))]

    right = spread(hands(tile, in3, (0, 0), (firsts[0], CHUNKS[0])))
    rights, others = [right], [exchange(right)]
    low = spread(hands(tile, in3, (0, LOWER), (firsts[1], CHUNKS[1])))
    rights.append(low[:, :, LOWER:])
    sent = hands(tile, in3, (LOWER, upper), (firsts[2], CHUNKS[2]))
    sent, others[0], rights[1] = tie((sent, others[0], rights[1]))
    others.append(exchange(rights[1]))
    high = spread(sent)
    rights.append(high[:, :, upper:])
    values, rights[2] = tie((blocks(1, 2, blocks(0, 2)), rights[2]))
    others.append(exchange(rights[2]))
    own = [run_head(delivered(values), 0, PARTS[0])]
    values, own[0] = tie((delivered(blocks(2)), own[0]))
    own.append(run_head(values, firsts[2], PARTS[1]))
    mirror = [mirrored_parts(block) for block in own]
    quarters = 4
    bins = distogram_bias.shape[0] // quarters
    bias = jnp.broadcast_to(distogram_bias.reshape(quarters, bins, 1), (quarters, bins, tile_cols))
    logits = symmetric(bias, own, mirror).reshape(tile_rows, quarters * bins, tile_cols)
    return jnp.swapaxes(logits, 1, 2)[None]


def solution(mesh):
    names = mesh.axis_names
    crops, rows, cols = (mesh.shape[name] for name in names)

    def run(pair, *parameters):
        crop_count, height, across, width = pair.shape
        tile_rows, tile_cols = height // rows, across // cols
        by_halves = (
            crop_count == crops
            and rows == cols == 4
            and tile_rows == tile_cols == LANES
            and width == LANES
        )
        if by_halves:
            halves = Mesh(mesh.devices.reshape(crops, 2, rows // 2, cols), ("crop", "half", "lo", "col"))
            spec, used, body = P("crop", ("half", "lo"), "col", None), halves, half_shards
        else:
            spec, used, body = P("crop", "row", "col", None), mesh, general_shards
        return jax.shard_map(
            body,
            mesh=used,
            in_specs=(spec,) + (P(),) * len(parameters),
            out_specs=spec,
            check_vma=False,
        )(pair, *parameters)

    return run
```

```python
import functools

import jax
import jax.numpy as jnp
from jax import lax
from jax.experimental import pallas as pl
from jax.experimental.pallas import tpu as pltpu
from jax.sharding import Mesh, PartitionSpec as P

HIGH = lax.Precision.HIGHEST
LANES = 128
GROUP = 8
CHUNKS = (40, 56, 32)
LOWER = 40
PARTS = (4, 4, 2)
VMEM = 56 * 1024 * 1024
SCALE = 8


def layer_norm(values, gain):
    center = values - jnp.mean(values, axis=-1, keepdims=True)
    spread = jnp.mean(center * center, axis=-1, keepdims=True)
    return center * lax.rsqrt(spread + 1e-05) * gain


def project(values, weights):
    return jnp.einsum("...c,cd->...d", values, weights, precision=HIGH)


def outgoing(left_hand, right_hand):
    return jnp.einsum("bikc,bjkc->bijc", left_hand, right_hand, precision=HIGH)


def mirrored(values):
    columns = lax.all_to_all(values, ("row", "col"), split_axis=2, concat_axis=1, tiled=True)
    return jnp.swapaxes(columns, 1, 2)


def general_shards(
    pair,
    gain_input,
    weights_in,
    gate_weights,
    weights_out,
    gain_product,
    gain_transition,
    transition_in,
    transition_out,
    distogram_weights,
    distogram_bias,
):
    row_count = lax.axis_size("row")
    col_count = lax.axis_size("col")
    crops, tile_rows, tile_cols, width = pair.shape
    normed = layer_norm(pair, gain_input)
    projected = project(normed, weights_in)
    left_hand = jax.nn.sigmoid(projected[..., width : 2 * width]) * projected[..., :width]
    right_hand = jax.nn.sigmoid(projected[..., 3 * width :]) * projected[..., 2 * width : 3 * width]
    stacked = jnp.stack([left_hand, right_hand], axis=0)
    received = lax.all_to_all(stacked, ("row", "col"), split_axis=4, concat_axis=2, tiled=True)
    items = received.shape[1]
    owned = received.shape[4]
    square = received.reshape(2, items, row_count, col_count, tile_rows, tile_cols, owned)
    square = square.transpose(0, 1, 2, 4, 3, 5, 6).reshape(
        2, items, row_count * tile_rows, col_count * tile_cols, owned
    )
    result = outgoing(square[0], square[1])
    product = lax.all_to_all(result, ("row", "col"), split_axis=1, concat_axis=3, tiled=True)
    base = lax.all_to_all(pair, "col", split_axis=1, concat_axis=2, tiled=True)
    normed_base = layer_norm(base, gain_input)
    gate = jax.nn.sigmoid(project(normed_base, gate_weights))
    updated = base + gate * project(layer_norm(product, gain_product), weights_out)
    hidden = project(layer_norm(updated, gain_transition), transition_in)
    hidden_width = transition_out.shape[0]
    activated = jax.nn.silu(hidden[..., :hidden_width]) * hidden[..., hidden_width:]
    pair_out = updated + project(activated, transition_out)
    symmetric = pair_out + mirrored(pair_out)
    line_logits = project(symmetric, distogram_weights) + distogram_bias
    return lax.all_to_all(line_logits, "col", split_axis=2, concat_axis=1, tiled=True)


def split_weights(weights, gain=None):
    if gain is not None:
        weights = gain[:, None] * weights
    flipped = weights.T
    high = lax.reduce_precision(flipped, 8, 7)
    low = flipped - high
    return jnp.concatenate([high, high, low], axis=1).astype(jnp.bfloat16)


def estimate(flops, moved):
    return pl.CostEstimate(flops=flops // SCALE, bytes_accessed=moved // SCALE, transcendentals=0)


def parts(values):
    high = values.astype(jnp.bfloat16)
    low = (values - high.astype(jnp.float32)).astype(jnp.bfloat16)
    return high, low


def times(weights3, values):
    high, low = parts(values)
    return jnp.dot(
        weights3, jnp.concatenate([high, low, high], axis=0), preferred_element_type=jnp.float32
    )


def normalized(values):
    center = values - jnp.mean(values, axis=0, keepdims=True)
    spread = jnp.mean(center * center, axis=0, keepdims=True)
    return center * lax.rsqrt(spread + 1e-05)


def hands_kernel(pair_ref, weights_ref, out_ref):
    rows, _, width = pair_ref.shape
    per = 4
    flat = out_ref.reshape(width * rows, LANES)
    for start in range(0, rows, per):
        values = jnp.concatenate([pair_ref[start + n].T for n in range(per)], axis=1)
        projected = times(weights_ref[...], normalized(values))
        result = jax.nn.sigmoid(projected[width:]) * projected[:width]
        for n in range(per):
            flat[pl.ds(start + n, width, stride=rows), :] = result[:, n * LANES : (n + 1) * LANES]


def hands(pair, weights3, left, right):
    _, tile_cols, width = pair.shape
    rows = left[1] + right[1]
    turn = left[1] // GROUP
    lead, shift = left[0] // GROUP, right[0] // GROUP - turn
    return pl.pallas_call(
        hands_kernel,
        grid=(rows // GROUP,),
        in_specs=[
            pl.BlockSpec((GROUP, tile_cols, width), lambda g: (g + jnp.where(g < turn, lead, shift), 0, 0)),
            pl.BlockSpec((2 * width, 3 * width), lambda g: (jnp.where(g < turn, 0, 1), 0)),
        ],
        out_specs=pl.BlockSpec((width, GROUP, tile_cols), lambda g: (0, g, 0)),
        out_shape=jax.ShapeDtypeStruct((width, rows, tile_cols), jnp.float32),
        compiler_params=pltpu.CompilerParams(vmem_limit_bytes=VMEM),
        cost_estimate=estimate(6 * rows * tile_cols * width * 2 * width, 8 * rows * tile_cols * width),
        name="hands",
    )(pair, weights3)


def product_kernel(half_ref, low_ref, high_ref, own_ref, other_ref, out_ref):
    cols = own_ref.shape[0] // 2
    half = half_ref[0]

    def line(ref, lo):
        return jnp.concatenate([ref[lo * cols + c, 0] for c in range(cols)], axis=1)

    left_high, left_low = parts(
        jnp.concatenate([line(ref, lo) for lo in range(2) for ref in (low_ref, high_ref)], axis=0)
    )
    right_high, right_low = parts(
        jnp.concatenate([line(ref, lo) for ref in (own_ref, other_ref) for lo in range(2)], axis=0)
    )
    result = lax.dot_general(
        jnp.concatenate([right_high, right_high, right_low], axis=1),
        jnp.concatenate([left_high, left_low, left_high], axis=1),
        (((1,), (1,)), ((), ())),
        preferred_element_type=jnp.float32,
    )
    rows = own_ref.shape[2]
    wide = result.shape[1] // 2
    for lo in range(2):
        for piece in range(cols):
            source, other_lo = divmod(piece, 2)
            plane = 2 * jnp.where(half == source, 0, 1) + other_lo
            out_ref[lo * cols + plane, 0] = result[
                piece * rows : (piece + 1) * rows, lo * wide : (lo + 1) * wide
            ]


def product(half, low, high, own, other, wide):
    sources, owned, rows, width = own.shape
    k_all = width * sources // 2
    spec = lambda height: pl.BlockSpec((sources, 1, height, width), lambda n, half: (0, n, 0, 0))
    return pl.pallas_call(
        product_kernel,
        grid_spec=pltpu.PrefetchScalarGridSpec(
            num_scalar_prefetch=1,
            grid=(owned,),
            in_specs=[spec(LOWER), spec(wide - LOWER), spec(rows), spec(rows)],
            out_specs=pl.BlockSpec((sources, 1, rows, wide), lambda n, half: (0, n, 0, 0)),
        ),
        out_shape=jax.ShapeDtypeStruct((sources, owned, rows, wide), jnp.float32),
        compiler_params=pltpu.CompilerParams(vmem_limit_bytes=VMEM),
        cost_estimate=estimate(
            6 * owned * 4 * rows * 2 * wide * k_all, 4 * owned * k_all * (2 * wide + 4 * rows)
        ),
        name="product",
    )(half, low, high, own, other)


def head_kernel(
    pair_ref, product_ref, gate_ref, output_ref, up_ref, down_ref, bins_ref, *out_refs
):
    tile_rows, cols, width = pair_ref.shape
    bins = out_refs[0].shape[1]
    per = 4
    flat_pair = pair_ref.reshape(tile_rows * cols, width)
    flat_product = product_ref.reshape(width * cols, tile_rows)
    hidden_width = up_ref.shape[0] // 2
    for start in range(0, cols, per):
        values = jnp.concatenate(
            [flat_pair[pl.ds(start + n, tile_rows, stride=cols), :].T for n in range(per)], axis=1
        )
        product_values = jnp.concatenate(
            [flat_product[pl.ds(start + n, width, stride=cols), :] for n in range(per)], axis=1
        )
        gate = jax.nn.sigmoid(times(gate_ref[...], normalized(values)))
        updated = values + gate * times(output_ref[...], normalized(product_values))
        hidden = times(up_ref[...], normalized(updated))
        activated = jax.nn.silu(hidden[:hidden_width]) * hidden[hidden_width:]
        pair_out = updated + times(down_ref[...], activated)
        logits = times(bins_ref[...], pair_out)
        for n in range(per):
            for part, out_ref in enumerate(out_refs):
                out_ref[start + n] = logits[
                    part * bins : (part + 1) * bins, n * tile_rows : (n + 1) * tile_rows
                ]


def head(pair, product_values, first, count, gate3, output3, up3, down3, bins3):
    tile_rows, tile_cols, width = pair.shape
    chunk_cols = product_values.shape[1]
    steps = chunk_cols // GROUP
    lead = first // GROUP
    bins = bins3.shape[0] // count
    whole = lambda array: pl.BlockSpec(array.shape, lambda g: (0, 0))
    macs = gate3.size + output3.size + up3.size + down3.size + bins3.size
    return pl.pallas_call(
        head_kernel,
        grid=(steps,),
        in_specs=[
            pl.BlockSpec((tile_rows, GROUP, width), lambda g: (0, lead + g, 0)),
            pl.BlockSpec((width, GROUP, tile_rows), lambda g: (0, g, 0)),
            whole(gate3),
            whole(output3),
            whole(up3),
            whole(down3),
            whole(bins3),
        ],
        out_specs=[pl.BlockSpec((GROUP, bins, tile_rows), lambda g: (g, 0, 0))] * count,
        out_shape=[jax.ShapeDtypeStruct((chunk_cols, bins, tile_rows), jnp.float32)] * count,
        compiler_params=pltpu.CompilerParams(vmem_limit_bytes=VMEM),
        cost_estimate=estimate(
            2 * chunk_cols * tile_rows * macs, 4 * chunk_cols * tile_rows * (2 * width + count * bins)
        ),
        name="head",
    )(pair, product_values, gate3, output3, up3, down3, bins3)


def symmetric_kernel(bias_ref, *refs):
    out_ref, blocks = refs[-1], refs[:-1]
    tile_rows, quarters, bins, tile_cols = out_ref.shape
    count = len(blocks) // (2 * quarters)
    flat = out_ref.reshape(tile_rows * quarters * bins, tile_cols)
    for quarter in range(quarters):
        for n in range(bins):

            def joined(start):
                chosen = blocks[(start + quarter) * count : (start + quarter + 1) * count]
                values = [
                    ref.reshape(ref.shape[0] * bins, ref.shape[2])[
                        pl.ds(n, ref.shape[0], stride=bins), :
                    ]
                    for ref in chosen
                ]
                return jnp.concatenate(values, axis=0)

            result = joined(0).T + joined(quarters) + bias_ref[quarter, n : n + 1, :]
            flat[pl.ds(quarter * bins + n, tile_rows, stride=quarters * bins), :] = result


def symmetric(bias, own, mirror):
    quarters, bins, tile_cols = bias.shape
    tile_rows = own[0][0].shape[2]
    arrays, specs = [], []
    for quarter in range(quarters):
        for block in own:
            part, rest = divmod(quarter * bins, block[0].shape[1])
            arrays.append((part, rest // GROUP, block[0].shape))
    chosen = [own[n % len(own)][part] for n, (part, _, _) in enumerate(arrays)]
    chosen += [mirror[n % len(own)][part] for n, (part, _, _) in enumerate(arrays)]
    specs = [
        pl.BlockSpec((shape[0], GROUP, shape[2]), lambda g, lead=lead: (0, lead + g, 0))
        for _, lead, shape in arrays
    ] * 2
    return pl.pallas_call(
        symmetric_kernel,
        grid=(bins // GROUP,),
        in_specs=[pl.BlockSpec((quarters, GROUP, tile_cols), lambda g: (0, g, 0))] + specs,
        out_specs=pl.BlockSpec((tile_rows, quarters, GROUP, tile_cols), lambda g: (0, 0, g, 0)),
        out_shape=jax.ShapeDtypeStruct((tile_rows, quarters, bins, tile_cols), jnp.float32),
        compiler_params=pltpu.CompilerParams(vmem_limit_bytes=VMEM),
        cost_estimate=estimate(0, 12 * tile_rows * quarters * bins * tile_cols),
        name="symmetric",
    )(bias, *chosen)


def move(values, count, target):
    every = [(r, c) for r in range(count) for c in range(count)]
    pairs = [(r * count + c, target(r, c)) for r, c in every]
    return lax.ppermute(values, ("half", "lo", "col"), pairs)


def turn_of(block, part):
    return part if len(block) == 4 else 2 * part


def aside(block, count):
    return [block[0]] + [
        move(block[n], count, lambda r, c: r * count + (c ^ turn_of(block, n)))
        for n in range(1, len(block))
    ]


def across(block, count, part):
    return move(block[part], count, lambda r, c: (c ^ turn_of(block, part)) * count + r)


def half_shards(
    pair,
    gain_input,
    weights_in,
    gate_weights,
    weights_out,
    gain_product,
    gain_transition,
    transition_in,
    transition_out,
    distogram_weights,
    distogram_bias,
):
    row_count = 2 * lax.axis_size("lo")
    col_count = lax.axis_size("col")
    _, tile_rows, tile_cols, width = pair.shape
    tile = pair[0]
    in3 = split_weights(weights_in, gain_input)
    gate3 = split_weights(gate_weights, gain_input)
    output3 = split_weights(weights_out, gain_product)
    up3 = split_weights(transition_in, gain_transition)
    down3 = split_weights(transition_out)
    bins3 = split_weights(distogram_weights)
    sources = 2 * col_count
    owned = width // sources

    def spread(values):
        values = values.reshape(sources, owned, *values.shape[1:])
        return lax.all_to_all(values, ("lo", "col"), split_axis=0, concat_axis=0, tiled=True)

    tie = lax.optimization_barrier
    half = lax.axis_index("half").astype(jnp.int32).reshape(1)
    firsts = [sum(CHUNKS[:n]) for n in range(len(CHUNKS))]
    upper = tile_rows - LOWER

    def exchange(values):
        return lax.ppermute(values, "half", [(0, 1), (1, 0)])

    def blocks(chunk):
        return product(half, low, high, rights[chunk], others[chunk], tile_rows)

    def delivered(values):
        values = lax.all_to_all(values, ("lo", "col"), split_axis=0, concat_axis=0, tiled=True)
        return values.reshape(width, values.shape[2], tile_rows)

    def run_head(values, chunk):
        return head(
            tile, values, firsts[chunk], PARTS[chunk], gate3, output3, up3, down3, bins3
        )

    def mirrored_parts(block):
        shifted = aside(block, row_count)
        return [across(shifted, row_count, part) for part in range(len(block))]

    right = spread(hands(tile, in3, (0, 0), (firsts[0], CHUNKS[0])))
    rights, others = [right], [exchange(right)]
    low = spread(hands(tile, in3, (0, LOWER), (firsts[1], CHUNKS[1])))
    rights.append(low[:, :, LOWER:])
    sent = hands(tile, in3, (LOWER, upper), (firsts[2], CHUNKS[2]))
    sent, others[0], rights[1] = tie((sent, others[0], rights[1]))
    others.append(exchange(rights[1]))
    high = spread(sent)
    rights.append(high[:, :, upper:])
    values, others[1], rights[2] = tie((blocks(0), others[1], rights[2]))
    others.append(exchange(rights[2]))
    values, after = tie((delivered(values), blocks(1)))
    own = [run_head(values, 0)]
    mirror = [mirrored_parts(own[0])]
    after, others[2], mirror[0] = tie((after, others[2], mirror[0]))
    own.append(run_head(delivered(after), 1))
    own.append(run_head(delivered(blocks(2)), 2))
    mirror += [mirrored_parts(block) for block in own[1:]]
    quarters = 4
    bins = distogram_bias.shape[0] // quarters
    bias = jnp.broadcast_to(distogram_bias.reshape(quarters, bins, 1), (quarters, bins, tile_cols))
    logits = symmetric(bias, own, mirror).reshape(tile_rows, quarters * bins, tile_cols)
    return jnp.swapaxes(logits, 1, 2)[None]


def solution(mesh):
    names = mesh.axis_names
    crops, rows, cols = (mesh.shape[name] for name in names)

    def run(pair, *parameters):
        crop_count, height, across, width = pair.shape
        tile_rows, tile_cols = height // rows, across // cols
        by_halves = (
            crop_count == crops
            and rows == cols == 4
            and tile_rows == tile_cols == LANES
            and width == LANES
        )
        if by_halves:
            halves = Mesh(mesh.devices.reshape(crops, 2, rows // 2, cols), ("crop", "half", "lo", "col"))
            spec, used, body = P("crop", ("half", "lo"), "col", None), halves, half_shards
        else:
            spec, used, body = P("crop", "row", "col", None), mesh, general_shards
        return jax.shard_map(
            body,
            mesh=used,
            in_specs=(spec,) + (P(),) * len(parameters),
            out_specs=spec,
            check_vma=False,
        )(pair, *parameters)

    return run
```

```python
import functools

import jax
import jax.numpy as jnp
from jax import lax
from jax.experimental import pallas as pl
from jax.experimental.pallas import tpu as pltpu
from jax.sharding import Mesh, PartitionSpec as P

HIGH = lax.Precision.HIGHEST
LANES = 128
GROUP = 8
CHUNKS = (40, 56, 32)
LOWER = 40
PARTS = (4, 4, 2)
VMEM = 56 * 1024 * 1024
SCALE = 8


def layer_norm(values, gain):
    center = values - jnp.mean(values, axis=-1, keepdims=True)
    spread = jnp.mean(center * center, axis=-1, keepdims=True)
    return center * lax.rsqrt(spread + 1e-05) * gain


def project(values, weights):
    return jnp.einsum("...c,cd->...d", values, weights, precision=HIGH)


def outgoing(left_hand, right_hand):
    return jnp.einsum("bikc,bjkc->bijc", left_hand, right_hand, precision=HIGH)


def mirrored(values):
    columns = lax.all_to_all(values, ("row", "col"), split_axis=2, concat_axis=1, tiled=True)
    return jnp.swapaxes(columns, 1, 2)


def general_shards(
    pair,
    gain_input,
    weights_in,
    gate_weights,
    weights_out,
    gain_product,
    gain_transition,
    transition_in,
    transition_out,
    distogram_weights,
    distogram_bias,
):
    row_count = lax.axis_size("row")
    col_count = lax.axis_size("col")
    crops, tile_rows, tile_cols, width = pair.shape
    normed = layer_norm(pair, gain_input)
    projected = project(normed, weights_in)
    left_hand = jax.nn.sigmoid(projected[..., width : 2 * width]) * projected[..., :width]
    right_hand = jax.nn.sigmoid(projected[..., 3 * width :]) * projected[..., 2 * width : 3 * width]
    stacked = jnp.stack([left_hand, right_hand], axis=0)
    received = lax.all_to_all(stacked, ("row", "col"), split_axis=4, concat_axis=2, tiled=True)
    items = received.shape[1]
    owned = received.shape[4]
    square = received.reshape(2, items, row_count, col_count, tile_rows, tile_cols, owned)
    square = square.transpose(0, 1, 2, 4, 3, 5, 6).reshape(
        2, items, row_count * tile_rows, col_count * tile_cols, owned
    )
    result = outgoing(square[0], square[1])
    product = lax.all_to_all(result, ("row", "col"), split_axis=1, concat_axis=3, tiled=True)
    base = lax.all_to_all(pair, "col", split_axis=1, concat_axis=2, tiled=True)
    normed_base = layer_norm(base, gain_input)
    gate = jax.nn.sigmoid(project(normed_base, gate_weights))
    updated = base + gate * project(layer_norm(product, gain_product), weights_out)
    hidden = project(layer_norm(updated, gain_transition), transition_in)
    hidden_width = transition_out.shape[0]
    activated = jax.nn.silu(hidden[..., :hidden_width]) * hidden[..., hidden_width:]
    pair_out = updated + project(activated, transition_out)
    symmetric = pair_out + mirrored(pair_out)
    line_logits = project(symmetric, distogram_weights) + distogram_bias
    return lax.all_to_all(line_logits, "col", split_axis=2, concat_axis=1, tiled=True)


def split_weights(weights, gain=None):
    if gain is not None:
        weights = gain[:, None] * weights
    flipped = weights.T
    high = lax.reduce_precision(flipped, 8, 7)
    low = flipped - high
    return jnp.concatenate([high, high, low], axis=1).astype(jnp.bfloat16)


def estimate(flops, moved):
    return pl.CostEstimate(flops=flops // SCALE, bytes_accessed=moved // SCALE, transcendentals=0)


def parts(values):
    high = values.astype(jnp.bfloat16)
    low = (values - high.astype(jnp.float32)).astype(jnp.bfloat16)
    return high, low


def times(weights3, values):
    high, low = parts(values)
    return jnp.dot(
        weights3, jnp.concatenate([high, low, high], axis=0), preferred_element_type=jnp.float32
    )


def normalized(values):
    center = values - jnp.mean(values, axis=0, keepdims=True)
    spread = jnp.mean(center * center, axis=0, keepdims=True)
    return center * lax.rsqrt(spread + 1e-05)


def hands_kernel(pair_ref, weights_ref, out_ref):
    rows, _, width = pair_ref.shape
    per = 4
    flat = out_ref.reshape(width * rows, LANES)
    for start in range(0, rows, per):
        values = jnp.concatenate([pair_ref[start + n].T for n in range(per)], axis=1)
        projected = times(weights_ref[...], normalized(values))
        result = jax.nn.sigmoid(projected[width:]) * projected[:width]
        for n in range(per):
            flat[pl.ds(start + n, width, stride=rows), :] = result[:, n * LANES : (n + 1) * LANES]


def hands(pair, weights3, left, right):
    _, tile_cols, width = pair.shape
    rows = left[1] + right[1]
    turn = left[1] // GROUP
    lead, shift = left[0] // GROUP, right[0] // GROUP - turn
    return pl.pallas_call(
        hands_kernel,
        grid=(rows // GROUP,),
        in_specs=[
            pl.BlockSpec((GROUP, tile_cols, width), lambda g: (g + jnp.where(g < turn, lead, shift), 0, 0)),
            pl.BlockSpec((2 * width, 3 * width), lambda g: (jnp.where(g < turn, 0, 1), 0)),
        ],
        out_specs=pl.BlockSpec((width, GROUP, tile_cols), lambda g: (0, g, 0)),
        out_shape=jax.ShapeDtypeStruct((width, rows, tile_cols), jnp.float32),
        compiler_params=pltpu.CompilerParams(vmem_limit_bytes=VMEM),
        cost_estimate=estimate(6 * rows * tile_cols * width * 2 * width, 8 * rows * tile_cols * width),
        name="hands",
    )(pair, weights3)


def product_kernel(half_ref, low_ref, high_ref, own_ref, other_ref, out_ref):
    cols = own_ref.shape[0] // 2
    half = half_ref[0]

    def line(ref, lo):
        return jnp.concatenate([ref[lo * cols + c, 0] for c in range(cols)], axis=1)

    left_high, left_low = parts(
        jnp.concatenate([line(ref, lo) for lo in range(2) for ref in (low_ref, high_ref)], axis=0)
    )
    right_high, right_low = parts(
        jnp.concatenate([line(ref, lo) for ref in (own_ref, other_ref) for lo in range(2)], axis=0)
    )
    result = lax.dot_general(
        jnp.concatenate([right_high, right_high, right_low], axis=1),
        jnp.concatenate([left_high, left_low, left_high], axis=1),
        (((1,), (1,)), ((), ())),
        preferred_element_type=jnp.float32,
    )
    rows = own_ref.shape[2]
    wide = result.shape[1] // 2
    for lo in range(2):
        for piece in range(cols):
            source, other_lo = divmod(piece, 2)
            plane = 2 * jnp.where(half == source, 0, 1) + other_lo
            out_ref[lo * cols + plane, 0] = result[
                piece * rows : (piece + 1) * rows, lo * wide : (lo + 1) * wide
            ]


def product(half, low, high, own, other, wide):
    sources, owned, rows, width = own.shape
    k_all = width * sources // 2
    spec = lambda height: pl.BlockSpec((sources, 1, height, width), lambda n, half: (0, n, 0, 0))
    return pl.pallas_call(
        product_kernel,
        grid_spec=pltpu.PrefetchScalarGridSpec(
            num_scalar_prefetch=1,
            grid=(owned,),
            in_specs=[spec(LOWER), spec(wide - LOWER), spec(rows), spec(rows)],
            out_specs=pl.BlockSpec((sources, 1, rows, wide), lambda n, half: (0, n, 0, 0)),
        ),
        out_shape=jax.ShapeDtypeStruct((sources, owned, rows, wide), jnp.float32),
        compiler_params=pltpu.CompilerParams(vmem_limit_bytes=VMEM),
        cost_estimate=estimate(
            6 * owned * 4 * rows * 2 * wide * k_all, 4 * owned * k_all * (2 * wide + 4 * rows)
        ),
        name="product",
    )(half, low, high, own, other)


def head_kernel(
    pair_ref, product_ref, gate_ref, output_ref, up_ref, down_ref, bins_ref, *out_refs
):
    tile_rows, cols, width = pair_ref.shape
    bins = out_refs[0].shape[1]
    per = 4
    flat_pair = pair_ref.reshape(tile_rows * cols, width)
    flat_product = product_ref.reshape(width * cols, tile_rows)
    hidden_width = up_ref.shape[0] // 2
    for start in range(0, cols, per):
        values = jnp.concatenate(
            [flat_pair[pl.ds(start + n, tile_rows, stride=cols), :].T for n in range(per)], axis=1
        )
        product_values = jnp.concatenate(
            [flat_product[pl.ds(start + n, width, stride=cols), :] for n in range(per)], axis=1
        )
        gate = jax.nn.sigmoid(times(gate_ref[...], normalized(values)))
        updated = values + gate * times(output_ref[...], normalized(product_values))
        hidden = times(up_ref[...], normalized(updated))
        activated = jax.nn.silu(hidden[:hidden_width]) * hidden[hidden_width:]
        pair_out = updated + times(down_ref[...], activated)
        logits = times(bins_ref[...], pair_out)
        for n in range(per):
            for part, out_ref in enumerate(out_refs):
                out_ref[start + n] = logits[
                    part * bins : (part + 1) * bins, n * tile_rows : (n + 1) * tile_rows
                ]


def head(pair, product_values, first, count, gate3, output3, up3, down3, bins3):
    tile_rows, tile_cols, width = pair.shape
    chunk_cols = product_values.shape[1]
    steps = chunk_cols // GROUP
    lead = first // GROUP
    bins = bins3.shape[0] // count
    whole = lambda array: pl.BlockSpec(array.shape, lambda g: (0, 0))
    macs = gate3.size + output3.size + up3.size + down3.size + bins3.size
    return pl.pallas_call(
        head_kernel,
        grid=(steps,),
        in_specs=[
            pl.BlockSpec((tile_rows, GROUP, width), lambda g: (0, lead + g, 0)),
            pl.BlockSpec((width, GROUP, tile_rows), lambda g: (0, g, 0)),
            whole(gate3),
            whole(output3),
            whole(up3),
            whole(down3),
            whole(bins3),
        ],
        out_specs=[pl.BlockSpec((GROUP, bins, tile_rows), lambda g: (g, 0, 0))] * count,
        out_shape=[jax.ShapeDtypeStruct((chunk_cols, bins, tile_rows), jnp.float32)] * count,
        compiler_params=pltpu.CompilerParams(vmem_limit_bytes=VMEM),
        cost_estimate=estimate(
            2 * chunk_cols * tile_rows * macs, 4 * chunk_cols * tile_rows * (2 * width + count * bins)
        ),
        name="head",
    )(pair, product_values, gate3, output3, up3, down3, bins3)


def symmetric_kernel(bias_ref, *refs):
    out_ref, blocks = refs[-1], refs[:-1]
    tile_rows, quarters, bins, tile_cols = out_ref.shape
    count = len(blocks) // (2 * quarters)
    flat = out_ref.reshape(tile_rows * quarters * bins, tile_cols)
    for quarter in range(quarters):
        for n in range(bins):

            def joined(start):
                chosen = blocks[(start + quarter) * count : (start + quarter + 1) * count]
                values = [
                    ref.reshape(ref.shape[0] * bins, ref.shape[2])[
                        pl.ds(n, ref.shape[0], stride=bins), :
                    ]
                    for ref in chosen
                ]
                return jnp.concatenate(values, axis=0)

            result = joined(0).T + joined(quarters) + bias_ref[quarter, n : n + 1, :]
            flat[pl.ds(quarter * bins + n, tile_rows, stride=quarters * bins), :] = result


def symmetric(bias, own, mirror):
    quarters, bins, tile_cols = bias.shape
    tile_rows = own[0][0].shape[2]
    arrays, specs = [], []
    for quarter in range(quarters):
        for block in own:
            part, rest = divmod(quarter * bins, block[0].shape[1])
            arrays.append((part, rest // GROUP, block[0].shape))
    chosen = [own[n % len(own)][part] for n, (part, _, _) in enumerate(arrays)]
    chosen += [mirror[n % len(own)][part] for n, (part, _, _) in enumerate(arrays)]
    specs = [
        pl.BlockSpec((shape[0], GROUP, shape[2]), lambda g, lead=lead: (0, lead + g, 0))
        for _, lead, shape in arrays
    ] * 2
    return pl.pallas_call(
        symmetric_kernel,
        grid=(bins // GROUP,),
        in_specs=[pl.BlockSpec((quarters, GROUP, tile_cols), lambda g: (0, g, 0))] + specs,
        out_specs=pl.BlockSpec((tile_rows, quarters, GROUP, tile_cols), lambda g: (0, 0, g, 0)),
        out_shape=jax.ShapeDtypeStruct((tile_rows, quarters, bins, tile_cols), jnp.float32),
        compiler_params=pltpu.CompilerParams(vmem_limit_bytes=VMEM),
        cost_estimate=estimate(0, 12 * tile_rows * quarters * bins * tile_cols),
        name="symmetric",
    )(bias, *chosen)


def move(values, count, target):
    every = [(r, c) for r in range(count) for c in range(count)]
    pairs = [(r * count + c, target(r, c)) for r, c in every]
    return lax.ppermute(values, ("half", "lo", "col"), pairs)


def turn_of(block, part):
    return part if len(block) == 4 else 2 * part


def aside(block, count):
    return [block[0]] + [
        move(block[n], count, lambda r, c: r * count + (c ^ turn_of(block, n)))
        for n in range(1, len(block))
    ]


def across(block, count, part):
    return move(block[part], count, lambda r, c: (c ^ turn_of(block, part)) * count + r)


def half_shards(
    pair,
    gain_input,
    weights_in,
    gate_weights,
    weights_out,
    gain_product,
    gain_transition,
    transition_in,
    transition_out,
    distogram_weights,
    distogram_bias,
):
    row_count = 2 * lax.axis_size("lo")
    col_count = lax.axis_size("col")
    _, tile_rows, tile_cols, width = pair.shape
    tile = pair[0]
    in3 = split_weights(weights_in, gain_input)
    gate3 = split_weights(gate_weights, gain_input)
    output3 = split_weights(weights_out, gain_product)
    up3 = split_weights(transition_in, gain_transition)
    down3 = split_weights(transition_out)
    bins3 = split_weights(distogram_weights)
    sources = 2 * col_count
    owned = width // sources

    def spread(values):
        values = values.reshape(sources, owned, *values.shape[1:])
        return lax.all_to_all(values, ("lo", "col"), split_axis=0, concat_axis=0, tiled=True)

    tie = lax.optimization_barrier
    half = lax.axis_index("half").astype(jnp.int32).reshape(1)
    firsts = [sum(CHUNKS[:n]) for n in range(len(CHUNKS))]
    upper = tile_rows - LOWER

    def exchange(values):
        return lax.ppermute(values, "half", [(0, 1), (1, 0)])

    def blocks(chunk):
        return product(half, low, high, rights[chunk], others[chunk], tile_rows)

    def delivered(values):
        values = lax.all_to_all(values, ("lo", "col"), split_axis=0, concat_axis=0, tiled=True)
        return values.reshape(width, values.shape[2], tile_rows)

    def run_head(values, chunk):
        return head(
            tile, values, firsts[chunk], PARTS[chunk], gate3, output3, up3, down3, bins3
        )

    def mirrored_parts(block):
        shifted = aside(block, row_count)
        return [across(shifted, row_count, part) for part in range(len(block))]

    right = spread(hands(tile, in3, (0, 0), (firsts[0], CHUNKS[0])))
    rights, others = [right], [exchange(right)]
    low = spread(hands(tile, in3, (0, LOWER), (firsts[1], CHUNKS[1])))
    rights.append(low[:, :, LOWER:])
    sent = hands(tile, in3, (LOWER, upper), (firsts[2], CHUNKS[2]))
    sent, others[0], rights[1] = tie((sent, others[0], rights[1]))
    others.append(exchange(rights[1]))
    high = spread(sent)
    rights.append(high[:, :, upper:])
    values, others[1], rights[2] = tie((blocks(0), others[1], rights[2]))
    others.append(exchange(rights[2]))
    values, after = tie((delivered(values), blocks(1)))
    own = [run_head(values, 0)]
    mirror = [mirrored_parts(own[0])]
    after, others[2], mirror[0] = tie((after, others[2], mirror[0]))
    values, after = tie((delivered(after), blocks(2)))
    own.append(run_head(values, 1))
    values, own[1] = tie((delivered(after), own[1]))
    own.append(run_head(values, 2))
    mirror += [mirrored_parts(block) for block in own[1:]]
    quarters = 4
    bins = distogram_bias.shape[0] // quarters
    bias = jnp.broadcast_to(distogram_bias.reshape(quarters, bins, 1), (quarters, bins, tile_cols))
    logits = symmetric(bias, own, mirror).reshape(tile_rows, quarters * bins, tile_cols)
    return jnp.swapaxes(logits, 1, 2)[None]


def solution(mesh):
    names = mesh.axis_names
    crops, rows, cols = (mesh.shape[name] for name in names)

    def run(pair, *parameters):
        crop_count, height, across, width = pair.shape
        tile_rows, tile_cols = height // rows, across // cols
        by_halves = (
            crop_count == crops
            and rows == cols == 4
            and tile_rows == tile_cols == LANES
            and width == LANES
        )
        if by_halves:
            halves = Mesh(mesh.devices.reshape(crops, 2, rows // 2, cols), ("crop", "half", "lo", "col"))
            spec, used, body = P("crop", ("half", "lo"), "col", None), halves, half_shards
        else:
            spec, used, body = P("crop", "row", "col", None), mesh, general_shards
        return jax.shard_map(
            body,
            mesh=used,
            in_specs=(spec,) + (P(),) * len(parameters),
            out_specs=spec,
            check_vma=False,
        )(pair, *parameters)

    return run
```

```python
import functools

import jax
import jax.numpy as jnp
from jax import lax
from jax.experimental import pallas as pl
from jax.experimental.pallas import tpu as pltpu
from jax.sharding import Mesh, PartitionSpec as P

HIGH = lax.Precision.HIGHEST
LANES = 128
GROUP = 8
CHUNKS = (40, 56, 32)
LOWER = 40
PARTS = (4, 4, 4)
VMEM = 56 * 1024 * 1024
SCALE = 8


def layer_norm(values, gain):
    center = values - jnp.mean(values, axis=-1, keepdims=True)
    spread = jnp.mean(center * center, axis=-1, keepdims=True)
    return center * lax.rsqrt(spread + 1e-05) * gain


def project(values, weights):
    return jnp.einsum("...c,cd->...d", values, weights, precision=HIGH)


def outgoing(left_hand, right_hand):
    return jnp.einsum("bikc,bjkc->bijc", left_hand, right_hand, precision=HIGH)


def mirrored(values):
    columns = lax.all_to_all(values, ("row", "col"), split_axis=2, concat_axis=1, tiled=True)
    return jnp.swapaxes(columns, 1, 2)


def general_shards(
    pair,
    gain_input,
    weights_in,
    gate_weights,
    weights_out,
    gain_product,
    gain_transition,
    transition_in,
    transition_out,
    distogram_weights,
    distogram_bias,
):
    row_count = lax.axis_size("row")
    col_count = lax.axis_size("col")
    crops, tile_rows, tile_cols, width = pair.shape
    normed = layer_norm(pair, gain_input)
    projected = project(normed, weights_in)
    left_hand = jax.nn.sigmoid(projected[..., width : 2 * width]) * projected[..., :width]
    right_hand = jax.nn.sigmoid(projected[..., 3 * width :]) * projected[..., 2 * width : 3 * width]
    stacked = jnp.stack([left_hand, right_hand], axis=0)
    received = lax.all_to_all(stacked, ("row", "col"), split_axis=4, concat_axis=2, tiled=True)
    items = received.shape[1]
    owned = received.shape[4]
    square = received.reshape(2, items, row_count, col_count, tile_rows, tile_cols, owned)
    square = square.transpose(0, 1, 2, 4, 3, 5, 6).reshape(
        2, items, row_count * tile_rows, col_count * tile_cols, owned
    )
    result = outgoing(square[0], square[1])
    product = lax.all_to_all(result, ("row", "col"), split_axis=1, concat_axis=3, tiled=True)
    base = lax.all_to_all(pair, "col", split_axis=1, concat_axis=2, tiled=True)
    normed_base = layer_norm(base, gain_input)
    gate = jax.nn.sigmoid(project(normed_base, gate_weights))
    updated = base + gate * project(layer_norm(product, gain_product), weights_out)
    hidden = project(layer_norm(updated, gain_transition), transition_in)
    hidden_width = transition_out.shape[0]
    activated = jax.nn.silu(hidden[..., :hidden_width]) * hidden[..., hidden_width:]
    pair_out = updated + project(activated, transition_out)
    symmetric = pair_out + mirrored(pair_out)
    line_logits = project(symmetric, distogram_weights) + distogram_bias
    return lax.all_to_all(line_logits, "col", split_axis=2, concat_axis=1, tiled=True)


def split_weights(weights, gain=None):
    if gain is not None:
        weights = gain[:, None] * weights
    flipped = weights.T
    high = lax.reduce_precision(flipped, 8, 7)
    low = flipped - high
    return jnp.concatenate([high, high, low], axis=1).astype(jnp.bfloat16)


def estimate(flops, moved):
    return pl.CostEstimate(flops=flops // SCALE, bytes_accessed=moved // SCALE, transcendentals=0)


def parts(values):
    high = values.astype(jnp.bfloat16)
    low = (values - high.astype(jnp.float32)).astype(jnp.bfloat16)
    return high, low


def times(weights3, values):
    high, low = parts(values)
    return jnp.dot(
        weights3, jnp.concatenate([high, low, high], axis=0), preferred_element_type=jnp.float32
    )


def normalized(values):
    center = values - jnp.mean(values, axis=0, keepdims=True)
    spread = jnp.mean(center * center, axis=0, keepdims=True)
    return center * lax.rsqrt(spread + 1e-05)


def hands_kernel(pair_ref, weights_ref, out_ref):
    rows, _, width = pair_ref.shape
    per = 4
    flat = out_ref.reshape(width * rows, LANES)
    for start in range(0, rows, per):
        values = jnp.concatenate([pair_ref[start + n].T for n in range(per)], axis=1)
        projected = times(weights_ref[...], normalized(values))
        result = jax.nn.sigmoid(projected[width:]) * projected[:width]
        for n in range(per):
            flat[pl.ds(start + n, width, stride=rows), :] = result[:, n * LANES : (n + 1) * LANES]


def hands(pair, weights3, left, right):
    _, tile_cols, width = pair.shape
    rows = left[1] + right[1]
    turn = left[1] // GROUP
    lead, shift = left[0] // GROUP, right[0] // GROUP - turn
    return pl.pallas_call(
        hands_kernel,
        grid=(rows // GROUP,),
        in_specs=[
            pl.BlockSpec((GROUP, tile_cols, width), lambda g: (g + jnp.where(g < turn, lead, shift), 0, 0)),
            pl.BlockSpec((2 * width, 3 * width), lambda g: (jnp.where(g < turn, 0, 1), 0)),
        ],
        out_specs=pl.BlockSpec((width, GROUP, tile_cols), lambda g: (0, g, 0)),
        out_shape=jax.ShapeDtypeStruct((width, rows, tile_cols), jnp.float32),
        compiler_params=pltpu.CompilerParams(vmem_limit_bytes=VMEM),
        cost_estimate=estimate(6 * rows * tile_cols * width * 2 * width, 8 * rows * tile_cols * width),
        name="hands",
    )(pair, weights3)


def product_kernel(half_ref, low_ref, high_ref, own_ref, other_ref, out_ref):
    cols = own_ref.shape[0] // 2
    half = half_ref[0]

    def line(ref, lo):
        return jnp.concatenate([ref[lo * cols + c, 0] for c in range(cols)], axis=1)

    left_high, left_low = parts(
        jnp.concatenate([line(ref, lo) for lo in range(2) for ref in (low_ref, high_ref)], axis=0)
    )
    right_high, right_low = parts(
        jnp.concatenate([line(ref, lo) for ref in (own_ref, other_ref) for lo in range(2)], axis=0)
    )
    result = lax.dot_general(
        jnp.concatenate([right_high, right_high, right_low], axis=1),
        jnp.concatenate([left_high, left_low, left_high], axis=1),
        (((1,), (1,)), ((), ())),
        preferred_element_type=jnp.float32,
    )
    rows = own_ref.shape[2]
    wide = result.shape[1] // 2
    for lo in range(2):
        for piece in range(cols):
            source, other_lo = divmod(piece, 2)
            plane = 2 * jnp.where(half == source, 0, 1) + other_lo
            out_ref[lo * cols + plane, 0] = result[
                piece * rows : (piece + 1) * rows, lo * wide : (lo + 1) * wide
            ]


def product(half, low, high, own, other, wide):
    sources, owned, rows, width = own.shape
    k_all = width * sources // 2
    spec = lambda height: pl.BlockSpec((sources, 1, height, width), lambda n, half: (0, n, 0, 0))
    return pl.pallas_call(
        product_kernel,
        grid_spec=pltpu.PrefetchScalarGridSpec(
            num_scalar_prefetch=1,
            grid=(owned,),
            in_specs=[spec(LOWER), spec(wide - LOWER), spec(rows), spec(rows)],
            out_specs=pl.BlockSpec((sources, 1, rows, wide), lambda n, half: (0, n, 0, 0)),
        ),
        out_shape=jax.ShapeDtypeStruct((sources, owned, rows, wide), jnp.float32),
        compiler_params=pltpu.CompilerParams(vmem_limit_bytes=VMEM),
        cost_estimate=estimate(
            6 * owned * 4 * rows * 2 * wide * k_all, 4 * owned * k_all * (2 * wide + 4 * rows)
        ),
        name="product",
    )(half, low, high, own, other)


def head_kernel(
    pair_ref, product_ref, gate_ref, output_ref, up_ref, down_ref, bins_ref, *out_refs
):
    tile_rows, cols, width = pair_ref.shape
    bins = out_refs[0].shape[1]
    per = 4
    flat_pair = pair_ref.reshape(tile_rows * cols, width)
    flat_product = product_ref.reshape(width * cols, tile_rows)
    hidden_width = up_ref.shape[0] // 2
    for start in range(0, cols, per):
        values = jnp.concatenate(
            [flat_pair[pl.ds(start + n, tile_rows, stride=cols), :].T for n in range(per)], axis=1
        )
        product_values = jnp.concatenate(
            [flat_product[pl.ds(start + n, width, stride=cols), :] for n in range(per)], axis=1
        )
        gate = jax.nn.sigmoid(times(gate_ref[...], normalized(values)))
        updated = values + gate * times(output_ref[...], normalized(product_values))
        hidden = times(up_ref[...], normalized(updated))
        activated = jax.nn.silu(hidden[:hidden_width]) * hidden[hidden_width:]
        pair_out = updated + times(down_ref[...], activated)
        logits = times(bins_ref[...], pair_out)
        for n in range(per):
            for part, out_ref in enumerate(out_refs):
                out_ref[start + n] = logits[
                    part * bins : (part + 1) * bins, n * tile_rows : (n + 1) * tile_rows
                ]


def head(pair, product_values, first, count, gate3, output3, up3, down3, bins3):
    tile_rows, tile_cols, width = pair.shape
    chunk_cols = product_values.shape[1]
    steps = chunk_cols // GROUP
    lead = first // GROUP
    bins = bins3.shape[0] // count
    whole = lambda array: pl.BlockSpec(array.shape, lambda g: (0, 0))
    macs = gate3.size + output3.size + up3.size + down3.size + bins3.size
    return pl.pallas_call(
        head_kernel,
        grid=(steps,),
        in_specs=[
            pl.BlockSpec((tile_rows, GROUP, width), lambda g: (0, lead + g, 0)),
            pl.BlockSpec((width, GROUP, tile_rows), lambda g: (0, g, 0)),
            whole(gate3),
            whole(output3),
            whole(up3),
            whole(down3),
            whole(bins3),
        ],
        out_specs=[pl.BlockSpec((GROUP, bins, tile_rows), lambda g: (g, 0, 0))] * count,
        out_shape=[jax.ShapeDtypeStruct((chunk_cols, bins, tile_rows), jnp.float32)] * count,
        compiler_params=pltpu.CompilerParams(vmem_limit_bytes=VMEM),
        cost_estimate=estimate(
            2 * chunk_cols * tile_rows * macs, 4 * chunk_cols * tile_rows * (2 * width + count * bins)
        ),
        name="head",
    )(pair, product_values, gate3, output3, up3, down3, bins3)


def symmetric_kernel(bias_ref, *refs):
    out_ref, blocks = refs[-1], refs[:-1]
    tile_rows, quarters, bins, tile_cols = out_ref.shape
    count = len(blocks) // (2 * quarters)
    flat = out_ref.reshape(tile_rows * quarters * bins, tile_cols)
    for quarter in range(quarters):
        for n in range(bins):

            def joined(start):
                chosen = blocks[(start + quarter) * count : (start + quarter + 1) * count]
                values = [
                    ref.reshape(ref.shape[0] * bins, ref.shape[2])[
                        pl.ds(n, ref.shape[0], stride=bins), :
                    ]
                    for ref in chosen
                ]
                return jnp.concatenate(values, axis=0)

            result = joined(0).T + joined(quarters) + bias_ref[quarter, n : n + 1, :]
            flat[pl.ds(quarter * bins + n, tile_rows, stride=quarters * bins), :] = result


def symmetric(bias, own, mirror):
    quarters, bins, tile_cols = bias.shape
    tile_rows = own[0][0].shape[2]
    arrays, specs = [], []
    for quarter in range(quarters):
        for block in own:
            part, rest = divmod(quarter * bins, block[0].shape[1])
            arrays.append((part, rest // GROUP, block[0].shape))
    chosen = [own[n % len(own)][part] for n, (part, _, _) in enumerate(arrays)]
    chosen += [mirror[n % len(own)][part] for n, (part, _, _) in enumerate(arrays)]
    specs = [
        pl.BlockSpec((shape[0], GROUP, shape[2]), lambda g, lead=lead: (0, lead + g, 0))
        for _, lead, shape in arrays
    ] * 2
    return pl.pallas_call(
        symmetric_kernel,
        grid=(bins // GROUP,),
        in_specs=[pl.BlockSpec((quarters, GROUP, tile_cols), lambda g: (0, g, 0))] + specs,
        out_specs=pl.BlockSpec((tile_rows, quarters, GROUP, tile_cols), lambda g: (0, 0, g, 0)),
        out_shape=jax.ShapeDtypeStruct((tile_rows, quarters, bins, tile_cols), jnp.float32),
        compiler_params=pltpu.CompilerParams(vmem_limit_bytes=VMEM),
        cost_estimate=estimate(0, 12 * tile_rows * quarters * bins * tile_cols),
        name="symmetric",
    )(bias, *chosen)


def move(values, count, target):
    every = [(r, c) for r in range(count) for c in range(count)]
    pairs = [(r * count + c, target(r, c)) for r, c in every]
    return lax.ppermute(values, ("half", "lo", "col"), pairs)


def turn_of(block, part):
    return part if len(block) == 4 else 2 * part


def aside(block, count):
    return [block[0]] + [
        move(block[n], count, lambda r, c: r * count + (c ^ turn_of(block, n)))
        for n in range(1, len(block))
    ]


def across(block, count, part):
    return move(block[part], count, lambda r, c: (c ^ turn_of(block, part)) * count + r)


def half_shards(
    pair,
    gain_input,
    weights_in,
    gate_weights,
    weights_out,
    gain_product,
    gain_transition,
    transition_in,
    transition_out,
    distogram_weights,
    distogram_bias,
):
    row_count = 2 * lax.axis_size("lo")
    col_count = lax.axis_size("col")
    _, tile_rows, tile_cols, width = pair.shape
    tile = pair[0]
    in3 = split_weights(weights_in, gain_input)
    gate3 = split_weights(gate_weights, gain_input)
    output3 = split_weights(weights_out, gain_product)
    up3 = split_weights(transition_in, gain_transition)
    down3 = split_weights(transition_out)
    bins3 = split_weights(distogram_weights)
    sources = 2 * col_count
    owned = width // sources

    def spread(values):
        values = values.reshape(sources, owned, *values.shape[1:])
        return lax.all_to_all(values, ("lo", "col"), split_axis=0, concat_axis=0, tiled=True)

    tie = lax.optimization_barrier
    half = lax.axis_index("half").astype(jnp.int32).reshape(1)
    firsts = [sum(CHUNKS[:n]) for n in range(len(CHUNKS))]
    upper = tile_rows - LOWER

    def exchange(values):
        return lax.ppermute(values, "half", [(0, 1), (1, 0)])

    def blocks(chunk):
        return product(half, low, high, rights[chunk], others[chunk], tile_rows)

    def delivered(values):
        values = lax.all_to_all(values, ("lo", "col"), split_axis=0, concat_axis=0, tiled=True)
        return values.reshape(width, values.shape[2], tile_rows)

    def run_head(values, chunk):
        return head(
            tile, values, firsts[chunk], PARTS[chunk], gate3, output3, up3, down3, bins3
        )

    def mirrored_parts(block):
        shifted = aside(block, row_count)
        return [across(shifted, row_count, part) for part in range(len(block))]

    right = spread(hands(tile, in3, (0, 0), (firsts[0], CHUNKS[0])))
    rights, others = [right], [exchange(right)]
    low = spread(hands(tile, in3, (0, LOWER), (firsts[1], CHUNKS[1])))
    rights.append(low[:, :, LOWER:])
    sent = hands(tile, in3, (LOWER, upper), (firsts[2], CHUNKS[2]))
    sent, others[0], rights[1] = tie((sent, others[0], rights[1]))
    others.append(exchange(rights[1]))
    high = spread(sent)
    rights.append(high[:, :, upper:])
    values, others[1], rights[2] = tie((blocks(0), others[1], rights[2]))
    others.append(exchange(rights[2]))
    values, after = tie((delivered(values), blocks(1)))
    own = [run_head(values, 0)]
    mirror = [mirrored_parts(own[0])]
    after, others[2], mirror[0] = tie((after, others[2], mirror[0]))
    values, after = tie((delivered(after), blocks(2)))
    own.append(run_head(values, 1))
    values, own[1] = tie((delivered(after), own[1]))
    own.append(run_head(values, 2))
    mirror += [mirrored_parts(block) for block in own[1:]]
    quarters = 4
    bins = distogram_bias.shape[0] // quarters
    bias = jnp.broadcast_to(distogram_bias.reshape(quarters, bins, 1), (quarters, bins, tile_cols))
    logits = symmetric(bias, own, mirror).reshape(tile_rows, quarters * bins, tile_cols)
    return jnp.swapaxes(logits, 1, 2)[None]


def solution(mesh):
    names = mesh.axis_names
    crops, rows, cols = (mesh.shape[name] for name in names)

    def run(pair, *parameters):
        crop_count, height, across, width = pair.shape
        tile_rows, tile_cols = height // rows, across // cols
        by_halves = (
            crop_count == crops
            and rows == cols == 4
            and tile_rows == tile_cols == LANES
            and width == LANES
        )
        if by_halves:
            halves = Mesh(mesh.devices.reshape(crops, 2, rows // 2, cols), ("crop", "half", "lo", "col"))
            spec, used, body = P("crop", ("half", "lo"), "col", None), halves, half_shards
        else:
            spec, used, body = P("crop", "row", "col", None), mesh, general_shards
        return jax.shard_map(
            body,
            mesh=used,
            in_specs=(spec,) + (P(),) * len(parameters),
            out_specs=spec,
            check_vma=False,
        )(pair, *parameters)

    return run
```

```python
import functools

import jax
import jax.numpy as jnp
from jax import lax
from jax.experimental import pallas as pl
from jax.experimental.pallas import tpu as pltpu
from jax.sharding import Mesh, PartitionSpec as P

HIGH = lax.Precision.HIGHEST
LANES = 128
GROUP = 8
CHUNKS = (40, 56, 32)
LOWER = 40
PARTS = (4, 4, 4)
VMEM = 56 * 1024 * 1024
SCALE = 8


def layer_norm(values, gain):
    center = values - jnp.mean(values, axis=-1, keepdims=True)
    spread = jnp.mean(center * center, axis=-1, keepdims=True)
    return center * lax.rsqrt(spread + 1e-05) * gain


def project(values, weights):
    return jnp.einsum("...c,cd->...d", values, weights, precision=HIGH)


def outgoing(left_hand, right_hand):
    return jnp.einsum("bikc,bjkc->bijc", left_hand, right_hand, precision=HIGH)


def mirrored(values):
    columns = lax.all_to_all(values, ("row", "col"), split_axis=2, concat_axis=1, tiled=True)
    return jnp.swapaxes(columns, 1, 2)


def general_shards(
    pair,
    gain_input,
    weights_in,
    gate_weights,
    weights_out,
    gain_product,
    gain_transition,
    transition_in,
    transition_out,
    distogram_weights,
    distogram_bias,
):
    row_count = lax.axis_size("row")
    col_count = lax.axis_size("col")
    crops, tile_rows, tile_cols, width = pair.shape
    normed = layer_norm(pair, gain_input)
    projected = project(normed, weights_in)
    left_hand = jax.nn.sigmoid(projected[..., width : 2 * width]) * projected[..., :width]
    right_hand = jax.nn.sigmoid(projected[..., 3 * width :]) * projected[..., 2 * width : 3 * width]
    stacked = jnp.stack([left_hand, right_hand], axis=0)
    received = lax.all_to_all(stacked, ("row", "col"), split_axis=4, concat_axis=2, tiled=True)
    items = received.shape[1]
    owned = received.shape[4]
    square = received.reshape(2, items, row_count, col_count, tile_rows, tile_cols, owned)
    square = square.transpose(0, 1, 2, 4, 3, 5, 6).reshape(
        2, items, row_count * tile_rows, col_count * tile_cols, owned
    )
    result = outgoing(square[0], square[1])
    product = lax.all_to_all(result, ("row", "col"), split_axis=1, concat_axis=3, tiled=True)
    base = lax.all_to_all(pair, "col", split_axis=1, concat_axis=2, tiled=True)
    normed_base = layer_norm(base, gain_input)
    gate = jax.nn.sigmoid(project(normed_base, gate_weights))
    updated = base + gate * project(layer_norm(product, gain_product), weights_out)
    hidden = project(layer_norm(updated, gain_transition), transition_in)
    hidden_width = transition_out.shape[0]
    activated = jax.nn.silu(hidden[..., :hidden_width]) * hidden[..., hidden_width:]
    pair_out = updated + project(activated, transition_out)
    symmetric = pair_out + mirrored(pair_out)
    line_logits = project(symmetric, distogram_weights) + distogram_bias
    return lax.all_to_all(line_logits, "col", split_axis=2, concat_axis=1, tiled=True)


def split_weights(weights, gain=None):
    if gain is not None:
        weights = gain[:, None] * weights
    flipped = weights.T
    high = lax.reduce_precision(flipped, 8, 7)
    low = flipped - high
    return jnp.concatenate([high, high, low], axis=1).astype(jnp.bfloat16)


def estimate(flops, moved):
    return pl.CostEstimate(flops=flops // SCALE, bytes_accessed=moved // SCALE, transcendentals=0)


def parts(values):
    high = values.astype(jnp.bfloat16)
    low = (values - high.astype(jnp.float32)).astype(jnp.bfloat16)
    return high, low


def times(weights3, values):
    high, low = parts(values)
    return jnp.dot(
        weights3, jnp.concatenate([high, low, high], axis=0), preferred_element_type=jnp.float32
    )


def normalized(values):
    center = values - jnp.mean(values, axis=0, keepdims=True)
    spread = jnp.mean(center * center, axis=0, keepdims=True)
    return center * lax.rsqrt(spread + 1e-05)


def hands_kernel(pair_ref, weights_ref, out_ref):
    rows, _, width = pair_ref.shape
    per = 4
    flat = out_ref.reshape(width * rows, LANES)
    for start in range(0, rows, per):
        values = jnp.concatenate([pair_ref[start + n].T for n in range(per)], axis=1)
        projected = times(weights_ref[...], normalized(values))
        result = jax.nn.sigmoid(projected[width:]) * projected[:width]
        for n in range(per):
            flat[pl.ds(start + n, width, stride=rows), :] = result[:, n * LANES : (n + 1) * LANES]


def hands(pair, weights3, left, right):
    _, tile_cols, width = pair.shape
    rows = left[1] + right[1]
    turn = left[1] // GROUP
    lead, shift = left[0] // GROUP, right[0] // GROUP - turn
    return pl.pallas_call(
        hands_kernel,
        grid=(rows // GROUP,),
        in_specs=[
            pl.BlockSpec((GROUP, tile_cols, width), lambda g: (g + jnp.where(g < turn, lead, shift), 0, 0)),
            pl.BlockSpec((2 * width, 3 * width), lambda g: (jnp.where(g < turn, 0, 1), 0)),
        ],
        out_specs=pl.BlockSpec((width, GROUP, tile_cols), lambda g: (0, g, 0)),
        out_shape=jax.ShapeDtypeStruct((width, rows, tile_cols), jnp.float32),
        compiler_params=pltpu.CompilerParams(vmem_limit_bytes=VMEM),
        cost_estimate=estimate(6 * rows * tile_cols * width * 2 * width, 8 * rows * tile_cols * width),
        name="hands",
    )(pair, weights3)


def product_kernel(half_ref, low_ref, high_ref, own_ref, other_ref, out_ref):
    cols = own_ref.shape[0] // 2
    half = half_ref[0]

    def line(ref, lo):
        return jnp.concatenate([ref[lo * cols + c, 0] for c in range(cols)], axis=1)

    left_high, left_low = parts(
        jnp.concatenate([line(ref, lo) for lo in range(2) for ref in (low_ref, high_ref)], axis=0)
    )
    right_high, right_low = parts(
        jnp.concatenate([line(ref, lo) for ref in (own_ref, other_ref) for lo in range(2)], axis=0)
    )
    result = lax.dot_general(
        jnp.concatenate([right_high, right_high, right_low], axis=1),
        jnp.concatenate([left_high, left_low, left_high], axis=1),
        (((1,), (1,)), ((), ())),
        preferred_element_type=jnp.float32,
    )
    rows = own_ref.shape[2]
    wide = result.shape[1] // 2
    for lo in range(2):
        for piece in range(cols):
            source, other_lo = divmod(piece, 2)
            plane = 2 * jnp.where(half == source, 0, 1) + other_lo
            out_ref[lo * cols + plane, 0] = result[
                piece * rows : (piece + 1) * rows, lo * wide : (lo + 1) * wide
            ]


def product(half, low, high, own, other, wide):
    sources, owned, rows, width = own.shape
    k_all = width * sources // 2
    spec = lambda height: pl.BlockSpec((sources, 1, height, width), lambda n, half: (0, n, 0, 0))
    return pl.pallas_call(
        product_kernel,
        grid_spec=pltpu.PrefetchScalarGridSpec(
            num_scalar_prefetch=1,
            grid=(owned,),
            in_specs=[spec(LOWER), spec(wide - LOWER), spec(rows), spec(rows)],
            out_specs=pl.BlockSpec((sources, 1, rows, wide), lambda n, half: (0, n, 0, 0)),
        ),
        out_shape=jax.ShapeDtypeStruct((sources, owned, rows, wide), jnp.float32),
        compiler_params=pltpu.CompilerParams(vmem_limit_bytes=VMEM),
        cost_estimate=estimate(
            6 * owned * 4 * rows * 2 * wide * k_all, 4 * owned * k_all * (2 * wide + 4 * rows)
        ),
        name="product",
    )(half, low, high, own, other)


def head_kernel(
    pair_ref, product_ref, gate_ref, output_ref, up_ref, down_ref, bins_ref, *out_refs
):
    tile_rows, cols, width = pair_ref.shape
    bins = out_refs[0].shape[1]
    per = 4
    flat_pair = pair_ref.reshape(tile_rows * cols, width)
    flat_product = product_ref.reshape(width * cols, tile_rows)
    hidden_width = up_ref.shape[0] // 2
    for start in range(0, cols, per):
        values = jnp.concatenate(
            [flat_pair[pl.ds(start + n, tile_rows, stride=cols), :].T for n in range(per)], axis=1
        )
        product_values = jnp.concatenate(
            [flat_product[pl.ds(start + n, width, stride=cols), :] for n in range(per)], axis=1
        )
        gate = jax.nn.sigmoid(times(gate_ref[...], normalized(values)))
        updated = values + gate * times(output_ref[...], normalized(product_values))
        hidden = times(up_ref[...], normalized(updated))
        activated = jax.nn.silu(hidden[:hidden_width]) * hidden[hidden_width:]
        pair_out = updated + times(down_ref[...], activated)
        logits = times(bins_ref[...], pair_out)
        for n in range(per):
            for part, out_ref in enumerate(out_refs):
                out_ref[start + n] = logits[
                    part * bins : (part + 1) * bins, n * tile_rows : (n + 1) * tile_rows
                ]


def head(pair, product_values, first, count, gate3, output3, up3, down3, bins3):
    tile_rows, tile_cols, width = pair.shape
    chunk_cols = product_values.shape[1]
    steps = chunk_cols // GROUP
    lead = first // GROUP
    bins = bins3.shape[0] // count
    whole = lambda array: pl.BlockSpec(array.shape, lambda g: (0, 0))
    macs = gate3.size + output3.size + up3.size + down3.size + bins3.size
    return pl.pallas_call(
        head_kernel,
        grid=(steps,),
        in_specs=[
            pl.BlockSpec((tile_rows, GROUP, width), lambda g: (0, lead + g, 0)),
            pl.BlockSpec((width, GROUP, tile_rows), lambda g: (0, g, 0)),
            whole(gate3),
            whole(output3),
            whole(up3),
            whole(down3),
            whole(bins3),
        ],
        out_specs=[pl.BlockSpec((GROUP, bins, tile_rows), lambda g: (g, 0, 0))] * count,
        out_shape=[jax.ShapeDtypeStruct((chunk_cols, bins, tile_rows), jnp.float32)] * count,
        compiler_params=pltpu.CompilerParams(vmem_limit_bytes=VMEM),
        cost_estimate=estimate(
            2 * chunk_cols * tile_rows * macs, 4 * chunk_cols * tile_rows * (2 * width + count * bins)
        ),
        name="head",
    )(pair, product_values, gate3, output3, up3, down3, bins3)


def symmetric_kernel(bias_ref, *refs):
    out_ref, blocks = refs[-1], refs[:-1]
    tile_rows, quarters, bins, tile_cols = out_ref.shape
    count = len(blocks) // (2 * quarters)
    flat = out_ref.reshape(tile_rows * quarters * bins, tile_cols)
    for quarter in range(quarters):
        for n in range(bins):

            def joined(start):
                chosen = blocks[(start + quarter) * count : (start + quarter + 1) * count]
                values = [
                    ref.reshape(ref.shape[0] * bins, ref.shape[2])[
                        pl.ds(n, ref.shape[0], stride=bins), :
                    ]
                    for ref in chosen
                ]
                return jnp.concatenate(values, axis=0)

            result = joined(0).T + joined(quarters) + bias_ref[quarter, n : n + 1, :]
            flat[pl.ds(quarter * bins + n, tile_rows, stride=quarters * bins), :] = result


def symmetric(bias, own, mirror):
    quarters, bins, tile_cols = bias.shape
    tile_rows = own[0][0].shape[2]
    arrays, specs = [], []
    for quarter in range(quarters):
        for block in own:
            part, rest = divmod(quarter * bins, block[0].shape[1])
            arrays.append((part, rest // GROUP, block[0].shape))
    chosen = [own[n % len(own)][part] for n, (part, _, _) in enumerate(arrays)]
    chosen += [mirror[n % len(own)][part] for n, (part, _, _) in enumerate(arrays)]
    specs = [
        pl.BlockSpec((shape[0], GROUP, shape[2]), lambda g, lead=lead: (0, lead + g, 0))
        for _, lead, shape in arrays
    ] * 2
    return pl.pallas_call(
        symmetric_kernel,
        grid=(bins // GROUP,),
        in_specs=[pl.BlockSpec((quarters, GROUP, tile_cols), lambda g: (0, g, 0))] + specs,
        out_specs=pl.BlockSpec((tile_rows, quarters, GROUP, tile_cols), lambda g: (0, 0, g, 0)),
        out_shape=jax.ShapeDtypeStruct((tile_rows, quarters, bins, tile_cols), jnp.float32),
        compiler_params=pltpu.CompilerParams(vmem_limit_bytes=VMEM),
        cost_estimate=estimate(0, 12 * tile_rows * quarters * bins * tile_cols),
        name="symmetric",
    )(bias, *chosen)


def move(values, count, target):
    every = [(r, c) for r in range(count) for c in range(count)]
    pairs = [(r * count + c, target(r, c)) for r, c in every]
    return lax.ppermute(values, ("half", "lo", "col"), pairs)


def turn_of(block, part):
    return part if len(block) == 4 else 2 * part


def aside(block, count):
    return [block[0]] + [
        move(block[n], count, lambda r, c: r * count + (c ^ turn_of(block, n)))
        for n in range(1, len(block))
    ]


def across(block, count, part):
    return move(block[part], count, lambda r, c: (c ^ turn_of(block, part)) * count + r)


def half_shards(
    pair,
    gain_input,
    weights_in,
    gate_weights,
    weights_out,
    gain_product,
    gain_transition,
    transition_in,
    transition_out,
    distogram_weights,
    distogram_bias,
):
    row_count = 2 * lax.axis_size("lo")
    col_count = lax.axis_size("col")
    _, tile_rows, tile_cols, width = pair.shape
    tile = pair[0]
    in3 = split_weights(weights_in, gain_input)
    gate3 = split_weights(gate_weights, gain_input)
    output3 = split_weights(weights_out, gain_product)
    up3 = split_weights(transition_in, gain_transition)
    down3 = split_weights(transition_out)
    bins3 = split_weights(distogram_weights)
    sources = 2 * col_count
    owned = width // sources

    def spread(values):
        values = values.reshape(sources, owned, *values.shape[1:])
        return lax.all_to_all(values, ("lo", "col"), split_axis=0, concat_axis=0, tiled=True)

    tie = lax.optimization_barrier
    half = lax.axis_index("half").astype(jnp.int32).reshape(1)
    firsts = [sum(CHUNKS[:n]) for n in range(len(CHUNKS))]
    upper = tile_rows - LOWER

    def exchange(values):
        return lax.ppermute(values, "half", [(0, 1), (1, 0)])

    def blocks(chunk):
        return product(half, low, high, rights[chunk], others[chunk], tile_rows)

    def delivered(values):
        values = lax.all_to_all(values, ("lo", "col"), split_axis=0, concat_axis=0, tiled=True)
        return values.reshape(width, values.shape[2], tile_rows)

    def run_head(values, chunk):
        return head(
            tile, values, firsts[chunk], PARTS[chunk], gate3, output3, up3, down3, bins3
        )

    def mirrored_parts(block):
        shifted = aside(block, row_count)
        return [across(shifted, row_count, part) for part in range(len(block))]

    right = spread(hands(tile, in3, (0, 0), (firsts[0], CHUNKS[0])))
    rights, others = [right], [exchange(right)]
    low = spread(hands(tile, in3, (0, LOWER), (firsts[1], CHUNKS[1])))
    rights.append(low[:, :, LOWER:])
    sent = hands(tile, in3, (LOWER, upper), (firsts[2], CHUNKS[2]))
    sent, others[0], rights[1] = tie((sent, others[0], rights[1]))
    others.append(exchange(rights[1]))
    high = spread(sent)
    rights.append(high[:, :, upper:])
    values, others[1], rights[2] = tie((blocks(0), others[1], rights[2]))
    others.append(exchange(rights[2]))
    values, after = tie((delivered(values), blocks(1)))
    own = [run_head(values, 0)]
    mirror = [mirrored_parts(own[0])]
    after, others[2], mirror[0] = tie((after, others[2], mirror[0]))
    values, after = tie((delivered(after), blocks(2)))
    own.append(run_head(values, 1))
    shifted = aside(own[1], row_count)
    straight = across(shifted, row_count, 0)
    values, own[1] = tie((delivered(after), own[1]))
    late, shifted, straight = tie((run_head(values, 2), shifted, straight))
    own.append(late)
    mirror.append([straight] + [across(shifted, row_count, part) for part in range(1, PARTS[1])])
    mirror.append(mirrored_parts(late))
    quarters = 4
    bins = distogram_bias.shape[0] // quarters
    bias = jnp.broadcast_to(distogram_bias.reshape(quarters, bins, 1), (quarters, bins, tile_cols))
    logits = symmetric(bias, own, mirror).reshape(tile_rows, quarters * bins, tile_cols)
    return jnp.swapaxes(logits, 1, 2)[None]


def solution(mesh):
    names = mesh.axis_names
    crops, rows, cols = (mesh.shape[name] for name in names)

    def run(pair, *parameters):
        crop_count, height, across, width = pair.shape
        tile_rows, tile_cols = height // rows, across // cols
        by_halves = (
            crop_count == crops
            and rows == cols == 4
            and tile_rows == tile_cols == LANES
            and width == LANES
        )
        if by_halves:
            halves = Mesh(mesh.devices.reshape(crops, 2, rows // 2, cols), ("crop", "half", "lo", "col"))
            spec, used, body = P("crop", ("half", "lo"), "col", None), halves, half_shards
        else:
            spec, used, body = P("crop", "row", "col", None), mesh, general_shards
        return jax.shard_map(
            body,
            mesh=used,
            in_specs=(spec,) + (P(),) * len(parameters),
            out_specs=spec,
            check_vma=False,
        )(pair, *parameters)

    return run
```

```python
import functools

import jax
import jax.numpy as jnp
from jax import lax
from jax.experimental import pallas as pl
from jax.experimental.pallas import tpu as pltpu
from jax.sharding import Mesh, PartitionSpec as P

HIGH = lax.Precision.HIGHEST
LANES = 128
GROUP = 8
STEP = 2
CHUNKS = (40, 56, 32)
LOWER = 40
PARTS = 4
VMEM = 56 * 1024 * 1024
SCALE = 8


def layer_norm(values, gain):
    center = values - jnp.mean(values, axis=-1, keepdims=True)
    spread = jnp.mean(center * center, axis=-1, keepdims=True)
    return center * lax.rsqrt(spread + 1e-05) * gain


def project(values, weights):
    return jnp.einsum("...c,cd->...d", values, weights, precision=HIGH)


def outgoing(left_hand, right_hand):
    return jnp.einsum("bikc,bjkc->bijc", left_hand, right_hand, precision=HIGH)


def mirrored(values):
    columns = lax.all_to_all(values, ("row", "col"), split_axis=2, concat_axis=1, tiled=True)
    return jnp.swapaxes(columns, 1, 2)


def general_shards(
    pair,
    gain_input,
    weights_in,
    gate_weights,
    weights_out,
    gain_product,
    gain_transition,
    transition_in,
    transition_out,
    distogram_weights,
    distogram_bias,
):
    row_count = lax.axis_size("row")
    col_count = lax.axis_size("col")
    crops, tile_rows, tile_cols, width = pair.shape
    normed = layer_norm(pair, gain_input)
    projected = project(normed, weights_in)
    left_hand = jax.nn.sigmoid(projected[..., width : 2 * width]) * projected[..., :width]
    right_hand = jax.nn.sigmoid(projected[..., 3 * width :]) * projected[..., 2 * width : 3 * width]
    stacked = jnp.stack([left_hand, right_hand], axis=0)
    received = lax.all_to_all(stacked, ("row", "col"), split_axis=4, concat_axis=2, tiled=True)
    items = received.shape[1]
    owned = received.shape[4]
    square = received.reshape(2, items, row_count, col_count, tile_rows, tile_cols, owned)
    square = square.transpose(0, 1, 2, 4, 3, 5, 6).reshape(
        2, items, row_count * tile_rows, col_count * tile_cols, owned
    )
    result = outgoing(square[0], square[1])
    product = lax.all_to_all(result, ("row", "col"), split_axis=1, concat_axis=3, tiled=True)
    base = lax.all_to_all(pair, "col", split_axis=1, concat_axis=2, tiled=True)
    normed_base = layer_norm(base, gain_input)
    gate = jax.nn.sigmoid(project(normed_base, gate_weights))
    updated = base + gate * project(layer_norm(product, gain_product), weights_out)
    hidden = project(layer_norm(updated, gain_transition), transition_in)
    hidden_width = transition_out.shape[0]
    activated = jax.nn.silu(hidden[..., :hidden_width]) * hidden[..., hidden_width:]
    pair_out = updated + project(activated, transition_out)
    symmetric = pair_out + mirrored(pair_out)
    line_logits = project(symmetric, distogram_weights) + distogram_bias
    return lax.all_to_all(line_logits, "col", split_axis=2, concat_axis=1, tiled=True)


def split_weights(weights, gain=None):
    if gain is not None:
        weights = gain[:, None] * weights
    flipped = weights.T
    high = lax.reduce_precision(flipped, 8, 7)
    low = flipped - high
    return jnp.concatenate([high, high, low], axis=1).astype(jnp.bfloat16)


def estimate(flops, moved):
    return pl.CostEstimate(flops=flops // SCALE, bytes_accessed=moved // SCALE, transcendentals=0)


def parts(values):
    high = values.astype(jnp.bfloat16)
    low = (values - high.astype(jnp.float32)).astype(jnp.bfloat16)
    return high, low


def times(weights3, values):
    high, low = parts(values)
    return jnp.dot(
        weights3, jnp.concatenate([high, low, high], axis=0), preferred_element_type=jnp.float32
    )


def normalized(values):
    center = values - jnp.mean(values, axis=0, keepdims=True)
    spread = jnp.mean(center * center, axis=0, keepdims=True)
    return center * lax.rsqrt(spread + 1e-05)


def hands_kernel(pair_ref, weights_ref, out_ref):
    rows, _, width = pair_ref.shape
    per = 4
    flat = out_ref.reshape(width * rows, LANES)
    for start in range(0, rows, per):
        values = jnp.concatenate([pair_ref[start + n].T for n in range(per)], axis=1)
        projected = times(weights_ref[...], normalized(values))
        result = jax.nn.sigmoid(projected[width:]) * projected[:width]
        for n in range(per):
            flat[pl.ds(start + n, width, stride=rows), :] = result[:, n * LANES : (n + 1) * LANES]


def hands(pair, weights3, left, right):
    _, tile_cols, width = pair.shape
    rows = left[1] + right[1]
    turn = left[1] // GROUP
    lead, shift = left[0] // GROUP, right[0] // GROUP - turn
    return pl.pallas_call(
        hands_kernel,
        grid=(rows // GROUP,),
        in_specs=[
            pl.BlockSpec((GROUP, tile_cols, width), lambda g: (g + jnp.where(g < turn, lead, shift), 0, 0)),
            pl.BlockSpec((2 * width, 3 * width), lambda g: (jnp.where(g < turn, 0, 1), 0)),
        ],
        out_specs=pl.BlockSpec((width, GROUP, tile_cols), lambda g: (0, g, 0)),
        out_shape=jax.ShapeDtypeStruct((width, rows, tile_cols), jnp.float32),
        compiler_params=pltpu.CompilerParams(vmem_limit_bytes=VMEM),
        cost_estimate=estimate(6 * rows * tile_cols * width * 2 * width, 8 * rows * tile_cols * width),
        name="hands",
    )(pair, weights3)


def product_kernel(half_ref, low_ref, high_ref, own_ref, other_ref, out_ref):
    cols = own_ref.shape[0] // 2
    half = half_ref[0]
    rows = own_ref.shape[2]
    for n in range(own_ref.shape[1]):

        def line(ref, lo):
            return jnp.concatenate([ref[lo * cols + c, n] for c in range(cols)], axis=1)

        left_high, left_low = parts(
            jnp.concatenate(
                [line(ref, lo) for lo in range(2) for ref in (low_ref, high_ref)], axis=0
            )
        )
        right_high, right_low = parts(
            jnp.concatenate(
                [line(ref, lo) for ref in (own_ref, other_ref) for lo in range(2)], axis=0
            )
        )
        result = lax.dot_general(
            jnp.concatenate([right_high, right_high, right_low], axis=1),
            jnp.concatenate([left_high, left_low, left_high], axis=1),
            (((1,), (1,)), ((), ())),
            preferred_element_type=jnp.float32,
        )
        wide = result.shape[1] // 2
        for lo in range(2):
            for piece in range(cols):
                source, other_lo = divmod(piece, 2)
                plane = 2 * jnp.where(half == source, 0, 1) + other_lo
                out_ref[lo * cols + plane, n] = result[
                    piece * rows : (piece + 1) * rows, lo * wide : (lo + 1) * wide
                ]


def product(half, low, high, own, other, wide):
    sources, owned, rows, width = own.shape
    k_all = width * sources // 2
    spec_out = pl.BlockSpec((sources, STEP, rows, wide), lambda n, half: (0, n, 0, 0))
    spec = lambda height: pl.BlockSpec(
        (sources, STEP, height, width), lambda n, half: (0, n, 0, 0)
    )
    return pl.pallas_call(
        product_kernel,
        grid_spec=pltpu.PrefetchScalarGridSpec(
            num_scalar_prefetch=1,
            grid=(owned // STEP,),
            in_specs=[spec(LOWER), spec(wide - LOWER), spec(rows), spec(rows)],
            out_specs=spec_out,
        ),
        out_shape=jax.ShapeDtypeStruct((sources, owned, rows, wide), jnp.float32),
        compiler_params=pltpu.CompilerParams(vmem_limit_bytes=VMEM),
        cost_estimate=estimate(
            6 * owned * 4 * rows * 2 * wide * k_all, 4 * owned * k_all * (2 * wide + 4 * rows)
        ),
        name="product",
    )(half, low, high, own, other)


def head_kernel(
    pair_ref, product_ref, gate_ref, output_ref, up_ref, down_ref, bins_ref, *out_refs
):
    tile_rows, cols, width = pair_ref.shape
    bins = out_refs[0].shape[1]
    per = 4
    flat_pair = pair_ref.reshape(tile_rows * cols, width)
    flat_product = product_ref.reshape(width * cols, tile_rows)
    hidden_width = up_ref.shape[0] // 2
    for start in range(0, cols, per):
        values = jnp.concatenate(
            [flat_pair[pl.ds(start + n, tile_rows, stride=cols), :].T for n in range(per)], axis=1
        )
        product_values = jnp.concatenate(
            [flat_product[pl.ds(start + n, width, stride=cols), :] for n in range(per)], axis=1
        )
        gate = jax.nn.sigmoid(times(gate_ref[...], normalized(values)))
        updated = values + gate * times(output_ref[...], normalized(product_values))
        hidden = times(up_ref[...], normalized(updated))
        activated = jax.nn.silu(hidden[:hidden_width]) * hidden[hidden_width:]
        pair_out = updated + times(down_ref[...], activated)
        logits = times(bins_ref[...], pair_out)
        for n in range(per):
            for part, out_ref in enumerate(out_refs):
                out_ref[start + n] = logits[
                    part * bins : (part + 1) * bins, n * tile_rows : (n + 1) * tile_rows
                ]


def head(pair, product_values, first, gate3, output3, up3, down3, bins3):
    tile_rows, tile_cols, width = pair.shape
    chunk_cols = product_values.shape[1]
    steps = chunk_cols // GROUP
    lead = first // GROUP
    bins = bins3.shape[0] // PARTS
    whole = lambda array: pl.BlockSpec(array.shape, lambda g: (0, 0))
    macs = gate3.size + output3.size + up3.size + down3.size + bins3.size
    return pl.pallas_call(
        head_kernel,
        grid=(steps,),
        in_specs=[
            pl.BlockSpec((tile_rows, GROUP, width), lambda g: (0, lead + g, 0)),
            pl.BlockSpec((width, GROUP, tile_rows), lambda g: (0, g, 0)),
            whole(gate3),
            whole(output3),
            whole(up3),
            whole(down3),
            whole(bins3),
        ],
        out_specs=[pl.BlockSpec((GROUP, bins, tile_rows), lambda g: (g, 0, 0))] * PARTS,
        out_shape=[jax.ShapeDtypeStruct((chunk_cols, bins, tile_rows), jnp.float32)] * PARTS,
        compiler_params=pltpu.CompilerParams(vmem_limit_bytes=VMEM),
        cost_estimate=estimate(
            2 * chunk_cols * tile_rows * macs, 4 * chunk_cols * tile_rows * (2 * width + PARTS * bins)
        ),
        name="head",
    )(pair, product_values, gate3, output3, up3, down3, bins3)


def turned_kernel(bias_ref, *refs):
    out_ref, sources = refs[-1], refs[:-1]
    count = len(sources) // PARTS
    tile_rows, _, bins, tile_cols = out_ref.shape
    flat = out_ref.reshape(tile_rows * PARTS * bins, tile_cols)
    for part in range(PARTS):
        for n in range(bins):
            values = [
                ref.reshape(ref.shape[0] * bins, tile_rows)[pl.ds(n, ref.shape[0], stride=bins), :]
                for ref in sources[part * count : (part + 1) * count]
            ]
            result = jnp.concatenate(values, axis=0).T + bias_ref[part, n : n + 1, :]
            flat[pl.ds(part * bins + n, tile_rows, stride=PARTS * bins), :] = result


def turned(bias, own):
    arrays = [block[part] for part in range(PARTS) for block in own]
    _, bins, tile_rows = arrays[0].shape
    tile_cols = sum(block[0].shape[0] for block in own)
    block = lambda rows: pl.BlockSpec((rows, GROUP, tile_rows), lambda g: (0, g, 0))
    return pl.pallas_call(
        turned_kernel,
        grid=(bins // GROUP,),
        in_specs=[pl.BlockSpec((PARTS, GROUP, tile_cols), lambda g: (0, g, 0))]
        + [block(array.shape[0]) for array in arrays],
        out_specs=pl.BlockSpec((tile_rows, PARTS, GROUP, tile_cols), lambda g: (0, 0, g, 0)),
        out_shape=jax.ShapeDtypeStruct((tile_rows, PARTS, bins, tile_cols), jnp.float32),
        compiler_params=pltpu.CompilerParams(vmem_limit_bytes=VMEM),
        cost_estimate=estimate(0, 8 * tile_rows * PARTS * bins * tile_cols),
        name="turned",
    )(bias, *arrays)


def joined_kernel(base_ref, *refs):
    out_ref = refs[-1]
    for part, ref in enumerate(refs[:-1]):
        out_ref[:, part] = base_ref[:, part] + ref[...]


def joined(base, mirror, first):
    rows, bins, tile_cols = mirror[0].shape
    lead = first // GROUP
    whole = pl.BlockSpec((GROUP, PARTS, bins, tile_cols), lambda g: (lead + g, 0, 0, 0))
    block = pl.BlockSpec((GROUP, bins, tile_cols), lambda g: (g, 0, 0))
    return pl.pallas_call(
        joined_kernel,
        grid=(rows // GROUP,),
        in_specs=[whole] + [block] * PARTS,
        out_specs=whole,
        out_shape=jax.ShapeDtypeStruct(base.shape, jnp.float32),
        input_output_aliases={0: 0},
        compiler_params=pltpu.CompilerParams(vmem_limit_bytes=VMEM),
        cost_estimate=estimate(0, 12 * PARTS * rows * bins * tile_cols),
        name="joined",
    )(base, *mirror)


def move(values, count, target):
    every = [(r, c) for r in range(count) for c in range(count)]
    pairs = [(r * count + c, target(r, c)) for r, c in every]
    return lax.ppermute(values, ("half", "lo", "col"), pairs)


def aside(block, count):
    return [block[0]] + [
        move(block[n], count, lambda r, c: r * count + (c ^ n)) for n in range(1, len(block))
    ]


def across(shifted, count):
    return [
        move(values, count, lambda r, c: (c ^ n) * count + r) for n, values in enumerate(shifted)
    ]


def half_shards(
    pair,
    gain_input,
    weights_in,
    gate_weights,
    weights_out,
    gain_product,
    gain_transition,
    transition_in,
    transition_out,
    distogram_weights,
    distogram_bias,
):
    row_count = 2 * lax.axis_size("lo")
    col_count = lax.axis_size("col")
    _, tile_rows, tile_cols, width = pair.shape
    tile = pair[0]
    in3 = split_weights(weights_in, gain_input)
    gate3 = split_weights(gate_weights, gain_input)
    output3 = split_weights(weights_out, gain_product)
    up3 = split_weights(transition_in, gain_transition)
    down3 = split_weights(transition_out)
    bins3 = split_weights(distogram_weights)
    sources = 2 * col_count
    owned = width // sources

    def spread(values):
        values = values.reshape(sources, owned, *values.shape[1:])
        return lax.all_to_all(values, ("lo", "col"), split_axis=0, concat_axis=0, tiled=True)

    tie = lax.optimization_barrier
    half = lax.axis_index("half").astype(jnp.int32).reshape(1)
    firsts = [sum(CHUNKS[:n]) for n in range(len(CHUNKS))]
    upper = tile_rows - LOWER

    def exchange(values):
        return lax.ppermute(values, "half", [(0, 1), (1, 0)])

    def finish(values, chunk):
        values = lax.all_to_all(values, ("lo", "col"), split_axis=0, concat_axis=0, tiled=True)
        values = values.reshape(width, CHUNKS[chunk], tile_rows)
        return head(tile, values, firsts[chunk], gate3, output3, up3, down3, bins3)

    right = spread(hands(tile, in3, (0, 0), (firsts[0], CHUNKS[0])))
    rights, others = [right], [exchange(right)]
    low = spread(hands(tile, in3, (0, LOWER), (firsts[1], CHUNKS[1])))
    rights.append(low[:, :, LOWER:])
    others.append(exchange(rights[1]))
    sent = hands(tile, in3, (LOWER, upper), (firsts[2], CHUNKS[2]))
    sent, others[0] = tie((sent, others[0]))
    high = spread(sent)
    rights.append(high[:, :, upper:])
    others.append(exchange(rights[2]))

    def blocks(chunk):
        return product(half, low, high, rights[chunk], others[chunk], tile_rows)

    values, others[1] = tie((blocks(0), others[1]))
    own = [finish(values, 0)]
    shifted = aside(own[0], row_count)
    values, others[2], shifted = tie((blocks(1), others[2], shifted))
    mirror = [across(shifted, row_count)]
    own.append(finish(values, 1))
    values, mirror[0] = tie((blocks(2), mirror[0]))
    own.append(finish(values, 2))
    mirror += [across(aside(block, row_count), row_count) for block in own[1:]]
    bins = distogram_bias.shape[0] // PARTS
    bias = jnp.broadcast_to(distogram_bias.reshape(PARTS, bins, 1), (PARTS, bins, tile_cols))
    logits = turned(bias, own)
    for first, block in zip(firsts, mirror):
        logits = joined(logits, block, first)
    logits = logits.reshape(tile_rows, PARTS * bins, tile_cols)
    return jnp.swapaxes(logits, 1, 2)[None]


def solution(mesh):
    names = mesh.axis_names
    crops, rows, cols = (mesh.shape[name] for name in names)

    def run(pair, *parameters):
        crop_count, height, across, width = pair.shape
        tile_rows, tile_cols = height // rows, across // cols
        by_halves = (
            crop_count == crops
            and rows == cols == 4
            and tile_rows == tile_cols == LANES
            and width == LANES
        )
        if by_halves:
            halves = Mesh(mesh.devices.reshape(crops, 2, rows // 2, cols), ("crop", "half", "lo", "col"))
            spec, used, body = P("crop", ("half", "lo"), "col", None), halves, half_shards
        else:
            spec, used, body = P("crop", "row", "col", None), mesh, general_shards
        return jax.shard_map(
            body,
            mesh=used,
            in_specs=(spec,) + (P(),) * len(parameters),
            out_specs=spec,
            check_vma=False,
        )(pair, *parameters)

    return run
```

```python
import functools

import jax
import jax.numpy as jnp
from jax import lax
from jax.experimental import pallas as pl
from jax.experimental.pallas import tpu as pltpu
from jax.sharding import Mesh, PartitionSpec as P

HIGH = lax.Precision.HIGHEST
LANES = 128
GROUP = 8
STEP = 2
CHUNKS = (40, 56, 32)
LOWER = 40
PARTS = 4
VMEM = 56 * 1024 * 1024
SCALE = 8


def layer_norm(values, gain):
    center = values - jnp.mean(values, axis=-1, keepdims=True)
    spread = jnp.mean(center * center, axis=-1, keepdims=True)
    return center * lax.rsqrt(spread + 1e-05) * gain


def project(values, weights):
    return jnp.einsum("...c,cd->...d", values, weights, precision=HIGH)


def outgoing(left_hand, right_hand):
    return jnp.einsum("bikc,bjkc->bijc", left_hand, right_hand, precision=HIGH)


def mirrored(values):
    columns = lax.all_to_all(values, ("row", "col"), split_axis=2, concat_axis=1, tiled=True)
    return jnp.swapaxes(columns, 1, 2)


def general_shards(
    pair,
    gain_input,
    weights_in,
    gate_weights,
    weights_out,
    gain_product,
    gain_transition,
    transition_in,
    transition_out,
    distogram_weights,
    distogram_bias,
):
    row_count = lax.axis_size("row")
    col_count = lax.axis_size("col")
    crops, tile_rows, tile_cols, width = pair.shape
    normed = layer_norm(pair, gain_input)
    projected = project(normed, weights_in)
    left_hand = jax.nn.sigmoid(projected[..., width : 2 * width]) * projected[..., :width]
    right_hand = jax.nn.sigmoid(projected[..., 3 * width :]) * projected[..., 2 * width : 3 * width]
    stacked = jnp.stack([left_hand, right_hand], axis=0)
    received = lax.all_to_all(stacked, ("row", "col"), split_axis=4, concat_axis=2, tiled=True)
    items = received.shape[1]
    owned = received.shape[4]
    square = received.reshape(2, items, row_count, col_count, tile_rows, tile_cols, owned)
    square = square.transpose(0, 1, 2, 4, 3, 5, 6).reshape(
        2, items, row_count * tile_rows, col_count * tile_cols, owned
    )
    result = outgoing(square[0], square[1])
    product = lax.all_to_all(result, ("row", "col"), split_axis=1, concat_axis=3, tiled=True)
    base = lax.all_to_all(pair, "col", split_axis=1, concat_axis=2, tiled=True)
    normed_base = layer_norm(base, gain_input)
    gate = jax.nn.sigmoid(project(normed_base, gate_weights))
    updated = base + gate * project(layer_norm(product, gain_product), weights_out)
    hidden = project(layer_norm(updated, gain_transition), transition_in)
    hidden_width = transition_out.shape[0]
    activated = jax.nn.silu(hidden[..., :hidden_width]) * hidden[..., hidden_width:]
    pair_out = updated + project(activated, transition_out)
    symmetric = pair_out + mirrored(pair_out)
    line_logits = project(symmetric, distogram_weights) + distogram_bias
    return lax.all_to_all(line_logits, "col", split_axis=2, concat_axis=1, tiled=True)


def split_weights(weights, gain=None):
    if gain is not None:
        weights = gain[:, None] * weights
    flipped = weights.T
    high = lax.reduce_precision(flipped, 8, 7)
    low = flipped - high
    return jnp.concatenate([high, high, low], axis=1).astype(jnp.bfloat16)


def estimate(flops, moved):
    return pl.CostEstimate(flops=flops // SCALE, bytes_accessed=moved // SCALE, transcendentals=0)


def parts(values):
    high = values.astype(jnp.bfloat16)
    low = (values - high.astype(jnp.float32)).astype(jnp.bfloat16)
    return high, low


def times(weights3, values):
    high, low = parts(values)
    return jnp.dot(
        weights3, jnp.concatenate([high, low, high], axis=0), preferred_element_type=jnp.float32
    )


def normalized(values):
    center = values - jnp.mean(values, axis=0, keepdims=True)
    spread = jnp.mean(center * center, axis=0, keepdims=True)
    return center * lax.rsqrt(spread + 1e-05)


def hands_kernel(pair_ref, weights_ref, out_ref):
    rows, _, width = pair_ref.shape
    per = 4
    flat = out_ref.reshape(width * rows, LANES)
    for start in range(0, rows, per):
        values = jnp.concatenate([pair_ref[start + n].T for n in range(per)], axis=1)
        projected = times(weights_ref[...], normalized(values))
        result = jax.nn.sigmoid(projected[width:]) * projected[:width]
        for n in range(per):
            flat[pl.ds(start + n, width, stride=rows), :] = result[:, n * LANES : (n + 1) * LANES]


def hands(pair, weights3, left, right):
    _, tile_cols, width = pair.shape
    rows = left[1] + right[1]
    turn = left[1] // GROUP
    lead, shift = left[0] // GROUP, right[0] // GROUP - turn
    return pl.pallas_call(
        hands_kernel,
        grid=(rows // GROUP,),
        in_specs=[
            pl.BlockSpec((GROUP, tile_cols, width), lambda g: (g + jnp.where(g < turn, lead, shift), 0, 0)),
            pl.BlockSpec((2 * width, 3 * width), lambda g: (jnp.where(g < turn, 0, 1), 0)),
        ],
        out_specs=pl.BlockSpec((width, GROUP, tile_cols), lambda g: (0, g, 0)),
        out_shape=jax.ShapeDtypeStruct((width, rows, tile_cols), jnp.float32),
        compiler_params=pltpu.CompilerParams(vmem_limit_bytes=VMEM),
        cost_estimate=estimate(6 * rows * tile_cols * width * 2 * width, 8 * rows * tile_cols * width),
        name="hands",
    )(pair, weights3)


def product_kernel(half_ref, low_ref, high_ref, own_ref, other_ref, out_ref):
    cols = own_ref.shape[0] // 2
    half = half_ref[0]
    rows = own_ref.shape[2]
    for n in range(own_ref.shape[1]):

        def line(ref, lo):
            return jnp.concatenate([ref[lo * cols + c, n] for c in range(cols)], axis=1)

        left_high, left_low = parts(
            jnp.concatenate(
                [line(ref, lo) for lo in range(2) for ref in (low_ref, high_ref)], axis=0
            )
        )
        right_high, right_low = parts(
            jnp.concatenate(
                [line(ref, lo) for ref in (own_ref, other_ref) for lo in range(2)], axis=0
            )
        )
        result = lax.dot_general(
            jnp.concatenate([right_high, right_high, right_low], axis=1),
            jnp.concatenate([left_high, left_low, left_high], axis=1),
            (((1,), (1,)), ((), ())),
            preferred_element_type=jnp.float32,
        )
        wide = result.shape[1] // 2
        for lo in range(2):
            for piece in range(cols):
                source, other_lo = divmod(piece, 2)
                plane = 2 * jnp.where(half == source, 0, 1) + other_lo
                out_ref[lo * cols + plane, n] = result[
                    piece * rows : (piece + 1) * rows, lo * wide : (lo + 1) * wide
                ]


def product(half, low, high, own, other, wide):
    sources, owned, rows, width = own.shape
    k_all = width * sources // 2
    spec_out = pl.BlockSpec((sources, STEP, rows, wide), lambda n, half: (0, n, 0, 0))
    spec = lambda height: pl.BlockSpec(
        (sources, STEP, height, width), lambda n, half: (0, n, 0, 0)
    )
    return pl.pallas_call(
        product_kernel,
        grid_spec=pltpu.PrefetchScalarGridSpec(
            num_scalar_prefetch=1,
            grid=(owned // STEP,),
            in_specs=[spec(LOWER), spec(wide - LOWER), spec(rows), spec(rows)],
            out_specs=spec_out,
        ),
        out_shape=jax.ShapeDtypeStruct((sources, owned, rows, wide), jnp.float32),
        compiler_params=pltpu.CompilerParams(vmem_limit_bytes=VMEM),
        cost_estimate=estimate(
            6 * owned * 4 * rows * 2 * wide * k_all, 4 * owned * k_all * (2 * wide + 4 * rows)
        ),
        name="product",
    )(half, low, high, own, other)


def head_kernel(
    pair_ref, product_ref, gate_ref, output_ref, up_ref, down_ref, bins_ref, *out_refs
):
    tile_rows, cols, width = pair_ref.shape
    bins = out_refs[0].shape[1]
    per = 4
    flat_pair = pair_ref.reshape(tile_rows * cols, width)
    flat_product = product_ref.reshape(width * cols, tile_rows)
    hidden_width = up_ref.shape[0] // 2
    for start in range(0, cols, per):
        values = jnp.concatenate(
            [flat_pair[pl.ds(start + n, tile_rows, stride=cols), :].T for n in range(per)], axis=1
        )
        product_values = jnp.concatenate(
            [flat_product[pl.ds(start + n, width, stride=cols), :] for n in range(per)], axis=1
        )
        gate = jax.nn.sigmoid(times(gate_ref[...], normalized(values)))
        updated = values + gate * times(output_ref[...], normalized(product_values))
        hidden = times(up_ref[...], normalized(updated))
        activated = jax.nn.silu(hidden[:hidden_width]) * hidden[hidden_width:]
        pair_out = updated + times(down_ref[...], activated)
        logits = times(bins_ref[...], pair_out)
        for n in range(per):
            for part, out_ref in enumerate(out_refs):
                out_ref[start + n] = logits[
                    part * bins : (part + 1) * bins, n * tile_rows : (n + 1) * tile_rows
                ]


def head(pair, product_values, first, gate3, output3, up3, down3, bins3):
    tile_rows, tile_cols, width = pair.shape
    chunk_cols = product_values.shape[1]
    steps = chunk_cols // GROUP
    lead = first // GROUP
    bins = bins3.shape[0] // PARTS
    whole = lambda array: pl.BlockSpec(array.shape, lambda g: (0, 0))
    macs = gate3.size + output3.size + up3.size + down3.size + bins3.size
    return pl.pallas_call(
        head_kernel,
        grid=(steps,),
        in_specs=[
            pl.BlockSpec((tile_rows, GROUP, width), lambda g: (0, lead + g, 0)),
            pl.BlockSpec((width, GROUP, tile_rows), lambda g: (0, g, 0)),
            whole(gate3),
            whole(output3),
            whole(up3),
            whole(down3),
            whole(bins3),
        ],
        out_specs=[pl.BlockSpec((GROUP, bins, tile_rows), lambda g: (g, 0, 0))] * PARTS,
        out_shape=[jax.ShapeDtypeStruct((chunk_cols, bins, tile_rows), jnp.float32)] * PARTS,
        compiler_params=pltpu.CompilerParams(vmem_limit_bytes=VMEM),
        cost_estimate=estimate(
            2 * chunk_cols * tile_rows * macs, 4 * chunk_cols * tile_rows * (2 * width + PARTS * bins)
        ),
        name="head",
    )(pair, product_values, gate3, output3, up3, down3, bins3)


def turned_kernel(bias_ref, *refs):
    out_ref, sources = refs[-1], refs[:-1]
    count = len(sources) // PARTS
    tile_rows, _, bins, tile_cols = out_ref.shape
    flat = out_ref.reshape(tile_rows * PARTS * bins, tile_cols)
    for part in range(PARTS):
        for n in range(bins):
            values = [
                ref.reshape(ref.shape[0] * bins, tile_rows)[pl.ds(n, ref.shape[0], stride=bins), :]
                for ref in sources[part * count : (part + 1) * count]
            ]
            result = jnp.concatenate(values, axis=0).T + bias_ref[part, n : n + 1, :]
            flat[pl.ds(part * bins + n, tile_rows, stride=PARTS * bins), :] = result


def turned(bias, own):
    arrays = [block[part] for part in range(PARTS) for block in own]
    _, bins, tile_rows = arrays[0].shape
    tile_cols = sum(block[0].shape[0] for block in own)
    block = lambda rows: pl.BlockSpec((rows, GROUP, tile_rows), lambda g: (0, g, 0))
    return pl.pallas_call(
        turned_kernel,
        grid=(bins // GROUP,),
        in_specs=[pl.BlockSpec((PARTS, GROUP, tile_cols), lambda g: (0, g, 0))]
        + [block(array.shape[0]) for array in arrays],
        out_specs=pl.BlockSpec((tile_rows, PARTS, GROUP, tile_cols), lambda g: (0, 0, g, 0)),
        out_shape=jax.ShapeDtypeStruct((tile_rows, PARTS, bins, tile_cols), jnp.float32),
        compiler_params=pltpu.CompilerParams(vmem_limit_bytes=VMEM),
        cost_estimate=estimate(0, 8 * tile_rows * PARTS * bins * tile_cols),
        name="turned",
    )(bias, *arrays)


def joined_kernel(base_ref, *refs):
    out_ref = refs[-1]
    for part, ref in enumerate(refs[:-1]):
        out_ref[:, part] = base_ref[:, part] + ref[...]


def joined(base, mirror, first):
    rows, bins, tile_cols = mirror[0].shape
    lead = first // GROUP
    whole = pl.BlockSpec((GROUP, PARTS, bins, tile_cols), lambda g: (lead + g, 0, 0, 0))
    block = pl.BlockSpec((GROUP, bins, tile_cols), lambda g: (g, 0, 0))
    return pl.pallas_call(
        joined_kernel,
        grid=(rows // GROUP,),
        in_specs=[whole] + [block] * PARTS,
        out_specs=whole,
        out_shape=jax.ShapeDtypeStruct(base.shape, jnp.float32),
        input_output_aliases={0: 0},
        compiler_params=pltpu.CompilerParams(vmem_limit_bytes=VMEM),
        cost_estimate=estimate(0, 12 * PARTS * rows * bins * tile_cols),
        name="joined",
    )(base, *mirror)


def move(values, count, target):
    every = [(r, c) for r in range(count) for c in range(count)]
    pairs = [(r * count + c, target(r, c)) for r, c in every]
    return lax.ppermute(values, ("half", "lo", "col"), pairs)


def aside(block, count):
    return [block[0]] + [
        move(block[n], count, lambda r, c: r * count + (c ^ n)) for n in range(1, len(block))
    ]


def across(shifted, count):
    return [
        move(values, count, lambda r, c: (c ^ n) * count + r) for n, values in enumerate(shifted)
    ]


def half_shards(
    pair,
    gain_input,
    weights_in,
    gate_weights,
    weights_out,
    gain_product,
    gain_transition,
    transition_in,
    transition_out,
    distogram_weights,
    distogram_bias,
):
    row_count = 2 * lax.axis_size("lo")
    col_count = lax.axis_size("col")
    _, tile_rows, tile_cols, width = pair.shape
    tile = pair[0]
    in3 = split_weights(weights_in, gain_input)
    gate3 = split_weights(gate_weights, gain_input)
    output3 = split_weights(weights_out, gain_product)
    up3 = split_weights(transition_in, gain_transition)
    down3 = split_weights(transition_out)
    bins3 = split_weights(distogram_weights)
    sources = 2 * col_count
    owned = width // sources

    def spread(values):
        values = values.reshape(sources, owned, *values.shape[1:])
        return lax.all_to_all(values, ("lo", "col"), split_axis=0, concat_axis=0, tiled=True)

    tie = lax.optimization_barrier
    half = lax.axis_index("half").astype(jnp.int32).reshape(1)
    firsts = [sum(CHUNKS[:n]) for n in range(len(CHUNKS))]
    upper = tile_rows - LOWER

    def exchange(values):
        return lax.ppermute(values, "half", [(0, 1), (1, 0)])

    def delivered(values):
        values = lax.all_to_all(values, ("lo", "col"), split_axis=0, concat_axis=0, tiled=True)
        return values.reshape(width, values.shape[2], tile_rows)

    def run_head(values, chunk):
        return head(tile, values, firsts[chunk], gate3, output3, up3, down3, bins3)

    right = spread(hands(tile, in3, (0, 0), (firsts[0], CHUNKS[0])))
    rights, others = [right], [exchange(right)]
    low = spread(hands(tile, in3, (0, LOWER), (firsts[1], CHUNKS[1])))
    rights.append(low[:, :, LOWER:])
    others.append(exchange(rights[1]))
    sent = hands(tile, in3, (LOWER, upper), (firsts[2], CHUNKS[2]))
    sent, others[0] = tie((sent, others[0]))
    high = spread(sent)
    rights.append(high[:, :, upper:])
    others.append(exchange(rights[2]))

    def blocks(chunk):
        return product(half, low, high, rights[chunk], others[chunk], tile_rows)

    values, others[1] = tie((blocks(0), others[1]))
    own = [run_head(delivered(values), 0)]
    shifted = aside(own[0], row_count)
    values, others[2], shifted = tie((blocks(1), others[2], shifted))
    mirror = [across(shifted, row_count)]
    values, after = tie((delivered(values), blocks(2)))
    own.append(run_head(values, 1))
    values, mirror[0] = tie((delivered(after), mirror[0]))
    own.append(run_head(values, 2))
    mirror.append(across(aside(own[1], row_count), row_count))
    shifted = aside(own[2], row_count)
    bins = distogram_bias.shape[0] // PARTS
    bias = jnp.broadcast_to(distogram_bias.reshape(PARTS, bins, 1), (PARTS, bins, tile_cols))
    logits = joined(turned(bias, own), mirror[0], firsts[0])
    logits, shifted[1:] = tie((logits, shifted[1:]))
    mirror.append(across(shifted, row_count))
    for first, block in zip(firsts[1:], mirror[1:]):
        logits = joined(logits, block, first)
    logits = logits.reshape(tile_rows, PARTS * bins, tile_cols)
    return jnp.swapaxes(logits, 1, 2)[None]


def solution(mesh):
    names = mesh.axis_names
    crops, rows, cols = (mesh.shape[name] for name in names)

    def run(pair, *parameters):
        crop_count, height, across, width = pair.shape
        tile_rows, tile_cols = height // rows, across // cols
        by_halves = (
            crop_count == crops
            and rows == cols == 4
            and tile_rows == tile_cols == LANES
            and width == LANES
        )
        if by_halves:
            halves = Mesh(mesh.devices.reshape(crops, 2, rows // 2, cols), ("crop", "half", "lo", "col"))
            spec, used, body = P("crop", ("half", "lo"), "col", None), halves, half_shards
        else:
            spec, used, body = P("crop", "row", "col", None), mesh, general_shards
        return jax.shard_map(
            body,
            mesh=used,
            in_specs=(spec,) + (P(),) * len(parameters),
            out_specs=spec,
            check_vma=False,
        )(pair, *parameters)

    return run
```

```python
import functools

import jax
import jax.numpy as jnp
from jax import lax
from jax.experimental import pallas as pl
from jax.experimental.pallas import tpu as pltpu
from jax.sharding import Mesh, PartitionSpec as P

HIGH = lax.Precision.HIGHEST
LANES = 128
GROUP = 8
STEP = 2
CHUNKS = (48, 56, 24)
LOWER = 40
PARTS = 4
VMEM = 56 * 1024 * 1024
SCALE = 8


def layer_norm(values, gain):
    center = values - jnp.mean(values, axis=-1, keepdims=True)
    spread = jnp.mean(center * center, axis=-1, keepdims=True)
    return center * lax.rsqrt(spread + 1e-05) * gain


def project(values, weights):
    return jnp.einsum("...c,cd->...d", values, weights, precision=HIGH)


def outgoing(left_hand, right_hand):
    return jnp.einsum("bikc,bjkc->bijc", left_hand, right_hand, precision=HIGH)


def mirrored(values):
    columns = lax.all_to_all(values, ("row", "col"), split_axis=2, concat_axis=1, tiled=True)
    return jnp.swapaxes(columns, 1, 2)


def general_shards(
    pair,
    gain_input,
    weights_in,
    gate_weights,
    weights_out,
    gain_product,
    gain_transition,
    transition_in,
    transition_out,
    distogram_weights,
    distogram_bias,
):
    row_count = lax.axis_size("row")
    col_count = lax.axis_size("col")
    crops, tile_rows, tile_cols, width = pair.shape
    normed = layer_norm(pair, gain_input)
    projected = project(normed, weights_in)
    left_hand = jax.nn.sigmoid(projected[..., width : 2 * width]) * projected[..., :width]
    right_hand = jax.nn.sigmoid(projected[..., 3 * width :]) * projected[..., 2 * width : 3 * width]
    stacked = jnp.stack([left_hand, right_hand], axis=0)
    received = lax.all_to_all(stacked, ("row", "col"), split_axis=4, concat_axis=2, tiled=True)
    items = received.shape[1]
    owned = received.shape[4]
    square = received.reshape(2, items, row_count, col_count, tile_rows, tile_cols, owned)
    square = square.transpose(0, 1, 2, 4, 3, 5, 6).reshape(
        2, items, row_count * tile_rows, col_count * tile_cols, owned
    )
    result = outgoing(square[0], square[1])
    product = lax.all_to_all(result, ("row", "col"), split_axis=1, concat_axis=3, tiled=True)
    base = lax.all_to_all(pair, "col", split_axis=1, concat_axis=2, tiled=True)
    normed_base = layer_norm(base, gain_input)
    gate = jax.nn.sigmoid(project(normed_base, gate_weights))
    updated = base + gate * project(layer_norm(product, gain_product), weights_out)
    hidden = project(layer_norm(updated, gain_transition), transition_in)
    hidden_width = transition_out.shape[0]
    activated = jax.nn.silu(hidden[..., :hidden_width]) * hidden[..., hidden_width:]
    pair_out = updated + project(activated, transition_out)
    symmetric = pair_out + mirrored(pair_out)
    line_logits = project(symmetric, distogram_weights) + distogram_bias
    return lax.all_to_all(line_logits, "col", split_axis=2, concat_axis=1, tiled=True)


def split_weights(weights, gain=None):
    if gain is not None:
        weights = gain[:, None] * weights
    flipped = weights.T
    high = lax.reduce_precision(flipped, 8, 7)
    low = flipped - high
    return jnp.concatenate([high, high, low], axis=1).astype(jnp.bfloat16)


def estimate(flops, moved):
    return pl.CostEstimate(flops=flops // SCALE, bytes_accessed=moved // SCALE, transcendentals=0)


def parts(values):
    high = values.astype(jnp.bfloat16)
    low = (values - high.astype(jnp.float32)).astype(jnp.bfloat16)
    return high, low


def times(weights3, values):
    high, low = parts(values)
    return jnp.dot(
        weights3, jnp.concatenate([high, low, high], axis=0), preferred_element_type=jnp.float32
    )


def normalized(values):
    center = values - jnp.mean(values, axis=0, keepdims=True)
    spread = jnp.mean(center * center, axis=0, keepdims=True)
    return center * lax.rsqrt(spread + 1e-05)


def hands_kernel(pair_ref, weights_ref, out_ref):
    rows, _, width = pair_ref.shape
    per = 4
    flat = out_ref.reshape(width * rows, LANES)
    for start in range(0, rows, per):
        values = jnp.concatenate([pair_ref[start + n].T for n in range(per)], axis=1)
        projected = times(weights_ref[...], normalized(values))
        result = jax.nn.sigmoid(projected[width:]) * projected[:width]
        for n in range(per):
            flat[pl.ds(start + n, width, stride=rows), :] = result[:, n * LANES : (n + 1) * LANES]


def hands(pair, weights3, left, right):
    _, tile_cols, width = pair.shape
    rows = left[1] + right[1]
    turn = left[1] // GROUP
    lead, shift = left[0] // GROUP, right[0] // GROUP - turn
    return pl.pallas_call(
        hands_kernel,
        grid=(rows // GROUP,),
        in_specs=[
            pl.BlockSpec((GROUP, tile_cols, width), lambda g: (g + jnp.where(g < turn, lead, shift), 0, 0)),
            pl.BlockSpec((2 * width, 3 * width), lambda g: (jnp.where(g < turn, 0, 1), 0)),
        ],
        out_specs=pl.BlockSpec((width, GROUP, tile_cols), lambda g: (0, g, 0)),
        out_shape=jax.ShapeDtypeStruct((width, rows, tile_cols), jnp.float32),
        compiler_params=pltpu.CompilerParams(vmem_limit_bytes=VMEM),
        cost_estimate=estimate(6 * rows * tile_cols * width * 2 * width, 8 * rows * tile_cols * width),
        name="hands",
    )(pair, weights3)


def product_kernel(half_ref, low_ref, high_ref, own_ref, other_ref, out_ref):
    cols = own_ref.shape[0] // 2
    half = half_ref[0]
    rows = own_ref.shape[2]
    for n in range(own_ref.shape[1]):

        def line(ref, lo):
            return jnp.concatenate([ref[lo * cols + c, n] for c in range(cols)], axis=1)

        left_high, left_low = parts(
            jnp.concatenate(
                [line(ref, lo) for lo in range(2) for ref in (low_ref, high_ref)], axis=0
            )
        )
        right_high, right_low = parts(
            jnp.concatenate(
                [line(ref, lo) for ref in (own_ref, other_ref) for lo in range(2)], axis=0
            )
        )
        result = lax.dot_general(
            jnp.concatenate([right_high, right_high, right_low], axis=1),
            jnp.concatenate([left_high, left_low, left_high], axis=1),
            (((1,), (1,)), ((), ())),
            preferred_element_type=jnp.float32,
        )
        wide = result.shape[1] // 2
        for lo in range(2):
            for piece in range(cols):
                source, other_lo = divmod(piece, 2)
                plane = 2 * jnp.where(half == source, 0, 1) + other_lo
                out_ref[lo * cols + plane, n] = result[
                    piece * rows : (piece + 1) * rows, lo * wide : (lo + 1) * wide
                ]


def product(half, low, high, own, other, wide):
    sources, owned, rows, width = own.shape
    k_all = width * sources // 2
    spec_out = pl.BlockSpec((sources, STEP, rows, wide), lambda n, half: (0, n, 0, 0))
    spec = lambda height: pl.BlockSpec(
        (sources, STEP, height, width), lambda n, half: (0, n, 0, 0)
    )
    return pl.pallas_call(
        product_kernel,
        grid_spec=pltpu.PrefetchScalarGridSpec(
            num_scalar_prefetch=1,
            grid=(owned // STEP,),
            in_specs=[spec(LOWER), spec(wide - LOWER), spec(rows), spec(rows)],
            out_specs=spec_out,
        ),
        out_shape=jax.ShapeDtypeStruct((sources, owned, rows, wide), jnp.float32),
        compiler_params=pltpu.CompilerParams(vmem_limit_bytes=VMEM),
        cost_estimate=estimate(
            6 * owned * 4 * rows * 2 * wide * k_all, 4 * owned * k_all * (2 * wide + 4 * rows)
        ),
        name="product",
    )(half, low, high, own, other)


def head_kernel(
    pair_ref, product_ref, gate_ref, output_ref, up_ref, down_ref, bins_ref, *out_refs
):
    tile_rows, cols, width = pair_ref.shape
    bins = out_refs[0].shape[1]
    per = 4
    flat_pair = pair_ref.reshape(tile_rows * cols, width)
    flat_product = product_ref.reshape(width * cols, tile_rows)
    hidden_width = up_ref.shape[0] // 2
    for start in range(0, cols, per):
        values = jnp.concatenate(
            [flat_pair[pl.ds(start + n, tile_rows, stride=cols), :].T for n in range(per)], axis=1
        )
        product_values = jnp.concatenate(
            [flat_product[pl.ds(start + n, width, stride=cols), :] for n in range(per)], axis=1
        )
        gate = jax.nn.sigmoid(times(gate_ref[...], normalized(values)))
        updated = values + gate * times(output_ref[...], normalized(product_values))
        hidden = times(up_ref[...], normalized(updated))
        activated = jax.nn.silu(hidden[:hidden_width]) * hidden[hidden_width:]
        pair_out = updated + times(down_ref[...], activated)
        logits = times(bins_ref[...], pair_out)
        for n in range(per):
            for part, out_ref in enumerate(out_refs):
                out_ref[start + n] = logits[
                    part * bins : (part + 1) * bins, n * tile_rows : (n + 1) * tile_rows
                ]


def head(pair, product_values, first, gate3, output3, up3, down3, bins3):
    tile_rows, tile_cols, width = pair.shape
    chunk_cols = product_values.shape[1]
    steps = chunk_cols // GROUP
    lead = first // GROUP
    bins = bins3.shape[0] // PARTS
    whole = lambda array: pl.BlockSpec(array.shape, lambda g: (0, 0))
    macs = gate3.size + output3.size + up3.size + down3.size + bins3.size
    return pl.pallas_call(
        head_kernel,
        grid=(steps,),
        in_specs=[
            pl.BlockSpec((tile_rows, GROUP, width), lambda g: (0, lead + g, 0)),
            pl.BlockSpec((width, GROUP, tile_rows), lambda g: (0, g, 0)),
            whole(gate3),
            whole(output3),
            whole(up3),
            whole(down3),
            whole(bins3),
        ],
        out_specs=[pl.BlockSpec((GROUP, bins, tile_rows), lambda g: (g, 0, 0))] * PARTS,
        out_shape=[jax.ShapeDtypeStruct((chunk_cols, bins, tile_rows), jnp.float32)] * PARTS,
        compiler_params=pltpu.CompilerParams(vmem_limit_bytes=VMEM),
        cost_estimate=estimate(
            2 * chunk_cols * tile_rows * macs, 4 * chunk_cols * tile_rows * (2 * width + PARTS * bins)
        ),
        name="head",
    )(pair, product_values, gate3, output3, up3, down3, bins3)


def turned_kernel(bias_ref, *refs):
    out_ref, sources = refs[-1], refs[:-1]
    count = len(sources) // PARTS
    tile_rows, _, bins, tile_cols = out_ref.shape
    flat = out_ref.reshape(tile_rows * PARTS * bins, tile_cols)
    for part in range(PARTS):
        for n in range(bins):
            values = [
                ref.reshape(ref.shape[0] * bins, tile_rows)[pl.ds(n, ref.shape[0], stride=bins), :]
                for ref in sources[part * count : (part + 1) * count]
            ]
            result = jnp.concatenate(values, axis=0).T + bias_ref[part, n : n + 1, :]
            flat[pl.ds(part * bins + n, tile_rows, stride=PARTS * bins), :] = result


def turned(bias, own):
    arrays = [block[part] for part in range(PARTS) for block in own]
    _, bins, tile_rows = arrays[0].shape
    tile_cols = sum(block[0].shape[0] for block in own)
    block = lambda rows: pl.BlockSpec((rows, GROUP, tile_rows), lambda g: (0, g, 0))
    return pl.pallas_call(
        turned_kernel,
        grid=(bins // GROUP,),
        in_specs=[pl.BlockSpec((PARTS, GROUP, tile_cols), lambda g: (0, g, 0))]
        + [block(array.shape[0]) for array in arrays],
        out_specs=pl.BlockSpec((tile_rows, PARTS, GROUP, tile_cols), lambda g: (0, 0, g, 0)),
        out_shape=jax.ShapeDtypeStruct((tile_rows, PARTS, bins, tile_cols), jnp.float32),
        compiler_params=pltpu.CompilerParams(vmem_limit_bytes=VMEM),
        cost_estimate=estimate(0, 8 * tile_rows * PARTS * bins * tile_cols),
        name="turned",
    )(bias, *arrays)


def joined_kernel(base_ref, *refs):
    out_ref = refs[-1]
    for part, ref in enumerate(refs[:-1]):
        out_ref[:, part] = base_ref[:, part] + ref[...]


def joined(base, mirror, first):
    rows, bins, tile_cols = mirror[0].shape
    lead = first // GROUP
    whole = pl.BlockSpec((GROUP, PARTS, bins, tile_cols), lambda g: (lead + g, 0, 0, 0))
    block = pl.BlockSpec((GROUP, bins, tile_cols), lambda g: (g, 0, 0))
    return pl.pallas_call(
        joined_kernel,
        grid=(rows // GROUP,),
        in_specs=[whole] + [block] * PARTS,
        out_specs=whole,
        out_shape=jax.ShapeDtypeStruct(base.shape, jnp.float32),
        input_output_aliases={0: 0},
        compiler_params=pltpu.CompilerParams(vmem_limit_bytes=VMEM),
        cost_estimate=estimate(0, 12 * PARTS * rows * bins * tile_cols),
        name="joined",
    )(base, *mirror)


def move(values, count, target):
    every = [(r, c) for r in range(count) for c in range(count)]
    pairs = [(r * count + c, target(r, c)) for r, c in every]
    return lax.ppermute(values, ("half", "lo", "col"), pairs)


def aside(block, count):
    return [block[0]] + [
        move(block[n], count, lambda r, c: r * count + (c ^ n)) for n in range(1, len(block))
    ]


def across(shifted, count):
    return [
        move(values, count, lambda r, c: (c ^ n) * count + r) for n, values in enumerate(shifted)
    ]


def half_shards(
    pair,
    gain_input,
    weights_in,
    gate_weights,
    weights_out,
    gain_product,
    gain_transition,
    transition_in,
    transition_out,
    distogram_weights,
    distogram_bias,
):
    row_count = 2 * lax.axis_size("lo")
    col_count = lax.axis_size("col")
    _, tile_rows, tile_cols, width = pair.shape
    tile = pair[0]
    in3 = split_weights(weights_in, gain_input)
    gate3 = split_weights(gate_weights, gain_input)
    output3 = split_weights(weights_out, gain_product)
    up3 = split_weights(transition_in, gain_transition)
    down3 = split_weights(transition_out)
    bins3 = split_weights(distogram_weights)
    sources = 2 * col_count
    owned = width // sources

    def spread(values):
        values = values.reshape(sources, owned, *values.shape[1:])
        return lax.all_to_all(values, ("lo", "col"), split_axis=0, concat_axis=0, tiled=True)

    tie = lax.optimization_barrier
    half = lax.axis_index("half").astype(jnp.int32).reshape(1)
    firsts = [sum(CHUNKS[:n]) for n in range(len(CHUNKS))]
    upper = tile_rows - LOWER

    def exchange(values):
        return lax.ppermute(values, "half", [(0, 1), (1, 0)])

    def delivered(values):
        values = lax.all_to_all(values, ("lo", "col"), split_axis=0, concat_axis=0, tiled=True)
        return values.reshape(width, values.shape[2], tile_rows)

    def run_head(values, chunk):
        return head(tile, values, firsts[chunk], gate3, output3, up3, down3, bins3)

    right = spread(hands(tile, in3, (0, 0), (firsts[0], CHUNKS[0])))
    rights, others = [right], [exchange(right)]
    low = spread(hands(tile, in3, (0, LOWER), (firsts[1], CHUNKS[1])))
    rights.append(low[:, :, LOWER:])
    others.append(exchange(rights[1]))
    sent = hands(tile, in3, (LOWER, upper), (firsts[2], CHUNKS[2]))
    sent, others[0] = tie((sent, others[0]))
    high = spread(sent)
    rights.append(high[:, :, upper:])
    others.append(exchange(rights[2]))

    def blocks(chunk):
        return product(half, low, high, rights[chunk], others[chunk], tile_rows)

    values, others[1] = tie((blocks(0), others[1]))
    own = [run_head(delivered(values), 0)]
    shifted = aside(own[0], row_count)
    values, others[2], shifted = tie((blocks(1), others[2], shifted))
    mirror = [across(shifted, row_count)]
    values, after = tie((delivered(values), blocks(2)))
    own.append(run_head(values, 1))
    values, mirror[0] = tie((delivered(after), mirror[0]))
    own.append(run_head(values, 2))
    mirror.append(across(aside(own[1], row_count), row_count))
    shifted = aside(own[2], row_count)
    bins = distogram_bias.shape[0] // PARTS
    bias = jnp.broadcast_to(distogram_bias.reshape(PARTS, bins, 1), (PARTS, bins, tile_cols))
    logits = joined(turned(bias, own), mirror[0], firsts[0])
    logits, shifted[1:] = tie((logits, shifted[1:]))
    mirror.append(across(shifted, row_count))
    for first, block in zip(firsts[1:], mirror[1:]):
        logits = joined(logits, block, first)
    logits = logits.reshape(tile_rows, PARTS * bins, tile_cols)
    return jnp.swapaxes(logits, 1, 2)[None]


def solution(mesh):
    names = mesh.axis_names
    crops, rows, cols = (mesh.shape[name] for name in names)

    def run(pair, *parameters):
        crop_count, height, across, width = pair.shape
        tile_rows, tile_cols = height // rows, across // cols
        by_halves = (
            crop_count == crops
            and rows == cols == 4
            and tile_rows == tile_cols == LANES
            and width == LANES
        )
        if by_halves:
            halves = Mesh(mesh.devices.reshape(crops, 2, rows // 2, cols), ("crop", "half", "lo", "col"))
            spec, used, body = P("crop", ("half", "lo"), "col", None), halves, half_shards
        else:
            spec, used, body = P("crop", "row", "col", None), mesh, general_shards
        return jax.shard_map(
            body,
            mesh=used,
            in_specs=(spec,) + (P(),) * len(parameters),
            out_specs=spec,
            check_vma=False,
        )(pair, *parameters)

    return run
```

```python
import functools

import jax
import jax.numpy as jnp
from jax import lax
from jax.experimental import pallas as pl
from jax.experimental.pallas import tpu as pltpu
from jax.sharding import Mesh, PartitionSpec as P

HIGH = lax.Precision.HIGHEST
LANES = 128
GROUP = 8
STEP = 2
CHUNKS = (40, 56, 32)
LOWER = 40
PARTS = 4
VMEM = 56 * 1024 * 1024
SCALE = 8


def layer_norm(values, gain):
    center = values - jnp.mean(values, axis=-1, keepdims=True)
    spread = jnp.mean(center * center, axis=-1, keepdims=True)
    return center * lax.rsqrt(spread + 1e-05) * gain


def project(values, weights):
    return jnp.einsum("...c,cd->...d", values, weights, precision=HIGH)


def outgoing(left_hand, right_hand):
    return jnp.einsum("bikc,bjkc->bijc", left_hand, right_hand, precision=HIGH)


def mirrored(values):
    columns = lax.all_to_all(values, ("row", "col"), split_axis=2, concat_axis=1, tiled=True)
    return jnp.swapaxes(columns, 1, 2)


def general_shards(
    pair,
    gain_input,
    weights_in,
    gate_weights,
    weights_out,
    gain_product,
    gain_transition,
    transition_in,
    transition_out,
    distogram_weights,
    distogram_bias,
):
    row_count = lax.axis_size("row")
    col_count = lax.axis_size("col")
    crops, tile_rows, tile_cols, width = pair.shape
    normed = layer_norm(pair, gain_input)
    projected = project(normed, weights_in)
    left_hand = jax.nn.sigmoid(projected[..., width : 2 * width]) * projected[..., :width]
    right_hand = jax.nn.sigmoid(projected[..., 3 * width :]) * projected[..., 2 * width : 3 * width]
    stacked = jnp.stack([left_hand, right_hand], axis=0)
    received = lax.all_to_all(stacked, ("row", "col"), split_axis=4, concat_axis=2, tiled=True)
    items = received.shape[1]
    owned = received.shape[4]
    square = received.reshape(2, items, row_count, col_count, tile_rows, tile_cols, owned)
    square = square.transpose(0, 1, 2, 4, 3, 5, 6).reshape(
        2, items, row_count * tile_rows, col_count * tile_cols, owned
    )
    result = outgoing(square[0], square[1])
    product = lax.all_to_all(result, ("row", "col"), split_axis=1, concat_axis=3, tiled=True)
    base = lax.all_to_all(pair, "col", split_axis=1, concat_axis=2, tiled=True)
    normed_base = layer_norm(base, gain_input)
    gate = jax.nn.sigmoid(project(normed_base, gate_weights))
    updated = base + gate * project(layer_norm(product, gain_product), weights_out)
    hidden = project(layer_norm(updated, gain_transition), transition_in)
    hidden_width = transition_out.shape[0]
    activated = jax.nn.silu(hidden[..., :hidden_width]) * hidden[..., hidden_width:]
    pair_out = updated + project(activated, transition_out)
    symmetric = pair_out + mirrored(pair_out)
    line_logits = project(symmetric, distogram_weights) + distogram_bias
    return lax.all_to_all(line_logits, "col", split_axis=2, concat_axis=1, tiled=True)


def split_weights(weights, gain=None):
    if gain is not None:
        weights = gain[:, None] * weights
    flipped = weights.T
    high = lax.reduce_precision(flipped, 8, 7)
    low = flipped - high
    return jnp.concatenate([high, high, low], axis=1).astype(jnp.bfloat16)


def estimate(flops, moved):
    return pl.CostEstimate(flops=flops // SCALE, bytes_accessed=moved // SCALE, transcendentals=0)


def parts(values):
    high = values.astype(jnp.bfloat16)
    low = (values - high.astype(jnp.float32)).astype(jnp.bfloat16)
    return high, low


def times(weights3, values):
    high, low = parts(values)
    return jnp.dot(
        weights3, jnp.concatenate([high, low, high], axis=0), preferred_element_type=jnp.float32
    )


def normalized(values):
    center = values - jnp.mean(values, axis=0, keepdims=True)
    spread = jnp.mean(center * center, axis=0, keepdims=True)
    return center * lax.rsqrt(spread + 1e-05)


def hands_kernel(pair_ref, weights_ref, out_ref):
    rows, _, width = pair_ref.shape
    per = 4
    flat = out_ref.reshape(width * rows, LANES)
    for start in range(0, rows, per):
        values = jnp.concatenate([pair_ref[start + n].T for n in range(per)], axis=1)
        projected = times(weights_ref[...], normalized(values))
        result = jax.nn.sigmoid(projected[width:]) * projected[:width]
        for n in range(per):
            flat[pl.ds(start + n, width, stride=rows), :] = result[:, n * LANES : (n + 1) * LANES]


def hands(pair, weights3, left, right):
    _, tile_cols, width = pair.shape
    rows = left[1] + right[1]
    turn = left[1] // GROUP
    lead, shift = left[0] // GROUP, right[0] // GROUP - turn
    return pl.pallas_call(
        hands_kernel,
        grid=(rows // GROUP,),
        in_specs=[
            pl.BlockSpec((GROUP, tile_cols, width), lambda g: (g + jnp.where(g < turn, lead, shift), 0, 0)),
            pl.BlockSpec((2 * width, 3 * width), lambda g: (jnp.where(g < turn, 0, 1), 0)),
        ],
        out_specs=pl.BlockSpec((width, GROUP, tile_cols), lambda g: (0, g, 0)),
        out_shape=jax.ShapeDtypeStruct((width, rows, tile_cols), jnp.float32),
        compiler_params=pltpu.CompilerParams(vmem_limit_bytes=VMEM),
        cost_estimate=estimate(6 * rows * tile_cols * width * 2 * width, 8 * rows * tile_cols * width),
        name="hands",
    )(pair, weights3)


def product_kernel(half_ref, low_ref, high_ref, own_ref, other_ref, out_ref):
    cols = own_ref.shape[0] // 2
    half = half_ref[0]
    rows = own_ref.shape[2]
    for n in range(own_ref.shape[1]):

        def line(ref, lo):
            return jnp.concatenate([ref[lo * cols + c, n] for c in range(cols)], axis=1)

        left_high, left_low = parts(
            jnp.concatenate(
                [line(ref, lo) for lo in range(2) for ref in (low_ref, high_ref)], axis=0
            )
        )
        right_high, right_low = parts(
            jnp.concatenate(
                [line(ref, lo) for ref in (own_ref, other_ref) for lo in range(2)], axis=0
            )
        )
        result = lax.dot_general(
            jnp.concatenate([right_high, right_high, right_low], axis=1),
            jnp.concatenate([left_high, left_low, left_high], axis=1),
            (((1,), (1,)), ((), ())),
            preferred_element_type=jnp.float32,
        )
        wide = result.shape[1] // 2
        for lo in range(2):
            for piece in range(cols):
                source, other_lo = divmod(piece, 2)
                plane = 2 * jnp.where(half == source, 0, 1) + other_lo
                out_ref[lo * cols + plane, n] = result[
                    piece * rows : (piece + 1) * rows, lo * wide : (lo + 1) * wide
                ]


def product(half, low, high, own, other, wide):
    sources, owned, rows, width = own.shape
    k_all = width * sources // 2
    spec_out = pl.BlockSpec((sources, STEP, rows, wide), lambda n, half: (0, n, 0, 0))
    spec = lambda height: pl.BlockSpec(
        (sources, STEP, height, width), lambda n, half: (0, n, 0, 0)
    )
    return pl.pallas_call(
        product_kernel,
        grid_spec=pltpu.PrefetchScalarGridSpec(
            num_scalar_prefetch=1,
            grid=(owned // STEP,),
            in_specs=[spec(LOWER), spec(wide - LOWER), spec(rows), spec(rows)],
            out_specs=spec_out,
        ),
        out_shape=jax.ShapeDtypeStruct((sources, owned, rows, wide), jnp.float32),
        compiler_params=pltpu.CompilerParams(vmem_limit_bytes=VMEM),
        cost_estimate=estimate(
            6 * owned * 4 * rows * 2 * wide * k_all, 4 * owned * k_all * (2 * wide + 4 * rows)
        ),
        name="product",
    )(half, low, high, own, other)


def head_kernel(
    pair_ref, product_ref, gate_ref, output_ref, up_ref, down_ref, bins_ref, *out_refs
):
    tile_rows, cols, width = pair_ref.shape
    bins = out_refs[0].shape[1]
    per = 4
    flat_pair = pair_ref.reshape(tile_rows * cols, width)
    flat_product = product_ref.reshape(width * cols, tile_rows)
    hidden_width = up_ref.shape[0] // 2
    for start in range(0, cols, per):
        values = jnp.concatenate(
            [flat_pair[pl.ds(start + n, tile_rows, stride=cols), :].T for n in range(per)], axis=1
        )
        product_values = jnp.concatenate(
            [flat_product[pl.ds(start + n, width, stride=cols), :] for n in range(per)], axis=1
        )
        gate = jax.nn.sigmoid(times(gate_ref[...], normalized(values)))
        updated = values + gate * times(output_ref[...], normalized(product_values))
        hidden = times(up_ref[...], normalized(updated))
        activated = jax.nn.silu(hidden[:hidden_width]) * hidden[hidden_width:]
        pair_out = updated + times(down_ref[...], activated)
        logits = times(bins_ref[...], pair_out)
        for n in range(per):
            for part, out_ref in enumerate(out_refs):
                out_ref[start + n] = logits[
                    part * bins : (part + 1) * bins, n * tile_rows : (n + 1) * tile_rows
                ]


def head(pair, product_values, first, gate3, output3, up3, down3, bins3):
    tile_rows, tile_cols, width = pair.shape
    chunk_cols = product_values.shape[1]
    steps = chunk_cols // GROUP
    lead = first // GROUP
    bins = bins3.shape[0] // PARTS
    whole = lambda array: pl.BlockSpec(array.shape, lambda g: (0, 0))
    macs = gate3.size + output3.size + up3.size + down3.size + bins3.size
    return pl.pallas_call(
        head_kernel,
        grid=(steps,),
        in_specs=[
            pl.BlockSpec((tile_rows, GROUP, width), lambda g: (0, lead + g, 0)),
            pl.BlockSpec((width, GROUP, tile_rows), lambda g: (0, g, 0)),
            whole(gate3),
            whole(output3),
            whole(up3),
            whole(down3),
            whole(bins3),
        ],
        out_specs=[pl.BlockSpec((GROUP, bins, tile_rows), lambda g: (g, 0, 0))] * PARTS,
        out_shape=[jax.ShapeDtypeStruct((chunk_cols, bins, tile_rows), jnp.float32)] * PARTS,
        compiler_params=pltpu.CompilerParams(vmem_limit_bytes=VMEM),
        cost_estimate=estimate(
            2 * chunk_cols * tile_rows * macs, 4 * chunk_cols * tile_rows * (2 * width + PARTS * bins)
        ),
        name="head",
    )(pair, product_values, gate3, output3, up3, down3, bins3)


def turned_kernel(bias_ref, *refs):
    out_ref, sources = refs[-1], refs[:-1]
    count = len(sources) // PARTS
    tile_rows, _, bins, tile_cols = out_ref.shape
    flat = out_ref.reshape(tile_rows * PARTS * bins, tile_cols)
    for part in range(PARTS):
        for n in range(bins):
            values = [
                ref.reshape(ref.shape[0] * bins, tile_rows)[pl.ds(n, ref.shape[0], stride=bins), :]
                for ref in sources[part * count : (part + 1) * count]
            ]
            result = jnp.concatenate(values, axis=0).T + bias_ref[part, n : n + 1, :]
            flat[pl.ds(part * bins + n, tile_rows, stride=PARTS * bins), :] = result


def turned(bias, own):
    arrays = [block[part] for part in range(PARTS) for block in own]
    _, bins, tile_rows = arrays[0].shape
    tile_cols = sum(block[0].shape[0] for block in own)
    block = lambda rows: pl.BlockSpec((rows, GROUP, tile_rows), lambda g: (0, g, 0))
    return pl.pallas_call(
        turned_kernel,
        grid=(bins // GROUP,),
        in_specs=[pl.BlockSpec((PARTS, GROUP, tile_cols), lambda g: (0, g, 0))]
        + [block(array.shape[0]) for array in arrays],
        out_specs=pl.BlockSpec((tile_rows, PARTS, GROUP, tile_cols), lambda g: (0, 0, g, 0)),
        out_shape=jax.ShapeDtypeStruct((tile_rows, PARTS, bins, tile_cols), jnp.float32),
        compiler_params=pltpu.CompilerParams(vmem_limit_bytes=VMEM),
        cost_estimate=estimate(0, 8 * tile_rows * PARTS * bins * tile_cols),
        name="turned",
    )(bias, *arrays)


def joined_kernel(base_ref, *refs):
    out_ref = refs[-1]
    for part, ref in enumerate(refs[:-1]):
        out_ref[:, part] = base_ref[:, part] + ref[...]


def joined(base, mirror, first):
    rows, bins, tile_cols = mirror[0].shape
    lead = first // GROUP
    whole = pl.BlockSpec((GROUP, PARTS, bins, tile_cols), lambda g: (lead + g, 0, 0, 0))
    block = pl.BlockSpec((GROUP, bins, tile_cols), lambda g: (g, 0, 0))
    return pl.pallas_call(
        joined_kernel,
        grid=(rows // GROUP,),
        in_specs=[whole] + [block] * PARTS,
        out_specs=whole,
        out_shape=jax.ShapeDtypeStruct(base.shape, jnp.float32),
        input_output_aliases={0: 0},
        compiler_params=pltpu.CompilerParams(vmem_limit_bytes=VMEM),
        cost_estimate=estimate(0, 12 * PARTS * rows * bins * tile_cols),
        name="joined",
    )(base, *mirror)


def move(values, count, target):
    every = [(r, c) for r in range(count) for c in range(count)]
    pairs = [(r * count + c, target(r, c)) for r, c in every]
    return lax.ppermute(values, ("half", "lo", "col"), pairs)


def aside(block, count):
    return [block[0]] + [
        move(block[n], count, lambda r, c: r * count + (c ^ n)) for n in range(1, len(block))
    ]


def across(shifted, count):
    return [
        move(values, count, lambda r, c: (c ^ n) * count + r) for n, values in enumerate(shifted)
    ]


def half_shards(
    pair,
    gain_input,
    weights_in,
    gate_weights,
    weights_out,
    gain_product,
    gain_transition,
    transition_in,
    transition_out,
    distogram_weights,
    distogram_bias,
):
    row_count = 2 * lax.axis_size("lo")
    col_count = lax.axis_size("col")
    _, tile_rows, tile_cols, width = pair.shape
    tile = pair[0]
    in3 = split_weights(weights_in, gain_input)
    gate3 = split_weights(gate_weights, gain_input)
    output3 = split_weights(weights_out, gain_product)
    up3 = split_weights(transition_in, gain_transition)
    down3 = split_weights(transition_out)
    bins3 = split_weights(distogram_weights)
    sources = 2 * col_count
    owned = width // sources

    def spread(values):
        values = values.reshape(sources, owned, *values.shape[1:])
        return lax.all_to_all(values, ("lo", "col"), split_axis=0, concat_axis=0, tiled=True)

    tie = lax.optimization_barrier
    half = lax.axis_index("half").astype(jnp.int32).reshape(1)
    firsts = [sum(CHUNKS[:n]) for n in range(len(CHUNKS))]
    upper = tile_rows - LOWER

    def exchange(values):
        return lax.ppermute(values, "half", [(0, 1), (1, 0)])

    def delivered(values):
        values = lax.all_to_all(values, ("lo", "col"), split_axis=0, concat_axis=0, tiled=True)
        return values.reshape(width, values.shape[2], tile_rows)

    def run_head(values, chunk):
        return head(tile, values, firsts[chunk], gate3, output3, up3, down3, bins3)

    right = spread(hands(tile, in3, (0, 0), (firsts[0], CHUNKS[0])))
    rights, others = [right], [exchange(right)]
    low = spread(hands(tile, in3, (0, LOWER), (firsts[1], CHUNKS[1])))
    rights.append(low[:, :, LOWER:])
    others.append(exchange(rights[1]))
    sent = hands(tile, in3, (LOWER, upper), (firsts[2], CHUNKS[2]))
    sent, others[0] = tie((sent, others[0]))
    high = spread(sent)
    rights.append(high[:, :, upper:])
    others.append(exchange(rights[2]))

    def blocks(chunk):
        return product(half, low, high, rights[chunk], others[chunk], tile_rows)

    values, others[1] = tie((blocks(0), others[1]))
    own = [run_head(delivered(values), 0)]
    shifted = aside(own[0], row_count)
    values, others[2], shifted = tie((blocks(1), others[2], shifted))
    mirror = [across(shifted, row_count)]
    values, after = tie((delivered(values), blocks(2)))
    own.append(run_head(values, 1))
    shifted, mirror[0] = tie((aside(own[1], row_count), mirror[0]))
    own.append(run_head(delivered(after), 2))
    mirror.append(across(shifted, row_count))
    mirror.append(across(aside(own[2], row_count), row_count))
    bins = distogram_bias.shape[0] // PARTS
    bias = jnp.broadcast_to(distogram_bias.reshape(PARTS, bins, 1), (PARTS, bins, tile_cols))
    logits = turned(bias, own)
    for first, block in zip(firsts, mirror):
        logits = joined(logits, block, first)
    logits = logits.reshape(tile_rows, PARTS * bins, tile_cols)
    return jnp.swapaxes(logits, 1, 2)[None]


def solution(mesh):
    names = mesh.axis_names
    crops, rows, cols = (mesh.shape[name] for name in names)

    def run(pair, *parameters):
        crop_count, height, across, width = pair.shape
        tile_rows, tile_cols = height // rows, across // cols
        by_halves = (
            crop_count == crops
            and rows == cols == 4
            and tile_rows == tile_cols == LANES
            and width == LANES
        )
        if by_halves:
            halves = Mesh(mesh.devices.reshape(crops, 2, rows // 2, cols), ("crop", "half", "lo", "col"))
            spec, used, body = P("crop", ("half", "lo"), "col", None), halves, half_shards
        else:
            spec, used, body = P("crop", "row", "col", None), mesh, general_shards
        return jax.shard_map(
            body,
            mesh=used,
            in_specs=(spec,) + (P(),) * len(parameters),
            out_specs=spec,
            check_vma=False,
        )(pair, *parameters)

    return run
```

```python
import functools

import jax
import jax.numpy as jnp
from jax import lax
from jax.experimental import pallas as pl
from jax.experimental.pallas import tpu as pltpu
from jax.sharding import Mesh, PartitionSpec as P

HIGH = lax.Precision.HIGHEST
LANES = 128
GROUP = 8
STEP = 2
CHUNKS = (40, 56, 32)
LOWER = 40
PARTS = 4
VMEM = 56 * 1024 * 1024
SCALE = 8


def layer_norm(values, gain):
    center = values - jnp.mean(values, axis=-1, keepdims=True)
    spread = jnp.mean(center * center, axis=-1, keepdims=True)
    return center * lax.rsqrt(spread + 1e-05) * gain


def project(values, weights):
    return jnp.einsum("...c,cd->...d", values, weights, precision=HIGH)


def outgoing(left_hand, right_hand):
    return jnp.einsum("bikc,bjkc->bijc", left_hand, right_hand, precision=HIGH)


def mirrored(values):
    columns = lax.all_to_all(values, ("row", "col"), split_axis=2, concat_axis=1, tiled=True)
    return jnp.swapaxes(columns, 1, 2)


def general_shards(
    pair,
    gain_input,
    weights_in,
    gate_weights,
    weights_out,
    gain_product,
    gain_transition,
    transition_in,
    transition_out,
    distogram_weights,
    distogram_bias,
):
    row_count = lax.axis_size("row")
    col_count = lax.axis_size("col")
    crops, tile_rows, tile_cols, width = pair.shape
    normed = layer_norm(pair, gain_input)
    projected = project(normed, weights_in)
    left_hand = jax.nn.sigmoid(projected[..., width : 2 * width]) * projected[..., :width]
    right_hand = jax.nn.sigmoid(projected[..., 3 * width :]) * projected[..., 2 * width : 3 * width]
    stacked = jnp.stack([left_hand, right_hand], axis=0)
    received = lax.all_to_all(stacked, ("row", "col"), split_axis=4, concat_axis=2, tiled=True)
    items = received.shape[1]
    owned = received.shape[4]
    square = received.reshape(2, items, row_count, col_count, tile_rows, tile_cols, owned)
    square = square.transpose(0, 1, 2, 4, 3, 5, 6).reshape(
        2, items, row_count * tile_rows, col_count * tile_cols, owned
    )
    result = outgoing(square[0], square[1])
    product = lax.all_to_all(result, ("row", "col"), split_axis=1, concat_axis=3, tiled=True)
    base = lax.all_to_all(pair, "col", split_axis=1, concat_axis=2, tiled=True)
    normed_base = layer_norm(base, gain_input)
    gate = jax.nn.sigmoid(project(normed_base, gate_weights))
    updated = base + gate * project(layer_norm(product, gain_product), weights_out)
    hidden = project(layer_norm(updated, gain_transition), transition_in)
    hidden_width = transition_out.shape[0]
    activated = jax.nn.silu(hidden[..., :hidden_width]) * hidden[..., hidden_width:]
    pair_out = updated + project(activated, transition_out)
    symmetric = pair_out + mirrored(pair_out)
    line_logits = project(symmetric, distogram_weights) + distogram_bias
    return lax.all_to_all(line_logits, "col", split_axis=2, concat_axis=1, tiled=True)


def split_weights(weights, gain=None):
    if gain is not None:
        weights = gain[:, None] * weights
    flipped = weights.T
    high = lax.reduce_precision(flipped, 8, 7)
    low = flipped - high
    return jnp.concatenate([high, high, low], axis=1).astype(jnp.bfloat16)


def estimate(flops, moved):
    return pl.CostEstimate(flops=flops // SCALE, bytes_accessed=moved // SCALE, transcendentals=0)


def parts(values):
    high = values.astype(jnp.bfloat16)
    low = (values - high.astype(jnp.float32)).astype(jnp.bfloat16)
    return high, low


def times(weights3, values):
    high, low = parts(values)
    return jnp.dot(
        weights3, jnp.concatenate([high, low, high], axis=0), preferred_element_type=jnp.float32
    )


def normalized(values):
    center = values - jnp.mean(values, axis=0, keepdims=True)
    spread = jnp.mean(center * center, axis=0, keepdims=True)
    return center * lax.rsqrt(spread + 1e-05)


def hands_kernel(pair_ref, weights_ref, out_ref):
    rows, _, width = pair_ref.shape
    per = 4
    flat = out_ref.reshape(width * rows, LANES)
    for start in range(0, rows, per):
        values = jnp.concatenate([pair_ref[start + n].T for n in range(per)], axis=1)
        projected = times(weights_ref[...], normalized(values))
        result = jax.nn.sigmoid(projected[width:]) * projected[:width]
        for n in range(per):
            flat[pl.ds(start + n, width, stride=rows), :] = result[:, n * LANES : (n + 1) * LANES]


def hands(pair, weights3, left, right):
    _, tile_cols, width = pair.shape
    rows = left[1] + right[1]
    turn = left[1] // GROUP
    lead, shift = left[0] // GROUP, right[0] // GROUP - turn
    return pl.pallas_call(
        hands_kernel,
        grid=(rows // GROUP,),
        in_specs=[
            pl.BlockSpec((GROUP, tile_cols, width), lambda g: (g + jnp.where(g < turn, lead, shift), 0, 0)),
            pl.BlockSpec((2 * width, 3 * width), lambda g: (jnp.where(g < turn, 0, 1), 0)),
        ],
        out_specs=pl.BlockSpec((width, GROUP, tile_cols), lambda g: (0, g, 0)),
        out_shape=jax.ShapeDtypeStruct((width, rows, tile_cols), jnp.float32),
        compiler_params=pltpu.CompilerParams(vmem_limit_bytes=VMEM),
        cost_estimate=estimate(6 * rows * tile_cols * width * 2 * width, 8 * rows * tile_cols * width),
        name="hands",
    )(pair, weights3)


def product_kernel(half_ref, low_ref, high_ref, own_ref, other_ref, out_ref):
    cols = own_ref.shape[0] // 2
    half = half_ref[0]
    rows = own_ref.shape[2]
    for n in range(own_ref.shape[1]):

        def line(ref, lo):
            return jnp.concatenate([ref[lo * cols + c, n] for c in range(cols)], axis=1)

        left_high, left_low = parts(
            jnp.concatenate(
                [line(ref, lo) for lo in range(2) for ref in (low_ref, high_ref)], axis=0
            )
        )
        right_high, right_low = parts(
            jnp.concatenate(
                [line(ref, lo) for ref in (own_ref, other_ref) for lo in range(2)], axis=0
            )
        )
        result = lax.dot_general(
            jnp.concatenate([right_high, right_high, right_low], axis=1),
            jnp.concatenate([left_high, left_low, left_high], axis=1),
            (((1,), (1,)), ((), ())),
            preferred_element_type=jnp.float32,
        )
        wide = result.shape[1] // 2
        for lo in range(2):
            for piece in range(cols):
                source, other_lo = divmod(piece, 2)
                plane = 2 * jnp.where(half == source, 0, 1) + other_lo
                out_ref[lo * cols + plane, n] = result[
                    piece * rows : (piece + 1) * rows, lo * wide : (lo + 1) * wide
                ]


def product(half, low, high, own, other, wide):
    sources, owned, rows, width = own.shape
    k_all = width * sources // 2
    spec_out = pl.BlockSpec((sources, STEP, rows, wide), lambda n, half: (0, n, 0, 0))
    spec = lambda height: pl.BlockSpec(
        (sources, STEP, height, width), lambda n, half: (0, n, 0, 0)
    )
    return pl.pallas_call(
        product_kernel,
        grid_spec=pltpu.PrefetchScalarGridSpec(
            num_scalar_prefetch=1,
            grid=(owned // STEP,),
            in_specs=[spec(LOWER), spec(wide - LOWER), spec(rows), spec(rows)],
            out_specs=spec_out,
        ),
        out_shape=jax.ShapeDtypeStruct((sources, owned, rows, wide), jnp.float32),
        compiler_params=pltpu.CompilerParams(vmem_limit_bytes=VMEM),
        cost_estimate=estimate(
            6 * owned * 4 * rows * 2 * wide * k_all, 4 * owned * k_all * (2 * wide + 4 * rows)
        ),
        name="product",
    )(half, low, high, own, other)


def head_kernel(
    pair_ref, product_ref, gate_ref, output_ref, up_ref, down_ref, bins_ref, *out_refs
):
    tile_rows, cols, width = pair_ref.shape
    bins = out_refs[0].shape[1]
    per = 4
    flat_pair = pair_ref.reshape(tile_rows * cols, width)
    flat_product = product_ref.reshape(width * cols, tile_rows)
    hidden_width = up_ref.shape[0] // 2
    for start in range(0, cols, per):
        values = jnp.concatenate(
            [flat_pair[pl.ds(start + n, tile_rows, stride=cols), :].T for n in range(per)], axis=1
        )
        product_values = jnp.concatenate(
            [flat_product[pl.ds(start + n, width, stride=cols), :] for n in range(per)], axis=1
        )
        gate = jax.nn.sigmoid(times(gate_ref[...], normalized(values)))
        updated = values + gate * times(output_ref[...], normalized(product_values))
        hidden = times(up_ref[...], normalized(updated))
        activated = jax.nn.silu(hidden[:hidden_width]) * hidden[hidden_width:]
        pair_out = updated + times(down_ref[...], activated)
        logits = times(bins_ref[...], pair_out)
        for n in range(per):
            for part, out_ref in enumerate(out_refs):
                out_ref[start + n] = logits[
                    part * bins : (part + 1) * bins, n * tile_rows : (n + 1) * tile_rows
                ]


def head(pair, product_values, first, gate3, output3, up3, down3, bins3):
    tile_rows, tile_cols, width = pair.shape
    chunk_cols = product_values.shape[1]
    steps = chunk_cols // GROUP
    lead = first // GROUP
    bins = bins3.shape[0] // PARTS
    whole = lambda array: pl.BlockSpec(array.shape, lambda g: (0, 0))
    macs = gate3.size + output3.size + up3.size + down3.size + bins3.size
    return pl.pallas_call(
        head_kernel,
        grid=(steps,),
        in_specs=[
            pl.BlockSpec((tile_rows, GROUP, width), lambda g: (0, lead + g, 0)),
            pl.BlockSpec((width, GROUP, tile_rows), lambda g: (0, g, 0)),
            whole(gate3),
            whole(output3),
            whole(up3),
            whole(down3),
            whole(bins3),
        ],
        out_specs=[pl.BlockSpec((GROUP, bins, tile_rows), lambda g: (g, 0, 0))] * PARTS,
        out_shape=[jax.ShapeDtypeStruct((chunk_cols, bins, tile_rows), jnp.float32)] * PARTS,
        compiler_params=pltpu.CompilerParams(vmem_limit_bytes=VMEM),
        cost_estimate=estimate(
            2 * chunk_cols * tile_rows * macs, 4 * chunk_cols * tile_rows * (2 * width + PARTS * bins)
        ),
        name="head",
    )(pair, product_values, gate3, output3, up3, down3, bins3)


def turned_kernel(bias_ref, *refs):
    out_ref, sources = refs[-1], refs[:-1]
    count = len(sources) // PARTS
    tile_rows, _, bins, tile_cols = out_ref.shape
    flat = out_ref.reshape(tile_rows * PARTS * bins, tile_cols)
    for part in range(PARTS):
        for n in range(bins):
            values = [
                ref.reshape(ref.shape[0] * bins, tile_rows)[pl.ds(n, ref.shape[0], stride=bins), :]
                for ref in sources[part * count : (part + 1) * count]
            ]
            result = jnp.concatenate(values, axis=0).T + bias_ref[part, n : n + 1, :]
            flat[pl.ds(part * bins + n, tile_rows, stride=PARTS * bins), :] = result


def turned(bias, own):
    arrays = [block[part] for part in range(PARTS) for block in own]
    _, bins, tile_rows = arrays[0].shape
    tile_cols = sum(block[0].shape[0] for block in own)
    block = lambda rows: pl.BlockSpec((rows, GROUP, tile_rows), lambda g: (0, g, 0))
    return pl.pallas_call(
        turned_kernel,
        grid=(bins // GROUP,),
        in_specs=[pl.BlockSpec((PARTS, GROUP, tile_cols), lambda g: (0, g, 0))]
        + [block(array.shape[0]) for array in arrays],
        out_specs=pl.BlockSpec((tile_rows, PARTS, GROUP, tile_cols), lambda g: (0, 0, g, 0)),
        out_shape=jax.ShapeDtypeStruct((tile_rows, PARTS, bins, tile_cols), jnp.float32),
        compiler_params=pltpu.CompilerParams(vmem_limit_bytes=VMEM),
        cost_estimate=estimate(0, 8 * tile_rows * PARTS * bins * tile_cols),
        name="turned",
    )(bias, *arrays)


def joined_kernel(base_ref, *refs):
    out_ref = refs[-1]
    for part, ref in enumerate(refs[:-1]):
        out_ref[:, part] = base_ref[:, part] + ref[...]


def joined(base, mirror, first):
    rows, bins, tile_cols = mirror[0].shape
    lead = first // GROUP
    whole = pl.BlockSpec((GROUP, PARTS, bins, tile_cols), lambda g: (lead + g, 0, 0, 0))
    block = pl.BlockSpec((GROUP, bins, tile_cols), lambda g: (g, 0, 0))
    return pl.pallas_call(
        joined_kernel,
        grid=(rows // GROUP,),
        in_specs=[whole] + [block] * PARTS,
        out_specs=whole,
        out_shape=jax.ShapeDtypeStruct(base.shape, jnp.float32),
        input_output_aliases={0: 0},
        compiler_params=pltpu.CompilerParams(vmem_limit_bytes=VMEM),
        cost_estimate=estimate(0, 12 * PARTS * rows * bins * tile_cols),
        name="joined",
    )(base, *mirror)


def move(values, count, target):
    every = [(r, c) for r in range(count) for c in range(count)]
    pairs = [(r * count + c, target(r, c)) for r, c in every]
    return lax.ppermute(values, ("half", "lo", "col"), pairs)


def aside(block, count):
    return [block[0]] + [
        move(block[n], count, lambda r, c: r * count + (c ^ n)) for n in range(1, len(block))
    ]


def across(shifted, count):
    return [
        move(values, count, lambda r, c: (c ^ n) * count + r) for n, values in enumerate(shifted)
    ]


def half_shards(
    pair,
    gain_input,
    weights_in,
    gate_weights,
    weights_out,
    gain_product,
    gain_transition,
    transition_in,
    transition_out,
    distogram_weights,
    distogram_bias,
):
    row_count = 2 * lax.axis_size("lo")
    col_count = lax.axis_size("col")
    _, tile_rows, tile_cols, width = pair.shape
    tile = pair[0]
    in3 = split_weights(weights_in, gain_input)
    gate3 = split_weights(gate_weights, gain_input)
    output3 = split_weights(weights_out, gain_product)
    up3 = split_weights(transition_in, gain_transition)
    down3 = split_weights(transition_out)
    bins3 = split_weights(distogram_weights)
    sources = 2 * col_count
    owned = width // sources

    def spread(values):
        values = values.reshape(sources, owned, *values.shape[1:])
        return lax.all_to_all(values, ("lo", "col"), split_axis=0, concat_axis=0, tiled=True)

    tie = lax.optimization_barrier
    half = lax.axis_index("half").astype(jnp.int32).reshape(1)
    firsts = [sum(CHUNKS[:n]) for n in range(len(CHUNKS))]
    upper = tile_rows - LOWER

    def exchange(values):
        return lax.ppermute(values, "half", [(0, 1), (1, 0)])

    def delivered(values):
        values = lax.all_to_all(values, ("lo", "col"), split_axis=0, concat_axis=0, tiled=True)
        return values.reshape(width, values.shape[2], tile_rows)

    def run_head(values, chunk):
        return head(tile, values, firsts[chunk], gate3, output3, up3, down3, bins3)

    right = spread(hands(tile, in3, (0, 0), (firsts[0], CHUNKS[0])))
    rights, others = [right], [exchange(right)]
    low = spread(hands(tile, in3, (0, LOWER), (firsts[1], CHUNKS[1])))
    rights.append(low[:, :, LOWER:])
    others.append(exchange(rights[1]))
    sent = hands(tile, in3, (LOWER, upper), (firsts[2], CHUNKS[2]))
    sent, others[0] = tie((sent, others[0]))
    high = spread(sent)
    rights.append(high[:, :, upper:])
    others.append(exchange(rights[2]))

    def blocks(chunk):
        return product(half, low, high, rights[chunk], others[chunk], tile_rows)

    values, others[1] = tie((blocks(0), others[1]))
    own = [run_head(delivered(values), 0)]
    shifted = aside(own[0], row_count)
    values, others[2], shifted = tie((blocks(1), others[2], shifted))
    mirror = [across(shifted, row_count)]
    values, after = tie((delivered(values), blocks(2)))
    own.append(run_head(values, 1))
    shifted, mirror[0], late = tie(
        (aside(own[1], row_count), mirror[0], run_head(delivered(after), 2))
    )
    own.append(late)
    mirror.append(across(shifted, row_count))
    mirror.append(across(aside(late, row_count), row_count))
    bins = distogram_bias.shape[0] // PARTS
    bias = jnp.broadcast_to(distogram_bias.reshape(PARTS, bins, 1), (PARTS, bins, tile_cols))
    logits = turned(bias, own)
    for first, block in zip(firsts, mirror):
        logits = joined(logits, block, first)
    logits = logits.reshape(tile_rows, PARTS * bins, tile_cols)
    return jnp.swapaxes(logits, 1, 2)[None]


def solution(mesh):
    names = mesh.axis_names
    crops, rows, cols = (mesh.shape[name] for name in names)

    def run(pair, *parameters):
        crop_count, height, across, width = pair.shape
        tile_rows, tile_cols = height // rows, across // cols
        by_halves = (
            crop_count == crops
            and rows == cols == 4
            and tile_rows == tile_cols == LANES
            and width == LANES
        )
        if by_halves:
            halves = Mesh(mesh.devices.reshape(crops, 2, rows // 2, cols), ("crop", "half", "lo", "col"))
            spec, used, body = P("crop", ("half", "lo"), "col", None), halves, half_shards
        else:
            spec, used, body = P("crop", "row", "col", None), mesh, general_shards
        return jax.shard_map(
            body,
            mesh=used,
            in_specs=(spec,) + (P(),) * len(parameters),
            out_specs=spec,
            check_vma=False,
        )(pair, *parameters)

    return run
```
